32 devices in a mesh: dp: 8 (over z, x), tensor: 4 (over y, core).
Axes of the slice: x: 2, y: 2, z: 4, core: 2. Of those that a mesh axis runs over, the one named last changes fastest.
Arguments:
- inputs: bfloat16 [2, 6144, 768], P(None, 'dp'), may hold values from -6 to 6
- time_first: bfloat16 [8, 13, 768], P('dp'), may hold values from -6 to 6
- time_second: bfloat16 [8, 7, 768], P('dp'), may hold values from -6 to 6
- lengths_first: int32 [8, 13], P('dp'), may hold values from 1 to 64, 720 in all within a row
- lengths_second: int32 [8, 7], P('dp'), may hold values from 1 to 128, 720 in all within a row
- cotangent: bfloat16 [2, 6144, 768], P(None, 'dp'), may hold values from -6 to 6
- w_qkv: float32 [768, 3, 768], P('dp', None, 'tensor'), may hold values from -0.21875 to 0.21875
- m_qkv: float32 [768, 3, 768], P('dp', None, 'tensor'), may hold values from -0.0078125 to 0.0078125
- v_qkv: float32 [768, 3, 768], P('dp', None, 'tensor'), may hold values from 2.7126737e-07 to 1.0850695e-06
- w_proj: float32 [768, 768], P('tensor', 'dp'), may hold values from -1.75 to 1.75
- m_proj: float32 [768, 768], P('tensor', 'dp'), may hold values from -0.0012207031 to 0.0012207031
- v_proj: float32 [768, 768], P('tensor', 'dp'), may hold values from 6.1035155e-09 to 2.4414062e-08
- w_up: float32 [768, 3072], P('dp', 'tensor'), may hold values from -0.21875 to 0.21875
- m_up: float32 [768, 3072], P('dp', 'tensor'), may hold values from -0.0029296875 to 0.0029296875
- v_up: float32 [768, 3072], P('dp', 'tensor'), may hold values from 3.8146972e-08 to 1.5258789e-07
- w_down: float32 [3072, 768], P('tensor', 'dp'), may hold values from -0.109375 to 0.109375
- m_down: float32 [3072, 768], P('tensor', 'dp'), may hold values from -0.0048828125 to 0.0048828125
- v_down: float32 [3072, 768], P('tensor', 'dp'), may hold values from 1.235962e-07 to 4.943848e-07
- w_vecs: float32 [6, 768], replicated, may hold values from -0.3 to 1.2
- m_vecs: float32 [6, 768], replicated, may hold values from -0.009765625 to 0.009765625
- v_vecs: float32 [6, 768], replicated, may hold values from 4.2385525e-07 to 1.695421e-06
- b_heads: float32 [2, 768], P(None, 'tensor'), may hold values from -4 to 4
- m_heads: float32 [2, 768], P(None, 'tensor'), may hold values from -0.0078125 to 0.0078125
- v_heads: float32 [2, 768], P(None, 'tensor'), may hold values from 3.4332277e-07 to 1.3732911e-06
- b_hidden: float32 [3072], P('tensor'), may hold values from -4 to 4
- m_hidden: float32 [3072], P('tensor'), may hold values from -0.0024414062 to 0.0024414062
- v_hidden: float32 [3072], P('tensor'), may hold values from 3.323025e-08 to 1.32921e-07
Outputs:
- block_out: bfloat16 [2, 6144, 768], P(None, 'dp')
- input_grad: float32 [2, 6144, 768], P(None, 'dp')
- grad_norm: float32 [1], replicated
- stream_rms: float32 [3], replicated
- qkv_next: float32 [768, 3, 768], P('dp', None, 'tensor')
- qkv_moment: float32 [768, 3, 768], P('dp', None, 'tensor')
- qkv_square: float32 [768, 3, 768], P('dp', None, 'tensor')
- proj_next: float32 [768, 768], P('tensor', 'dp')
- proj_moment: float32 [768, 768], P('tensor', 'dp')
- proj_square: float32 [768, 768], P('tensor', 'dp')
- up_next: float32 [768, 3072], P('dp', 'tensor')
- up_moment: float32 [768, 3072], P('dp', 'tensor')
- up_square: float32 [768, 3072], P('dp', 'tensor')
- down_next: float32 [3072, 768], P('tensor', 'dp')
- down_moment: float32 [3072, 768], P('tensor', 'dp')
- down_square: float32 [3072, 768], P('tensor', 'dp')
- vecs_next: float32 [6, 768], replicated
- vecs_moment: float32 [6, 768], replicated
- vecs_square: float32 [6, 768], replicated
- heads_next: float32 [2, 768], P(None, 'tensor')
- heads_moment: float32 [2, 768], P(None, 'tensor')
- heads_square: float32 [2, 768], P(None, 'tensor')
- hidden_next: float32 [3072], P('tensor')
- hidden_moment: float32 [3072], P('tensor')
- hidden_square: float32 [3072], P('tensor')
The draws below stay inside these ranges and needn't reach their ends.
Inputs may be any that keep to these rules, and one draw needn't show every extreme that they name: `lengths_first`: each row sums to 720 and its longest entry is exactly 64. `lengths_second`: each row sums to 720 and its longest entry is exactly 128.
All inputs are finite; a program needn't handle non-finite values.
Results may differ from the reference program's by a relative error of at most 0.008.
The reference program's roundings to bfloat16 on the way count: a program that leaves them out, or rounds other values in their place, can miss the bound.
Values may be sent and summed in bfloat16 or wider, within the bound.
No kernel may reach another device: no remote copies, remote signals or barrier semaphores. Data moves between devices by JAX's collectives and lax.ppermute only.
A program may use at most 128 MiB of HBM per device.

```python
import math
from functools import partial
import jax
import jax.numpy as jnp
import numpy as np
from jax import lax

D = 768
H = 12
HD = 64
F = 3072
MB_DEV = 768
LEN_A = 64
LEN_B = 128
STEP = 5
VALID = 720
A_SEQ = 13
B_SEQ = 7
TOK_MB = 6144
N_DP = 8


def draw_w_vecs(key, part):
    gain_key, offset_key = jax.random.split(key)
    gain_rows = jax.random.uniform(gain_key, (6, D), jnp.float32, 0.8, 1.2)
    offset_rows = jax.random.uniform(offset_key, (6, D), jnp.float32, -0.3, 0.3)
    row_index = jnp.arange(6, dtype=jnp.int32)[:, None]
    is_gain = (row_index % 2 == 0) & (row_index < 4)
    return jnp.where(is_gain, gain_rows, offset_rows)


def steps_of(key, extent, shards, smallest, largest):
    def one(dim, parts):
        draws = jax.random.uniform(jax.random.fold_in(jax.random.fold_in(key, 6), dim), (parts,), jnp.float32, smallest / len(shards), largest / len(shards))
        return jnp.repeat(jnp.exp(draws), extent[dim] // parts).reshape((-1,) + (1,) * (len(extent) - dim - 1))

    level = one(*shards[0])
    for cut in shards[1:]:
        level = level * one(*cut)
    return level


def split_up(amount, total, limit, lean):
    loads = [(1 << 20) // math.isqrt(standing ** lean) + 1 for standing in range(2, amount + 1)]
    rest, holding = total - limit - (amount - 1), [1] * (amount - 1)
    while rest > 0:
        candidates = [i for i in range(amount - 1) if holding[i] < limit]
        whole, remaining = sum([loads[i] for i in candidates]), rest
        for i in candidates:
            more = min(limit - holding[i], max(1, remaining * loads[i] // whole), rest)
            holding[i] = holding[i] + more
            rest = rest - more
    return np.array([limit] + holding)


def uneven_parts(key, count, total, reach, slope):
    if count == 2:
        one = jax.random.randint(key, (), max(1, total - reach), min(reach, total - 1) + 1)
        return jnp.stack([one, total - one])
    tallies = jnp.asarray(split_up(count, total, reach, slope), jnp.int32)
    pairs = (count - 1) // 2
    giver, sink = tallies[1:1 + 2 * pairs:2], tallies[2:2 + 2 * pairs:2]
    slack = jnp.minimum(giver - 1, reach - sink)
    passed = jax.random.randint(jax.random.fold_in(key, 1), (pairs,), 0, 1 << 20) % (slack + 1)
    tallies = tallies.at[1:1 + 2 * pairs:2].set(giver - passed).at[2:2 + 2 * pairs:2].set(sink + passed)
    return tallies[jax.random.permutation(jax.random.fold_in(key, 2), count)]


def centred(rng, shape, scale, limit, cuts=(), kind=jnp.bfloat16):
    values = jax.random.normal(rng, shape, jnp.float32) * scale
    if len(cuts) > 0:
        values = steps_of(rng, shape, cuts, -0.22, 0.18) * values
    return jnp.clip(values, min=-limit, max=limit).astype(kind)


def setup_inputs(seed: int = 0) -> dict:
    seeds = jax.random.split(jax.random.key(seed), 28)
    inputs = centred(seeds[0], (2, TOK_MB, D), 1.0, 6.0, ((1, 8),))
    time_first = centred(seeds[1], (N_DP, A_SEQ, D), 1.0, 6.0, ((0, 8),))
    time_second = centred(seeds[2], (N_DP, B_SEQ, D), 1.0, 6.0, ((0, 8),))
    lengths_first = jax.vmap(lambda own: uneven_parts(own, A_SEQ, VALID, LEN_A, 2))(jax.random.split(seeds[3], N_DP)).reshape((N_DP, A_SEQ)).astype(jnp.int32)
    lengths_second = jax.vmap(lambda own: uneven_parts(own, B_SEQ, VALID, LEN_B, 2))(jax.random.split(seeds[4], N_DP)).reshape((N_DP, B_SEQ)).astype(jnp.int32)
    cotangent = centred(seeds[5], (2, TOK_MB, D), 1.0, 6.0, ((1, 8),))
    w_qkv = centred(seeds[6], (D, 3, D), D ** -0.5, 0.21875, ((0, 8), (2, 4)), jnp.float32)
    m_qkv = centred(seeds[7], (D, 3, D), (0.4 / D), 0.0078125, ((0, 8), (2, 4)), jnp.float32)
    v_qkv = jnp.clip(jnp.exp(math.log(1.0850694707187358e-06) - 1.3862944 * jax.random.uniform(seeds[8], (D, 3, D), jnp.float32) ** steps_of(seeds[8], (D, 3, D), ((0, 8), (2, 4)), -0.2, 0.2)), 2.7126736767968396e-07, 1.0850694707187358e-06)
    w_proj = centred(seeds[9], (D, D), (max(D // 64, 1)) ** -0.5, 1.75, ((0, 4), (1, 8)), jnp.float32)
    m_proj = centred(seeds[10], (D, D), (0.06 / D), 0.0012207031, ((0, 4), (1, 8)), jnp.float32)
    v_proj = jnp.clip(jnp.exp(math.log(2.4414061883248905e-08) - 1.3862944 * jax.random.uniform(seeds[11], (D, D), jnp.float32) ** steps_of(seeds[11], (D, D), ((0, 4), (1, 8)), -0.2, 0.2)), 6.103515470812226e-09, 2.4414061883248905e-08)
    w_up = centred(seeds[12], (D, F), D ** -0.5, 0.21875, ((0, 8), (1, 4)), jnp.float32)
    m_up = centred(seeds[13], (D, F), (0.15 / D), 0.0029296875, ((0, 8), (1, 4)), jnp.float32)
    v_up = jnp.clip(jnp.exp(math.log(1.5258788721439487e-07) - 1.3862944 * jax.random.uniform(seeds[14], (D, F), jnp.float32) ** steps_of(seeds[14], (D, F), ((0, 8), (1, 4)), -0.2, 0.2)), 3.814697180359872e-08, 1.5258788721439487e-07)
    w_down = centred(seeds[15], (F, D), F ** -0.5, 0.109375, ((0, 4), (1, 8)), jnp.float32)
    m_down = centred(seeds[16], (F, D), (0.27 / D), 0.0048828125, ((0, 4), (1, 8)), jnp.float32)
    v_down = jnp.clip(jnp.exp(math.log(4.943847784488753e-07) - 1.3862944 * jax.random.uniform(seeds[17], (F, D), jnp.float32) ** steps_of(seeds[17], (F, D), ((0, 4), (1, 8)), -0.2, 0.2)), 1.2359619461221882e-07, 4.943847784488753e-07)
    w_vecs = draw_w_vecs(jax.random.fold_in(seeds[27], 71), 0)
    m_vecs = centred(seeds[19], (6, D), (0.5 / D), 0.009765625, (), jnp.float32)
    v_vecs = jnp.clip(jnp.exp(jax.random.uniform(seeds[20], (6, D), jnp.float32, math.log(4.238552548940788e-07), math.log(1.6954210195763153e-06))), 4.238552548940788e-07, 1.6954210195763153e-06)
    b_heads = centred(seeds[21], (2, D), 0.3, 4.0, ((1, 4),), jnp.float32)
    m_heads = centred(seeds[22], (2, D), (0.45 / D), 0.0078125, ((1, 4),), jnp.float32)
    v_heads = jnp.clip(jnp.exp(math.log(1.3732910701946821e-06) - 1.3862944 * jax.random.uniform(seeds[23], (2, D), jnp.float32) ** steps_of(seeds[23], (2, D), ((1, 4),), -0.2, 0.2)), 3.4332276754867053e-07, 1.3732910701946821e-06)
    b_hidden = centred(seeds[24], (F,), 0.3, 4.0, ((0, 4),), jnp.float32)
    m_hidden = centred(seeds[25], (F,), (0.14 / D), 0.0024414062, ((0, 4),), jnp.float32)
    v_hidden = jnp.clip(jnp.exp(math.log(1.329210022049665e-07) - 1.3862944 * jax.random.uniform(seeds[26], (F,), jnp.float32) ** steps_of(seeds[26], (F,), ((0, 4),), -0.2, 0.2)), 3.3230250551241625e-08, 1.329210022049665e-07)
    return dict(inputs=inputs, time_first=time_first, time_second=time_second, lengths_first=lengths_first, lengths_second=lengths_second, cotangent=cotangent, w_qkv=w_qkv, m_qkv=m_qkv, v_qkv=v_qkv, w_proj=w_proj, m_proj=m_proj, v_proj=v_proj, w_up=w_up, m_up=m_up, v_up=v_up, w_down=w_down, m_down=m_down, v_down=v_down, w_vecs=w_vecs, m_vecs=m_vecs, v_vecs=v_vecs, b_heads=b_heads, m_heads=m_heads, v_heads=v_heads, b_hidden=b_hidden, m_hidden=m_hidden, v_hidden=v_hidden)


@jax.custom_vjp
def low(v):
    return lax.optimization_barrier(v.astype(jnp.bfloat16)).astype(jnp.float32)

@jax.custom_vjp
def low_back(v):
    return v

def low_keep(v):
    return (low(v), None)

def low_pass(kept, grad):
    return (grad,)

def back_keep(v):
    return (v, None)

def back_low(kept, grad):
    return (low(grad),)
low.defvjp(low_keep, low_pass)
low_back.defvjp(back_keep, back_low)
norm_eps = 1e-05
clip_limit = 1.0
beta_first = 0.5
beta_second = 0.5
adam_eps = 1e-08
matrix_decay = 0.01
masked_score = -1e+30
step_rates = (0.03, 0.2, 0.03, 0.015, 0.3, 0.3, 0.3)
decay_table = (0.01, 0.01, 0.01, 0.01, 0.0, 0.0, 0.0)

def both_ways(value_in):
    return low_back(low(value_in))

def matmul(left_side, right_side):
    return jnp.dot(left_side, right_side, precision=lax.Precision.HIGHEST, preferred_element_type=jnp.float32)

def layer_norm(stream, gain_row, offset_row):
    center = stream - lax.optimization_barrier(jnp.mean(stream, axis=-1, keepdims=True))
    spread = lax.optimization_barrier(jnp.mean(center * center, axis=-1, keepdims=True))
    return center * lax.rsqrt(spread + norm_eps) * gain_row + offset_row

def segment_ids(lengths_row, rows_count, first_id):
    bounds = jnp.cumsum(lengths_row)
    places = jnp.arange(rows_count, dtype=jnp.int32)
    return first_id + lax.optimization_barrier(jnp.sum((places[:, None] >= bounds[None, :]).astype(jnp.int32), axis=1))

def slab_attention(pieces):
    queries, keyset, valueset, segments = pieces
    scores = jnp.einsum('qhc,khc->hqk', queries, keyset, precision=lax.Precision.HIGHEST) * HD ** (-0.5)
    scores = low_back(scores)
    allowed = segments[:, None] == segments[None, :]
    scores = jnp.where(allowed[None], scores, masked_score)
    softmaxed = jax.nn.softmax(scores, axis=-1)
    return jnp.einsum('hqk,khc->qhc', low(softmaxed), valueset, precision=lax.Precision.HIGHEST)

def forward(params, stream_in, time_rows, segments):
    w_qkv, w_proj, w_up, w_down, w_vecs, b_heads, b_hidden = params
    stream = stream_in + time_rows
    normed = low(layer_norm(stream, w_vecs[0], w_vecs[1]))
    mixed_all = matmul(normed, low(w_qkv).reshape(D, 3 * D))
    queries = both_ways(mixed_all[:, :D] + b_heads[0])
    keyset = both_ways(mixed_all[:, D:2 * D])
    valueset = both_ways(mixed_all[:, 2 * D:] + b_heads[1])
    slab_shape = (N_DP, 2 * MB_DEV, H, HD)
    attended = lax.map(jax.checkpoint(slab_attention), (queries.reshape(slab_shape), keyset.reshape(slab_shape), valueset.reshape(slab_shape), segments))
    attended = both_ways(attended.reshape(N_DP * 2 * MB_DEV, D))
    branch = low_back(matmul(attended, low(w_proj))) + w_vecs[4]
    middle = stream + branch
    normed_two = low(layer_norm(middle, w_vecs[2], w_vecs[3]))
    hidden = low_back(matmul(normed_two, low(w_up))) + b_hidden
    active = low(jax.nn.gelu(hidden, approximate=False))
    branch_two = low_back(matmul(active, low(w_down))) + w_vecs[5]
    return (middle + branch_two, branch, branch_two)

def adamw_step(weight, moment_old, square_old, gradient, step_rate, decay_value, clip_factor, correct_one, correct_two):
    clipped = gradient * clip_factor
    moment_new = beta_first * moment_old + (1.0 - beta_first) * clipped
    square_new = beta_second * square_old + (1.0 - beta_second) * clipped * clipped
    divisor = jnp.sqrt(square_new / correct_two) + adam_eps
    weight_new = weight - step_rate * (moment_new / correct_one / divisor + decay_value * weight)
    return (weight_new, moment_new, square_new)

def to_slabs(array_in):
    return array_in.astype(jnp.float32).reshape(2, N_DP, MB_DEV, D).transpose(1, 0, 2, 3).reshape(N_DP * 2 * MB_DEV, D)

def from_slabs(array_in):
    return array_in.reshape(N_DP, 2, MB_DEV, D).transpose(1, 0, 2, 3).reshape(2, TOK_MB, D)

def reference(inputs, time_first, time_second, lengths_first, lengths_second, cotangent, w_qkv, m_qkv, v_qkv, w_proj, m_proj, v_proj, w_up, m_up, v_up, w_down, m_down, v_down, w_vecs, m_vecs, v_vecs, b_heads, m_heads, v_heads, b_hidden, m_hidden, v_hidden):
    ids_first = jax.vmap(partial(segment_ids, rows_count=MB_DEV, first_id=0))(lengths_first)
    ids_second = jax.vmap(partial(segment_ids, rows_count=MB_DEV, first_id=A_SEQ + 1))(lengths_second)
    segments = jnp.concatenate([ids_first, ids_second], axis=1)
    valid_rows = jnp.concatenate([ids_first < A_SEQ, ids_second < A_SEQ + 1 + B_SEQ], axis=1).astype(jnp.float32).reshape(N_DP * 2 * MB_DEV, 1)
    pick_first = (ids_first[:, :, None] == jnp.arange(A_SEQ, dtype=jnp.int32)[None, None, :]).astype(jnp.float32)
    pick_second = (ids_second[:, :, None] == A_SEQ + 1 + jnp.arange(B_SEQ, dtype=jnp.int32)[None, None, :]).astype(jnp.float32)
    time_one = jnp.einsum('gra,gac->grc', pick_first, time_first.astype(jnp.float32), precision=lax.Precision.HIGHEST)
    time_two = jnp.einsum('gra,gac->grc', pick_second, time_second.astype(jnp.float32), precision=lax.Precision.HIGHEST)
    time_rows = jnp.concatenate([time_one, time_two], axis=1).reshape(N_DP * 2 * MB_DEV, D)
    params = (w_qkv, w_proj, w_up, w_down, w_vecs, b_heads, b_hidden)
    outputs, pullback = jax.vjp(partial(forward, time_rows=time_rows, segments=segments), params, to_slabs(inputs))
    block_sum, branch, branch_two = outputs
    gradients, grad_rows = pullback((to_slabs(cotangent) * valid_rows, jnp.zeros_like(branch), jnp.zeros_like(branch_two)))
    total_square = jnp.zeros((), jnp.float32)
    for grad_item in gradients:
        total_square = total_square + jnp.sum(grad_item * grad_item)
    grad_norm = jnp.sqrt(total_square)
    clip_factor = jnp.minimum(1.0, clip_limit / (grad_norm + 1e-06))
    correct_one = 1.0 - beta_first ** STEP
    correct_two = 1.0 - beta_second ** STEP
    moments = (m_qkv, m_proj, m_up, m_down, m_vecs, m_heads, m_hidden)
    squares = (v_qkv, v_proj, v_up, v_down, v_vecs, v_heads, v_hidden)
    results = []
    for index_item in range(7):
        results.append(adamw_step(params[index_item], moments[index_item], squares[index_item], gradients[index_item], step_rates[index_item], decay_table[index_item], clip_factor, correct_one, correct_two))
    valid_count = jnp.sum(valid_rows)

    def rms_of(values_in):
        return jnp.sqrt(jnp.sum(valid_rows * values_in * values_in) / (valid_count * D))
    stream_rms = jnp.stack([rms_of(block_sum), rms_of(branch), rms_of(branch_two)])
    return (from_slabs(block_sum).astype(jnp.bfloat16), from_slabs(grad_rows), grad_norm.reshape(1), stream_rms, results[0][0], results[0][1], results[0][2], results[1][0], results[1][1], results[1][2], results[2][0], results[2][1], results[2][2], results[3][0], results[3][1], results[3][2], results[4][0], results[4][1], results[4][2], results[5][0], results[5][1], results[5][2], results[6][0], results[6][1], results[6][2])
```

```python
import jax
import jax.numpy as jnp
from jax import lax
from jax.sharding import PartitionSpec as P

HD = 64
STEP = 5

norm_eps = 1e-05
clip_limit = 1.0
beta_first = 0.5
beta_second = 0.5
adam_eps = 1e-08
matrix_decay = 0.01
masked_score = -1e30
step_rates = (0.03, 0.2, 0.03, 0.015, 0.3, 0.3, 0.3)
bf16 = jnp.bfloat16
f32 = jnp.float32


def dot(a, b, dims):
    return lax.dot_general(a, b, (dims, ((), ())), preferred_element_type=f32)


NN = ((1,), (0,))
NT = ((1,), (1,))
TN = ((0,), (0,))


def swap_bit(v, axis, size, bit):
    return lax.ppermute(v, axis, [(i, i ^ bit) for i in range(size)])


def norm_parts(stream):
    center = stream - jnp.mean(stream, axis=-1, keepdims=True)
    spread = jnp.mean(center * center, axis=-1, keepdims=True)
    scale = lax.rsqrt(spread + norm_eps)
    return center * scale, scale


def norm_back(scaled, xhat, scale):
    return scale * (
        scaled
        - jnp.mean(scaled, axis=-1, keepdims=True)
        - xhat * jnp.mean(scaled * xhat, axis=-1, keepdims=True)
    )


def segment_ids(lengths_row, rows_count):
    count = lengths_row.shape[0]
    places = jnp.arange(rows_count, dtype=jnp.int32)
    ids = jnp.zeros((rows_count,), jnp.int32)
    bound = jnp.zeros((), jnp.int32)
    for k in range(count):
        bound = bound + lengths_row[k]
        ids = ids + (places >= bound).astype(jnp.int32)
    return ids


def tensor_sum(part, core):
    half = part.shape[0] // 2
    pieces = part.reshape(2, half, part.shape[1])
    away = lax.dynamic_index_in_dim(pieces, 1 - core, 0, False).astype(bf16)
    keep = lax.dynamic_index_in_dim(pieces, core, 0, False).astype(f32)
    low = (keep + swap_bit(away, "tensor", 4, 1).astype(f32)).astype(bf16)
    both = (low.astype(f32) + swap_bit(low, "tensor", 4, 2).astype(f32)).astype(bf16)
    other = swap_bit(both, "tensor", 4, 1)
    return jnp.where(core == 0, jnp.concatenate([both, other]), jnp.concatenate([other, both]))


def scatter_rows(grad, n):
    outer, width = n // 2, grad.shape[1]
    r = grad.shape[0] // n
    me = lax.axis_index("dp")
    inner, mine = me % 2, me // 2
    view = grad.reshape(outer, 2, r, width)
    away = lax.dynamic_index_in_dim(view, 1 - inner, 1, False).astype(bf16)
    keep = lax.dynamic_index_in_dim(view, inner, 1, False).astype(f32)
    half = keep + swap_bit(away, "dp", n, 1).astype(f32)
    low = half.astype(bf16)
    total = lax.dynamic_index_in_dim(half, mine, 0, False)
    for k in range(1, outer):
        block = lax.dynamic_index_in_dim(low, (mine + k) % outer, 0, False)
        pairs = [(i, ((i // 2 + k) % outer) * 2 + i % 2) for i in range(n)]
        total = total + lax.ppermute(block, "dp", pairs).astype(f32)
    return total


def dp_sum(v, n):
    bit = 1
    while bit < n:
        v = v + swap_bit(v, "dp", n, bit)
        bit *= 2
    return v


def adamw_step(weight, moment_old, square_old, gradient, step_rate, decay_value, clip_factor):
    correct_one = 1.0 - beta_first**STEP
    correct_two = 1.0 - beta_second**STEP
    clipped = gradient * clip_factor
    moment_new = beta_first * moment_old + (1.0 - beta_first) * clipped
    square_new = beta_second * square_old + (1.0 - beta_second) * clipped * clipped
    divisor = jnp.sqrt(square_new / correct_two) + adam_eps
    weight_new = weight - step_rate * (moment_new / correct_one / divisor + decay_value * weight)
    return (weight_new, moment_new, square_new)


def attend_forward(queries, keyset, valueset, ids):
    rows = queries.shape[0]
    allowed = ids[:, None] == ids[None, :]
    outs, peaks = [], []
    for h in range(queries.shape[1] // HD):
        cut = slice(h * HD, (h + 1) * HD)
        scores = jnp.where(allowed, dot(queries[:, cut], keyset[:, cut], NT) * HD**-0.5, masked_score)
        peak = jnp.max(scores, axis=-1, keepdims=True)
        exponent = jnp.exp(scores - peak)
        total = jnp.sum(exponent, axis=-1, keepdims=True)
        low = (exponent / total).astype(bf16)
        outs.append(dot(low, valueset[:, cut], NN).astype(bf16))
        peaks.append(peak + jnp.log(total))
    return jnp.concatenate(outs, axis=1), jnp.concatenate(peaks, axis=1)


def attend_backward(queries, keyset, valueset, ids, lse, grad_att):
    allowed = ids[:, None] == ids[None, :]
    dqs, dks, dvs = [], [], []
    for h in range(queries.shape[1] // HD):
        cut = slice(h * HD, (h + 1) * HD)
        q, k, v, g = queries[:, cut], keyset[:, cut], valueset[:, cut], grad_att[:, cut]
        scores = jnp.where(allowed, dot(q, k, NT) * HD**-0.5, masked_score)
        probs = jnp.exp(scores - lse[:, h : h + 1])
        low = probs.astype(bf16)
        grad_probs = dot(g, v, NT)
        inner = jnp.sum(probs * grad_probs, axis=-1, keepdims=True)
        gs = (probs * (grad_probs - inner)).astype(bf16)
        dvs.append(dot(low, g, TN))
        dqs.append(dot(gs, k, NN) * HD**-0.5)
        dks.append(dot(gs, q, TN) * HD**-0.5)
    return jnp.concatenate(dqs + dks + dvs, axis=1).astype(bf16)


def build(n):
    def local(
        inputs,
        time_first,
        time_second,
        lengths_first,
        lengths_second,
        cotangent,
        w_qkv,
        m_qkv,
        v_qkv,
        w_proj,
        m_proj,
        v_proj,
        w_up,
        m_up,
        v_up,
        w_down,
        m_down,
        v_down,
        w_vecs,
        m_vecs,
        v_vecs,
        b_heads,
        m_heads,
        v_heads,
        b_hidden,
        m_hidden,
        v_hidden,
    ):
        rows, features = inputs.shape[1], inputs.shape[2]
        r = w_qkv.shape[0]
        width = w_qkv.shape[2]
        tensor_index = lax.axis_index("tensor")
        core = tensor_index % 2

        first_shard = jnp.concatenate(
            [w_qkv.astype(bf16).reshape(r, 3 * width), w_proj.T.astype(bf16)], axis=1
        )
        bulk_shard = jnp.concatenate([w_up.astype(bf16), w_down.T.astype(bf16)], axis=1)
        bulk = lax.all_gather(bulk_shard, "dp", axis=0, tiled=True)
        first = lax.all_to_all(jnp.tile(first_shard, (n, 1)), "dp", 0, 0, tiled=True)
        qkv_matrix = first[:, : 3 * width]
        proj_own = first[:, 3 * width :]
        hidden_width = w_up.shape[1]
        up_matrix, down_matrix = bulk[:, :hidden_width], bulk[:, hidden_width:]

        def spread(v):
            over_y = swap_bit(v, "tensor", 4, 2)
            return jnp.concatenate(
                [v, swap_bit(v, "tensor", 4, 1), over_y, swap_bit(over_y, "tensor", 4, 1)], axis=1
            )

        proj_all = spread(proj_own)

        halves = []
        for b, (times, lengths) in enumerate(
            ((time_first[0], lengths_first[0]), (time_second[0], lengths_second[0]))
        ):
            seqs = times.shape[0]
            ids = segment_ids(lengths, rows)
            pick = (ids[:, None] == jnp.arange(seqs, dtype=jnp.int32)[None, :]).astype(bf16)
            valid = (ids < seqs).astype(f32)[:, None]
            stream = inputs[b].astype(f32) + dot(pick, times, NN)
            xhat, scale = norm_parts(stream)
            normed = (xhat * w_vecs[0] + w_vecs[1]).astype(bf16)
            upstream = cotangent[b].astype(f32) * valid
            halves.append(
                dict(ids=ids, valid=valid, stream=stream, normed=normed, upstream=upstream)
            )

        for s in halves:
            mixed = dot(s["normed"], qkv_matrix, NN)
            s["q"] = (mixed[:, :width] + b_heads[0]).astype(bf16)
            s["k"] = mixed[:, width : 2 * width].astype(bf16)
            s["v"] = (mixed[:, 2 * width :] + b_heads[1]).astype(bf16)
            s["att"], s["lse"] = attend_forward(s["q"], s["k"], s["v"], s["ids"])
            s["att_all"] = spread(s["att"])

        for s in halves:
            s["branch"] = dot(s["att_all"], proj_all, NT) + w_vecs[4]
            s["middle"] = s["stream"] + s["branch"]
            xhat, scale = norm_parts(s["middle"])
            s["normed_two"] = (xhat * w_vecs[2] + w_vecs[3]).astype(bf16)
            hidden = dot(s["normed_two"], up_matrix, NN) + b_hidden
            cdf = 0.5 * (1.0 + lax.erf(hidden * 0.5**0.5))
            pdf = jnp.exp(-0.5 * hidden * hidden) * 0.3989422804014327
            s["active"] = (hidden * cdf).astype(bf16)
            s["upstream_low"] = s["upstream"].astype(bf16)
            grad_active = dot(s["upstream_low"], down_matrix, NN)
            grad_hidden = grad_active * (cdf + hidden * pdf)
            s["offsets"] = jnp.sum(grad_hidden, axis=0)
            s["grad_hidden"] = grad_hidden.astype(bf16)
            s["gnt"] = tensor_sum(dot(s["grad_hidden"], up_matrix, NT), core)

        for s in halves:
            s["two"] = tensor_sum(dot(s["active"], down_matrix, NT), core)

        def joined(key):
            return jnp.concatenate([s[key] for s in halves])

        grad_up = dot(joined("normed_two"), joined("grad_hidden"), TN)
        grad_down = dot(joined("upstream_low"), joined("active"), TN)
        own_bulk = lax.psum_scatter(
            jnp.concatenate([grad_up, grad_down], axis=1).astype(bf16),
            "dp",
            scatter_dimension=0,
            tiled=True,
        ).astype(f32)

        for s in halves:
            gnt = s["gnt"].astype(f32)
            xhat, scale = norm_parts(s["middle"])
            s["gain_two"] = jnp.sum(gnt * xhat, axis=0)
            s["offset_two"] = jnp.sum(gnt, axis=0)
            grad_middle = s["upstream"] + norm_back(gnt * w_vecs[2], xhat, scale)
            s["grad_middle"] = grad_middle
            s["middle_low"] = grad_middle.astype(bf16)
            grad_att = dot(s["middle_low"], proj_own, NN).astype(bf16)
            s["grad_mixed"] = attend_backward(s["q"], s["k"], s["v"], s["ids"], s["lse"], grad_att)
            s["gn"] = tensor_sum(dot(s["grad_mixed"], qkv_matrix, NT), core)

        grad_first = jnp.concatenate(
            [
                dot(joined("normed"), joined("grad_mixed"), TN),
                dot(joined("middle_low"), joined("att"), TN),
            ],
            axis=1,
        )
        own_first = scatter_rows(grad_first, n)

        block_out, input_grad = [], []
        squares = [0.0, 0.0, 0.0]
        for s in halves:
            two = s["two"].astype(f32) + w_vecs[5]
            total = s["middle"] + two
            block_out.append(total.astype(bf16))
            for i, v in enumerate((total, s["branch"], two)):
                squares[i] = squares[i] + jnp.sum(s["valid"] * v * v)
            gn = s["gn"].astype(f32)
            xhat, scale = norm_parts(s["stream"])
            s["gain_one"] = jnp.sum(gn * xhat, axis=0)
            s["offset_one"] = jnp.sum(gn, axis=0)
            input_grad.append(s["grad_middle"] + norm_back(gn * w_vecs[0], xhat, scale))
        block_out = jnp.stack(block_out)
        input_grad = jnp.stack(input_grad)

        def added(key):
            return halves[0][key] + halves[1][key]

        def summed(key):
            return jnp.sum(halves[0][key], axis=0, dtype=f32) + jnp.sum(
                halves[1][key], axis=0, dtype=f32
            )

        mixed_sums = summed("grad_mixed")
        count = jnp.sum(halves[0]["valid"]) + jnp.sum(halves[1]["valid"])
        scalars = jnp.stack([squares[0], squares[1], squares[2], count])
        message = jnp.stack(
            [
                added("gain_one"),
                added("offset_one"),
                added("gain_two"),
                added("offset_two"),
                summed("grad_middle"),
                summed("upstream"),
                jnp.pad(mixed_sums[:width], (0, features - width)),
                jnp.pad(mixed_sums[2 * width :], (0, features - width)),
                added("offsets"),
                jnp.pad(scalars, (0, features - 4)),
            ]
        )
        message = dp_sum(message, n)
        sum_vecs = message[:6]
        sum_heads = message[6:8, :width]
        sum_hidden = message[8]
        sum_squares, sum_count = message[9, :3], message[9, 3]

        matrix_square = dp_sum(jnp.sum(own_bulk * own_bulk) + jnp.sum(own_first * own_first), n)
        partial_square = matrix_square + jnp.sum(sum_heads * sum_heads) + jnp.sum(
            sum_hidden * sum_hidden
        )
        partial_square = partial_square + swap_bit(partial_square, "tensor", 4, 1)
        partial_square = partial_square + swap_bit(partial_square, "tensor", 4, 2)
        total_square = partial_square + jnp.sum(sum_vecs * sum_vecs)
        grad_norm = jnp.sqrt(total_square)
        clip_factor = jnp.minimum(1.0, clip_limit / (grad_norm + 1e-06))

        updates = (
            (w_qkv, m_qkv, v_qkv, own_first[:, : 3 * width].reshape(r, 3, width), matrix_decay),
            (w_proj, m_proj, v_proj, own_first[:, 3 * width :].T, matrix_decay),
            (w_up, m_up, v_up, own_bulk[:, :hidden_width], matrix_decay),
            (w_down, m_down, v_down, own_bulk[:, hidden_width:].T, matrix_decay),
            (w_vecs, m_vecs, v_vecs, sum_vecs, 0.0),
            (b_heads, m_heads, v_heads, sum_heads, 0.0),
            (b_hidden, m_hidden, v_hidden, sum_hidden, 0.0),
        )
        outs = [block_out, input_grad, grad_norm.reshape(1), jnp.sqrt(sum_squares / (sum_count * features))]
        for (weight, moment, square, gradient, decay), rate in zip(updates, step_rates):
            outs.extend(adamw_step(weight, moment, square, gradient, rate, decay, clip_factor))
        return tuple(outs)

    return local


def solution(mesh):
    rows = P(None, "dp", None)
    group = P("dp", None, None)
    qkv, proj, up = P("dp", None, "tensor"), P("tensor", "dp"), P("dp", "tensor")
    params = [qkv] * 3 + [proj] * 3 + [up] * 3 + [proj] * 3 + [P()] * 3
    params += [P(None, "tensor")] * 3 + [P("tensor")] * 3
    return jax.shard_map(
        build(mesh.shape["dp"]),
        mesh=mesh,
        in_specs=(rows, group, group, P("dp", None), P("dp", None), rows, *params),
        out_specs=(rows, rows, P(), P(), *params),
        check_vma=False,
    )
```

```python
import functools

import jax
import jax.numpy as jnp
from jax import lax
from jax.experimental import pallas as pl
from jax.experimental.pallas import tpu as pltpu
from jax.sharding import PartitionSpec as P

HD = 64
STEP = 5
TILE = 128
BLOCK = 256
CHUNK = 192
REACH = (64, 128)

norm_eps = 1e-05
clip_limit = 1.0
beta_first = 0.5
beta_second = 0.5
adam_eps = 1e-08
matrix_decay = 0.01
masked_score = -1e30
step_rates = (0.03, 0.2, 0.03, 0.015, 0.3, 0.3, 0.3)
bf16 = jnp.bfloat16
f32 = jnp.float32

NN = ((1,), (0,))
NT = ((1,), (1,))
TN = ((0,), (0,))


def dot(a, b, dims):
    return lax.dot_general(a, b, (dims, ((), ())), preferred_element_type=f32)


def shape(dims, dtype):
    return jax.ShapeDtypeStruct(dims, dtype)


def call(body, outs, words, arrays, after=(), limit=16, scratch=()):
    count = len(after)

    def kernel(*refs):
        body(*refs[: len(words)], *refs[len(words) + count :])

    in_vmem = pl.BlockSpec(memory_space=pltpu.VMEM)
    in_specs = [pl.BlockSpec(memory_space=pltpu.SMEM)] * len(words)
    in_specs += [pl.BlockSpec(memory_space=pl.ANY)] * count
    operands = []
    for v in arrays:
        if isinstance(v, tuple):
            v, plane = v
            in_specs.append(pl.BlockSpec((None, *v.shape[1:]), functools.partial(plane_index, plane)))
        else:
            in_specs.append(in_vmem)
        operands.append(v)
    planes = any(isinstance(v, tuple) for v in arrays)
    return pl.pallas_call(
        kernel,
        grid=(1,) if planes else (),
        out_shape=outs,
        in_specs=in_specs,
        out_specs=(in_vmem,) * len(outs) if isinstance(outs, tuple) else in_vmem,
        scratch_shapes=list(scratch),
        compiler_params=pltpu.CompilerParams(vmem_limit_bytes=limit * 2**20),
        cost_estimate=pl.CostEstimate(flops=0, bytes_accessed=0, transcendentals=0),
    )(*words, *after, *operands)


def plane_index(plane, step):
    return (plane, 0, 0)


def core_index():
    return lax.rem(lax.axis_index("tensor"), 2)


def dp_place():
    me = lax.axis_index("dp")
    return lax.div(me, 2), lax.rem(me, 2)


def rows_sum(v):
    return jnp.sum(v, axis=0, keepdims=True)


def whole_sum(v):
    return jnp.sum(rows_sum(v), axis=1, keepdims=True)


def norm_parts(stream):
    center = stream - jnp.mean(stream, axis=-1, keepdims=True)
    spread = jnp.mean(center * center, axis=-1, keepdims=True)
    scale = lax.rsqrt(spread + norm_eps)
    return center * scale, scale


def norm_back(scaled, xhat, scale):
    mean = jnp.mean(scaled, axis=-1, keepdims=True)
    return scale * (scaled - mean - xhat * jnp.mean(scaled * xhat, axis=-1, keepdims=True))


def adamw_step(weight, moment_old, square_old, gradient, step_rate, decay_value, clip_factor):
    correct_one = 1.0 - beta_first**STEP
    correct_two = 1.0 - beta_second**STEP
    clipped = gradient * clip_factor
    moment_new = beta_first * moment_old + (1.0 - beta_first) * clipped
    square_new = beta_second * square_old + (1.0 - beta_second) * clipped * clipped
    divisor = jnp.sqrt(square_new / correct_two) + adam_eps
    weight_new = weight - step_rate * (moment_new / correct_one / divisor + decay_value * weight)
    return (weight_new, moment_new, square_new)


def swap_bit(v, axis, size, bit):
    return lax.ppermute(v, axis, [(i, i ^ bit) for i in range(size)])


def outer_blocks(shard, n):
    outer = n // 2
    blocks = []
    for k in range(1, outer):
        pairs = [(i, ((i // 2 - k) % outer) * 2 + i % 2) for i in range(n)]
        blocks.append(lax.ppermute(shard, "dp", pairs))
    return blocks + [shard]


def dp_sum(v, n):
    bit = 1
    while bit < n:
        v = v + swap_bit(v, "dp", n, bit)
        bit *= 2
    return v


def stack_kernel(*refs):
    r = refs[0].shape[0]
    for j, ref in enumerate(refs[:-1]):
        refs[-1][j * r : (j + 1) * r, :] = ref[...]


def order_kernel(r, own_ref, other_ref, *out_refs):
    mine, inner = dp_place()
    outer = own_ref.shape[0] // r
    for j in range(outer):
        source = lax.rem(mine + 1 + j, outer)
        for ref, side in ((own_ref, inner), (other_ref, 1 - inner)):
            start = pl.multiple_of((source * 2 + side) * r, 16)
            column = 0
            for out_ref in out_refs:
                stop = column + out_ref.shape[1]
                out_ref[pl.ds(start, r), :] = ref[j * r : (j + 1) * r, column:stop]
                column = stop


def stacked(blocks, after):
    r, width = blocks[0].shape
    if r % 16:
        return jnp.concatenate(blocks)
    return call(stack_kernel, shape((len(blocks) * r, width), bf16), (), blocks, after, 8)


def in_order(own, other, n, *widths):
    r, width = own.shape[0] * 2 // n, own.shape[1]
    if r % 16:
        mine, inner = dp_place()
        own, other = (v.reshape(n // 2, r, width) for v in (own, other))
        sides = [jnp.where(inner == 0, own, other), jnp.where(inner == 0, other, own)]
        rows = jnp.roll(jnp.stack(sides, axis=1), mine + 1, axis=0).reshape(n * r, width)
        return tuple(jnp.split(rows, [sum(widths[:i]) for i in range(1, len(widths))], axis=1))
    outs = tuple(shape((n * r, w), bf16) for w in widths)
    return call(functools.partial(order_kernel, r), outs, (), (own, other), (), 8)


def add_kernel(keep_ref, moved_ref, out_ref):
    out_ref[...] = (keep_ref[...].astype(f32) + moved_ref[...].astype(f32)).astype(bf16)


def add(keep, moved, after=()):
    return call(add_kernel, shape(keep.shape, bf16), (), (keep, moved), after, 8)


def over_core(v):
    return swap_bit(v, "tensor", 4, 1)


def over_chip(v):
    return swap_bit(v, "tensor", 4, 2)


def pack_first_kernel(qkv_ref, proj_ref, qk_ref, vp_ref):
    qk_ref[...] = jnp.concatenate([qkv_ref[0], qkv_ref[1]], axis=1).astype(bf16)
    vp_ref[...] = jnp.concatenate([qkv_ref[2], proj_ref[...].T], axis=1).astype(bf16)


def cast_kernel(*refs):
    half = len(refs) // 2
    for source, out in zip(refs[:half], refs[half:]):
        out[...] = source[...].astype(bf16)


def segment_grid(lengths_ref, dims, axis):
    places = lax.broadcasted_iota(jnp.int32, dims, axis)
    ids = jnp.zeros(dims, jnp.int32)
    bound = jnp.int32(0)
    for k in range(lengths_ref.shape[1]):
        bound = bound + lengths_ref[0, k]
        ids = ids + (places >= bound).astype(jnp.int32)
    return ids


def valid_count(lengths_ref):
    total = jnp.int32(0)
    for k in range(lengths_ref.shape[1]):
        total = total + lengths_ref[0, k]
    return total


def first_norm_kernel(lengths_one, lengths_two, inputs_ref, times_one, times_two, vecs_ref, *refs):
    rows = inputs_ref.shape[1]
    for b, (lengths_ref, times_ref) in enumerate(((lengths_one, times_one), (lengths_two, times_two))):
        stream_ref, normed_ref = refs[2 * b : 2 * b + 2]
        depth = times_ref.shape[0]
        ids = segment_grid(lengths_ref, (rows, 1), 0)
        for start in range(0, rows, BLOCK):
            here = slice(start, start + BLOCK)
            lanes = lax.broadcasted_iota(jnp.int32, (BLOCK, depth), 1)
            pick = (ids[here] == lanes).astype(f32).astype(bf16)
            stream = inputs_ref[b, here, :].astype(f32) + dot(pick, times_ref[...], NN)
            stream_ref[here, :] = stream
            xhat, _ = norm_parts(stream)
            normed_ref[here, :] = (xhat * vecs_ref[0:1, :] + vecs_ref[1:2, :]).astype(bf16)


def windows(rows, reach):
    size = min(rows, TILE + 2 * reach)
    out = []
    for start in range(0, rows, TILE):
        low = max(0, start - reach)
        high = min(rows, start + TILE + reach)
        if (high - low) % 128:
            low = min(low, rows - size)
            high = low + size
        out.append((start, low, high))
    return out


def split_heads(low, rows, q_s, k_s, v_s):
    heads = q_s.shape[0]
    width = heads * HD
    for h in range(heads):
        cut = h * HD
        q_s[h, rows, :] = low[:, cut : cut + HD] * jnp.array(HD**-0.5, bf16)
        k_s[h, rows, :] = low[:, width + cut : width + cut + HD]
        v_s[h, rows, :] = low[:, 2 * width + cut : 2 * width + cut + HD]


def forward_kernel(reach, lengths_ref, normed_ref, qk_ref, wv_ref, bias_ref, att_ref, qkv_ref, lse_ref, q_s, k_s, v_s):
    rows, width = att_ref.shape
    heads = range(width // HD)
    for start in range(0, rows, BLOCK):
        piece = slice(start, start + BLOCK)
        normed = normed_ref[piece, :]
        pair = dot(normed, qk_ref[...], NN)
        values = dot(normed, wv_ref[...], NN)
        low = (jnp.concatenate([pair, values], axis=1) + bias_ref[...]).astype(bf16)
        qkv_ref[piece, :] = low
        split_heads(low, piece, q_s, k_s, v_s)
    ids_col = segment_grid(lengths_ref, (rows, 1), 0)
    ids_row = segment_grid(lengths_ref, (1, rows), 1)
    lanes = lax.broadcasted_iota(jnp.int32, (TILE, 128), 1)
    for start, low, high in windows(rows, reach):
        tile = slice(start, start + TILE)
        allowed = ids_col[tile] == ids_row[:, low:high]
        scores = [dot(q_s[h, tile, :], k_s[h, low:high, :], NT) for h in heads]
        scores = [jnp.where(allowed, s, masked_score) for s in scores]
        peaks = [jnp.max(s, axis=-1, keepdims=True) for s in scores]
        exponents = [jnp.exp(s - p) for s, p in zip(scores, peaks)]
        totals = [jnp.sum(e, axis=-1, keepdims=True) for e in exponents]
        probs = [(e * (1.0 / t)).astype(bf16) for e, t in zip(exponents, totals)]
        outs = [dot(p, v_s[h, low:high, :], NN).astype(bf16) for h, p in enumerate(probs)]
        att_ref[tile, :] = jnp.concatenate(outs, axis=1)
        logs = jnp.zeros((TILE, 128), f32)
        for h in heads:
            logs = jnp.where(lanes == h, peaks[h] + jnp.log(totals[h]), logs)
        lse_ref[tile, :] = logs


def hidden_kernel(lengths_ref, *refs):
    att_refs, proj_refs = refs[:4], refs[4:8]
    stream_ref, vecs_ref, up_ref, down_ref, bias_ref, cot_ref = refs[8:14]
    middle_ref, normed_ref, active_ref, upstream_ref, grad_ref, away_ref, keep_ref, square_ref, offset_ref = refs[14:]
    rows, features = stream_ref.shape
    half = rows // 2
    core = core_index()
    total = valid_count(lengths_ref)
    squares = jnp.zeros((1, features), f32)
    offsets = jnp.zeros((1, grad_ref.shape[1]), f32)
    for out_ref, base in ((away_ref, (1 - core) * half), (keep_ref, core * half)):
        for start in range(0, half, CHUNK):
            off = pl.multiple_of(base + start, CHUNK)
            here = pl.ds(off, CHUNK)
            valid = off + lax.broadcasted_iota(jnp.int32, (CHUNK, 1), 0) < total
            upstream = jnp.where(valid, cot_ref[here, :].astype(f32), 0.0).astype(bf16)
            upstream_ref[here, :] = upstream
            own, near, over, across = (dot(a[here, :], p[...], NT) for a, p in zip(att_refs, proj_refs))
            branch = ((own + near) + (over + across)) + vecs_ref[4:5, :]
            kept = jnp.where(valid, branch, 0.0)
            squares = squares + rows_sum(kept * kept)
            middle = stream_ref[here, :] + branch
            middle_ref[here, :] = middle
            xhat, _ = norm_parts(middle)
            normed = (xhat * vecs_ref[2:3, :] + vecs_ref[3:4, :]).astype(bf16)
            normed_ref[here, :] = normed
            hidden = dot(normed, up_ref[...], NN) + bias_ref[...]
            cdf = 0.5 + 0.5 * lax.erf(hidden * 0.5**0.5)
            pdf = jnp.exp(-0.5 * hidden * hidden) * 0.3989422804014327
            active_ref[here, :] = (hidden * cdf).astype(bf16)
            grad = dot(upstream, down_ref[...], NN) * (cdf + hidden * pdf)
            offsets = offsets + rows_sum(grad)
            low = grad.astype(bf16)
            grad_ref[here, :] = low
            out_ref[start : start + CHUNK, :] = dot(low, up_ref[...], NT).astype(out_ref.dtype)
    square_ref[...] = squares
    offset_ref[...] = offsets


def down_kernel(active_ref, down_ref, away_ref, keep_ref):
    half = active_ref.shape[0] // 2
    core = core_index()
    for out_ref, base in ((away_ref, (1 - core) * half), (keep_ref, core * half)):
        here = pl.ds(pl.multiple_of(base, half), half)
        out_ref[...] = dot(active_ref[here, :], down_ref[...], NT).astype(out_ref.dtype)


def products_kernel(pairs, *refs):
    out_ref = refs[-1]
    for m in range(0, out_ref.shape[0], BLOCK):
        cut = slice(m, m + BLOCK)
        column = 0
        for p in range(pairs):
            left_one, left_two, right_one, right_two = refs[4 * p : 4 * p + 4]
            part = dot(left_one[:, cut], right_one[...], TN) + dot(left_two[:, cut], right_two[...], TN)
            out_ref[cut, column : column + part.shape[1]] = part.astype(out_ref.dtype)
            column += part.shape[1]


def parted_kernel(r, *refs):
    away_ref, keep_ref, full_s = refs[-3:]
    products_kernel(len(refs) // 4, *refs[:-3], full_s)
    _, inner = dp_place()
    for o in range(away_ref.shape[0] // r):
        for out_ref, side in ((away_ref, 1 - inner), (keep_ref, inner)):
            start = pl.multiple_of((o * 2 + side) * r, 8)
            out_ref[o * r : (o + 1) * r, :] = full_s[pl.ds(start, r), :].astype(bf16)


def parted(arrays, n, after):
    rows, width = arrays[0].shape[1], sum(v.shape[1] for v in arrays[2::4])
    r = rows // n
    if r % 16:
        kernel = functools.partial(products_kernel, len(arrays) // 4)
        full = call(kernel, shape((rows, width), bf16), (), arrays, after)
        view = full.reshape(n // 2, 2, r, width)
        _, inner = dp_place()
        pieces = [lax.dynamic_index_in_dim(view, i, 1, False) for i in (1 - inner, inner)]
        return [v.reshape(rows // 2, width) for v in pieces]
    outs = (shape((rows // 2, width), bf16),) * 2
    scratch = [pltpu.VMEM((rows, width), f32)]
    return call(functools.partial(parted_kernel, r), outs, (), arrays, after, 24, scratch)


def blocks_kernel(r, keep_ref, moved_ref, own_ref, *out_refs):
    mine, _ = dp_place()
    outer = keep_ref.shape[0] // r
    for k, out_ref in enumerate((own_ref, *out_refs)):
        here = pl.ds(pl.multiple_of(lax.rem(mine + k, outer) * r, 16), r)
        total = keep_ref[here, :].astype(f32) + moved_ref[here, :].astype(f32)
        out_ref[...] = total.astype(out_ref.dtype)


def scattered(away, keep, n, after):
    outer, width = n // 2, keep.shape[1]
    r = keep.shape[0] // outer
    moved = swap_bit(away, "dp", n, 1)
    if r % 16:
        mine, _ = dp_place()
        total = (keep.astype(f32) + moved.astype(f32)).reshape(outer, r, width)
        own, *sent = (lax.dynamic_index_in_dim(total, lax.rem(mine + k, outer), 0, False) for k in range(outer))
        sent = [v.astype(bf16) for v in sent]
    else:
        outs = (shape((r, width), f32),) + (shape((r, width), bf16),) * (outer - 1)
        own, *sent = call(functools.partial(blocks_kernel, r), outs, (), (keep, moved), after, 8)
    blocks = [own]
    for k in range(1, outer):
        pairs = [(i, ((i // 2 + k) % outer) * 2 + i % 2) for i in range(n)]
        blocks.append(lax.ppermute(sent[k - 1], "dp", pairs))
    return blocks


def backward_kernel(
    reach,
    lengths_ref,
    both_ref,
    other_ref,
    middle_ref,
    upstream_ref,
    vecs_ref,
    qk_ref,
    wv_ref,
    proj_ref,
    qkv_ref,
    lse_ref,
    grad_middle_ref,
    low_ref,
    mixed_ref,
    away_ref,
    keep_ref,
    sums_ref,
    heads_ref,
    q_s,
    k_s,
    v_s,
    g_s,
    dk_s,
    dv_s,
):
    rows, features = middle_ref.shape
    half = rows // 2
    width = qkv_ref.shape[1] // 3
    heads = range(width // HD)
    core = core_index()
    ids_col = segment_grid(lengths_ref, (rows, 1), 0)
    ids_row = segment_grid(lengths_ref, (1, rows), 1)
    gain = vecs_ref[2:3, :]
    sums = []
    for piece_ref, base in ((both_ref, core * half), (other_ref, (1 - core) * half)):

        def rows_step(t, acc, piece_ref=piece_ref, base=base):
            off = pl.multiple_of(base + t * TILE, TILE)
            here = pl.ds(off, TILE)
            gnt = piece_ref[pl.ds(pl.multiple_of(t * TILE, TILE), TILE), :].astype(f32)
            xhat, scale = norm_parts(middle_ref[here, :])
            upstream = upstream_ref[here, :].astype(f32)
            grad_middle = upstream + norm_back(gnt * gain, xhat, scale)
            grad_middle_ref[here, :] = grad_middle
            low_ref[here, :] = grad_middle.astype(bf16)
            terms = (gnt * xhat, gnt, grad_middle, upstream)
            return tuple(a + rows_sum(v) for a, v in zip(acc, terms))

        start = (jnp.zeros((1, features), f32),) * 4
        sums.append(lax.fori_loop(0, half // TILE, rows_step, start))
    sums_ref[...] = jnp.concatenate([a + b for a, b in zip(*sums)], axis=0)
    for start in range(0, rows, BLOCK):
        piece = slice(start, start + BLOCK)
        split_heads(qkv_ref[piece, :], piece, q_s, k_s, v_s)
        grad_att = dot(low_ref[piece, :], proj_ref[...], NN).astype(bf16)
        for h in heads:
            g_s[h, piece, :] = grad_att[:, h * HD : (h + 1) * HD]
    dk_s[...] = jnp.zeros_like(dk_s)
    dv_s[...] = jnp.zeros_like(dv_s)
    for start, low, high in windows(rows, reach):
        tile = slice(start, start + TILE)
        keys = slice(low, high)
        allowed = ids_col[tile] == ids_row[:, keys]
        scores = [dot(q_s[h, tile, :], k_s[h, keys, :], NT) for h in heads]
        grad_probs = [dot(g_s[h, tile, :], v_s[h, keys, :], NT) for h in heads]
        probs = [jnp.exp(jnp.where(allowed, s, masked_score) - lse_ref[tile, h : h + 1]) for h, s in enumerate(scores)]
        inner = [jnp.sum(p * g, axis=-1, keepdims=True) for p, g in zip(probs, grad_probs)]
        grads = [(p * (g - i)).astype(bf16) for p, g, i in zip(probs, grad_probs, inner)]
        lows = [p.astype(bf16) for p in probs]
        dqs = [(dot(g, k_s[h, keys, :], NN) * HD**-0.5).astype(bf16) for h, g in enumerate(grads)]
        mixed_ref[tile, :width] = jnp.concatenate(dqs, axis=1)
        dks = [dot(g, q_s[h, tile, :], TN) for h, g in enumerate(grads)]
        dvs = [dot(p, g_s[h, tile, :], TN) for h, p in enumerate(lows)]
        for h in heads:
            dk_s[h, keys, :] += dks[h]
            dv_s[h, keys, :] += dvs[h]
    for start in range(0, rows, BLOCK):
        piece = slice(start, start + BLOCK)
        both = [ref[h, piece, :].astype(bf16) for ref in (dk_s, dv_s) for h in heads]
        mixed_ref[piece, width:] = jnp.concatenate(both, axis=1)
    heads_ref[...] = rows_sum(mixed_ref[...].astype(f32))
    for out_ref, base in ((away_ref, (1 - core) * half), (keep_ref, core * half)):
        here = pl.ds(pl.multiple_of(base, half), half)
        part = dot(mixed_ref[here, : 2 * width], qk_ref[...], NT)
        part = part + dot(mixed_ref[here, 2 * width :], wv_ref[...], NT)
        out_ref[...] = part.astype(out_ref.dtype)


def input_grad_kernel(both_ref, other_ref, stream_ref, middle_ref, vecs_ref, *refs):
    out_ref, sums_ref = refs[-2:]
    rows, features = stream_ref.shape
    half = rows // 2
    core = core_index()
    gain = vecs_ref[0:1, :]
    sums = []
    for piece_ref, base in ((both_ref, core * half), (other_ref, (1 - core) * half)):

        def rows_step(t, acc, piece_ref=piece_ref, base=base):
            here = pl.ds(pl.multiple_of(base + t * TILE, TILE), TILE)
            grad = piece_ref[pl.ds(pl.multiple_of(t * TILE, TILE), TILE), :].astype(f32)
            xhat, scale = norm_parts(stream_ref[here, :])
            out_ref[0, here, :] = middle_ref[here, :] + norm_back(grad * gain, xhat, scale)
            return (acc[0] + rows_sum(grad * xhat), acc[1] + rows_sum(grad))

        start = (jnp.zeros((1, features), f32),) * 2
        sums.append(lax.fori_loop(0, half // TILE, rows_step, start))
    sums_ref[...] = jnp.concatenate([a + b for a, b in zip(*sums)], axis=0)


def input_grad_call(which, both, other, stream, middle, vecs, filled, after):
    rows, features = stream.shape
    count = len(after)

    def kernel(*refs):
        input_grad_kernel(*refs[count:])

    whole = pl.BlockSpec(memory_space=pltpu.VMEM)
    anywhere = pl.BlockSpec(memory_space=pl.ANY)
    return pl.pallas_call(
        kernel,
        grid=(1,),
        out_shape=(shape((2, rows, features), f32), shape((2, features), f32)),
        in_specs=[anywhere] * count + [whole] * 5 + [anywhere] * len(filled),
        out_specs=(pl.BlockSpec((1, rows, features), lambda i: (which, 0, 0)), whole),
        input_output_aliases={count + 5: 0} if filled else {},
        compiler_params=pltpu.CompilerParams(vmem_limit_bytes=24 * 2**20),
        cost_estimate=pl.CostEstimate(flops=0, bytes_accessed=0, transcendentals=0),
    )(*after, both, other, stream, middle, vecs, *filled)


def output_kernel(lengths_one, lengths_two, *refs):
    vecs_ref, branch_one, branch_two, out_ref, sums_ref = refs[6:]
    features = out_ref.shape[2]
    half = out_ref.shape[1] // 2
    core = core_index()
    sums = []
    count = jnp.int32(0)
    for b, lengths_ref in enumerate((lengths_one, lengths_two)):
        total = valid_count(lengths_ref)
        count = count + total
        both_ref, other_ref, middle_ref = refs[3 * b : 3 * b + 3]
        for piece_ref, base in ((both_ref, core * half), (other_ref, (1 - core) * half)):

            def rows_step(t, acc, piece_ref=piece_ref, base=base, middle_ref=middle_ref, total=total, b=b):
                off = pl.multiple_of(base + t * TILE, TILE)
                here = pl.ds(off, TILE)
                two = piece_ref[pl.ds(pl.multiple_of(t * TILE, TILE), TILE), :].astype(f32) + vecs_ref[5:6, :]
                whole = middle_ref[here, :] + two
                out_ref[b, here, :] = whole.astype(bf16)
                valid = off + lax.broadcasted_iota(jnp.int32, (TILE, 1), 0) < total
                terms = [jnp.where(valid, v, 0.0) for v in (whole, two)]
                return tuple(a + rows_sum(v * v) for a, v in zip(acc, terms))

            start = (jnp.zeros((1, features), f32),) * 2
            sums.append(lax.fori_loop(0, half // TILE, rows_step, start))
    whole, two = ((a + b) + (c + d) for a, b, c, d in zip(*sums))
    lines = [jnp.sum(v, axis=1, keepdims=True) for v in (whole, branch_one[...] + branch_two[...], two)]
    lines.append(jnp.full((1, 1), count.astype(f32), f32))
    for i in range(8):
        sums_ref[i : i + 1, :] = jnp.broadcast_to(lines[min(i, 3)], (1, 128))


def message_kernel(*refs):
    out_ref, grads_ref = refs[-2:]
    norm_one, norm_two, sums_one, sums_two, off_one, off_two, heads_one, heads_two = refs[-10:-2]
    block_refs = refs[:-10]
    count = len(block_refs) // 2
    width = heads_one.shape[1] // 3
    column = 0
    squares = jnp.zeros((1, 1), f32)
    for group in (block_refs[:count], block_refs[count:]):
        grad = group[0][...]
        for ref in group[1:]:
            grad = grad + ref[...].astype(f32)
        stop = column + grad.shape[1]
        grads_ref[:, column:stop] = grad
        squares = squares + whole_sum(grad * grad)
        column = stop
    out_ref[...] = jnp.zeros_like(out_ref)
    out_ref[0:2, :] = norm_one[...] + norm_two[...]
    out_ref[2:6, :] = sums_one[...] + sums_two[...]
    out_ref[6:7, :] = off_one[...] + off_two[...]
    heads = heads_one[...] + heads_two[...]
    out_ref[8:9, :width] = heads[:, :width]
    out_ref[9:10, :width] = heads[:, 2 * width :]
    out_ref[10:11, :] = jnp.broadcast_to(squares, (1, out_ref.shape[1]))


def partial_kernel(message_ref, out_ref):
    squares = whole_sum(message_ref[8:10, :] * message_ref[8:10, :])
    squares = squares + whole_sum(message_ref[6:7, :] * message_ref[6:7, :])
    out_ref[...] = jnp.broadcast_to(squares + message_ref[10:11, 0:1], out_ref.shape)


def adamw_kernel(partial_ref, moved_ref, message_ref, grads_ref, *refs):
    count = 21
    sources, targets, norm_ref = refs[:count], refs[count : 2 * count], refs[2 * count]
    inputs, outputs = refs[2 * count + 1 : 3 * count + 1], refs[3 * count + 1 : 4 * count + 1]
    read_sems, write_sems = refs[4 * count + 1 :]
    reads = [pltpu.make_async_copy(sources[i], inputs[i], read_sems.at[i]) for i in range(count)]
    writes = [pltpu.make_async_copy(outputs[i], targets[i], write_sems.at[i]) for i in range(count)]
    for copy in reads:
        copy.start()
    width = inputs[0].shape[2]
    hidden = inputs[6].shape[1]
    vecs = message_ref[0:6, :]
    norm = jnp.sqrt(partial_ref[0:1, 0:1] + moved_ref[0:1, 0:1] + whole_sum(vecs * vecs))
    norm_ref[...] = jnp.broadcast_to(norm, norm_ref.shape)
    clip = jnp.minimum(1.0, clip_limit / (norm + 1e-06))

    def step(p, gradient, at=Ellipsis):
        weight, moment, square = (ref[at] for ref in inputs[3 * p : 3 * p + 3])
        decay = matrix_decay if p < 4 else 0.0
        values = adamw_step(weight, moment, square, gradient, step_rates[p], decay, clip)
        for ref, value in zip(outputs[3 * p : 3 * p + 3], values):
            ref[at] = value

    start = 4 * width
    parts = (
        tuple((grads_ref[:, j * width : (j + 1) * width], j) for j in range(3)),
        ((grads_ref[:, 3 * width : start].T,),),
        ((grads_ref[:, start : start + hidden],),),
        ((grads_ref[:, start + hidden :],),),
        ((vecs,),),
        ((message_ref[8:10, : inputs[15].shape[1]],),),
        ((message_ref[6:7, :],),),
    )
    for p, steps in enumerate(parts):
        for copy in reads[3 * p : 3 * p + 3]:
            copy.wait()
        for arguments in steps:
            step(p, *arguments)
        for copy in writes[3 * p : 3 * p + 3]:
            copy.start()
    for copy in writes:
        copy.wait()


def adamw_call(partial, moved, message, grads, state):
    in_vmem = pl.BlockSpec(memory_space=pltpu.VMEM)
    anywhere = pl.BlockSpec(memory_space=pltpu.MemorySpace.HBM)
    count = len(state)
    return pl.pallas_call(
        adamw_kernel,
        out_shape=tuple(shape(v.shape, f32) for v in state) + (shape((1, 128), f32),),
        in_specs=[in_vmem] * 4 + [anywhere] * count,
        out_specs=(anywhere,) * count + (in_vmem,),
        scratch_shapes=[pltpu.VMEM(v.shape, f32) for v in state] * 2 + [pltpu.SemaphoreType.DMA((count,))] * 2,
        compiler_params=pltpu.CompilerParams(vmem_limit_bytes=24 * 2**20),
        cost_estimate=pl.CostEstimate(flops=10**7, bytes_accessed=10**7, transcendentals=0),
    )(partial, moved, message, grads, *state)


def build(n):
    def local(
        inputs,
        time_first,
        time_second,
        lengths_first,
        lengths_second,
        cotangent,
        w_qkv,
        m_qkv,
        v_qkv,
        w_proj,
        m_proj,
        v_proj,
        w_up,
        m_up,
        v_up,
        w_down,
        m_down,
        v_down,
        w_vecs,
        m_vecs,
        v_vecs,
        b_heads,
        m_heads,
        v_heads,
        b_hidden,
        m_hidden,
        v_hidden,
    ):
        rows, features = inputs.shape[1], inputs.shape[2]
        r, _, width = w_qkv.shape
        hidden = w_up.shape[1]
        heads = width // HD
        half = rows // 2
        lengths = (lengths_first, lengths_second)
        whole_f = shape((rows, features), f32)
        whole_b = shape((rows, features), bf16)
        half_b = shape((half, features), bf16)
        half_f = shape((half, features), f32)
        line = shape((1, features), f32)

        qkv_planes = w_qkv.transpose(1, 0, 2)
        qk_shard, vp_shard = call(
            pack_first_kernel, (shape((r, 2 * width), bf16),) * 2, (), (qkv_planes, w_proj), (), 8
        )
        qk_blocks, vp_blocks = outer_blocks(qk_shard, n), outer_blocks(vp_shard, n)
        stream_one, normed_one, stream_two, normed_two = call(
            first_norm_kernel,
            (whole_f, whole_b) * 2,
            lengths,
            (inputs, *(jnp.pad(t[0], ((0, 16 - t.shape[1]), (0, 0))) for t in (time_first, time_second)), w_vecs),
            (qk_shard,),
            24,
        )
        stream, normed = (stream_one, stream_two), (normed_one, normed_two)
        qk_own = stacked(qk_blocks, (normed_two,))
        qk_other = swap_bit(qk_own, "dp", n, 1)
        up_shard, down_shard = call(
            cast_kernel, (shape((r, hidden), bf16),) * 2, (), (w_up, w_down.T), (qk_own,), 8
        )
        up_blocks = outer_blocks(up_shard, n)
        vp_own = stacked(vp_blocks, (up_shard,))
        vp_other = swap_bit(vp_own, "dp", n, 1)
        down_blocks = outer_blocks(down_shard, n)
        (qk,) = in_order(qk_own, qk_other, n, 2 * width)
        wv, proj_own = in_order(vp_own, vp_other, n, width, width)

        def spread(v):
            moved = over_chip(v)
            return [v, over_core(v), moved, over_core(moved)]

        proj = spread(proj_own)
        bias = jnp.concatenate([b_heads[0], jnp.zeros_like(b_heads[0]), b_heads[1]])[None]
        head_low = pltpu.VMEM((heads, rows, HD), bf16)
        head_full = pltpu.VMEM((heads, rows, HD), f32)

        after = (proj_own,)
        att, qkv, lse, att_all = [], [], [], []
        for b in range(2):
            a, q, l = call(
                functools.partial(forward_kernel, REACH[b]),
                (shape((rows, width), bf16), shape((rows, 3 * width), bf16), shape((rows, 128), f32)),
                (lengths[b],),
                (normed[b], qk, wv, bias),
                after,
                12,
                [head_low] * 3,
            )
            att.append(a)
            qkv.append(q)
            lse.append(l)
            att_all.append(spread(a))
            if b == 0:
                up_own = stacked(up_blocks, (l,))
                up_other = swap_bit(up_own, "dp", n, 1)
                down_own = stacked(down_blocks, (up_own,))
                down_other = swap_bit(down_own, "dp", n, 1)
                after = (down_own, proj[2])
        (up,) = in_order(up_own, up_other, n, hidden)
        (down,) = in_order(down_own, down_other, n, hidden)
        after = (lse[1], att_all[0][2])

        names = [[] for _ in range(9)]
        low = []
        for b in range(2):
            outs = call(
                hidden_kernel,
                (
                    whole_f,
                    whole_b,
                    shape((rows, hidden), bf16),
                    whole_b,
                    shape((rows, hidden), bf16),
                    half_b,
                    half_f,
                    line,
                    shape((1, hidden), f32),
                ),
                (lengths[b],),
                (*att_all[b], *proj, stream[b], w_vecs, up, down, b_hidden[None], (cotangent, b)),
                after,
                20,
            )
            for kept, v in zip(names, outs):
                kept.append(v)
            low.append(add(outs[6], over_core(outs[5]), (outs[-1],)))
            after = (low[b],)
        middle, normed_mid, active, upstream, grad_hidden, away, keep, branch_square, offsets = names

        bulk = parted((*normed_mid, *grad_hidden, *upstream, *active), n, after)
        after = (bulk[0],)
        parts = []
        for b in range(2):
            parts.append(call(down_kernel, (half_b, half_f), (), (active[b], down), after))
            after = (parts[b][0],)
        gnt = []
        for b in range(2):
            both = add(low[b], over_chip(low[b]), after if b == 0 else ())
            gnt.append((both, over_core(both)))
        after = (gnt[0][0],)

        grad_middle, middle_low, grad_mixed, sums, head_sums, back_low = [], [], [], [], [], []
        for b in range(2):
            outs = call(
                functools.partial(backward_kernel, REACH[b]),
                (
                    whole_f,
                    whole_b,
                    shape((rows, 3 * width), bf16),
                    half_b,
                    half_f,
                    shape((4, features), f32),
                    shape((1, 3 * width), f32),
                ),
                (lengths[b],),
                (*gnt[b], middle[b], upstream[b], w_vecs, qk, wv, proj_own, qkv[b], lse[b]),
                after,
                24,
                [head_low] * 4 + [head_full] * 2,
            )
            grad_middle.append(outs[0])
            middle_low.append(outs[1])
            grad_mixed.append(outs[2])
            sums.append(outs[5])
            head_sums.append(outs[6])
            back_low.append(add(outs[4], over_core(outs[3])))
            after = (back_low[b],)

        bulk_grads = scattered(*bulk, n, after)
        first = parted((*normed, *grad_mixed, *middle_low, *att), n, (bulk_grads[0],))
        both = add(back_low[0], over_chip(back_low[0]), (first[0],))
        pieces = [(both, over_core(both))]
        first_grads = scattered(*first, n, (both,))
        both = add(back_low[1], over_chip(back_low[1]), (first_grads[0],))
        pieces.append((both, over_core(both)))
        after = (first_grads[0],)

        filled, norm_sums = (), []
        for b in range(2):
            grad, pair = input_grad_call(
                b, *pieces[b], stream[b], grad_middle[b], w_vecs, filled, after
            )
            filled = (grad,)
            norm_sums.append(pair)
            after = (pair,)
        input_grad = filled[0]

        two = []
        for b in range(2):
            part = add(parts[b][1], over_core(parts[b][0]), (first[0],) if b == 0 else (first_grads[0],))
            both = add(part, over_chip(part))
            two += [both, over_core(both), middle[b]]
        message, grads = call(
            message_kernel,
            (shape((16, features), f32), shape((r, 4 * width + 2 * hidden), f32)),
            (),
            (*first_grads, *bulk_grads, *norm_sums, *sums, *offsets, *head_sums),
            (),
            16,
        )
        block_out, out_sums = call(
            output_kernel,
            (shape((2, rows, features), bf16), shape((8, 128), f32)),
            lengths,
            (*two, w_vecs, *branch_square),
            (message,),
        )
        message = dp_sum(message, n)
        partial = call(partial_kernel, shape((8, 128), f32), (), (message,), (), 8)
        partial = partial + over_core(partial)
        state = (
            *(v.transpose(1, 0, 2) for v in (w_qkv, m_qkv, v_qkv)),
            *(w_proj, m_proj, v_proj),
            *(w_up, m_up, v_up),
            *(v.T for v in (w_down, m_down, v_down)),
            *(w_vecs, m_vecs, v_vecs),
            *(b_heads, m_heads, v_heads),
            *(b_hidden[None], m_hidden[None], v_hidden[None]),
        )
        *updated, grad_norm = adamw_call(partial, over_chip(partial), message, grads, state)
        out_sums = dp_sum(out_sums, n)
        return (
            block_out,
            input_grad,
            grad_norm[0, :1],
            jnp.sqrt(out_sums[:3, 0] / (out_sums[3, 0] * features)),
            *(v.transpose(1, 0, 2) for v in updated[:3]),
            *updated[3:9],
            *(v.T for v in updated[9:12]),
            *updated[12:18],
            *(v.reshape(hidden) for v in updated[18:]),
        )

    return local


def solution(mesh):
    rows = P(None, "dp", None)
    group = P("dp", None, None)
    qkv, proj, up = P("dp", None, "tensor"), P("tensor", "dp"), P("dp", "tensor")
    params = [qkv] * 3 + [proj] * 3 + [up] * 3 + [proj] * 3 + [P()] * 3
    params += [P(None, "tensor")] * 3 + [P("tensor")] * 3
    return jax.shard_map(
        build(mesh.shape["dp"]),
        mesh=mesh,
        in_specs=(rows, group, group, P("dp", None), P("dp", None), rows, *params),
        out_specs=(rows, rows, P(), P(), *params),
        check_vma=False,
    )
```

```python
import functools

import jax
import jax.numpy as jnp
from jax import lax
from jax.experimental import pallas as pl
from jax.experimental.pallas import tpu as pltpu
from jax.sharding import PartitionSpec as P

HD = 64
STEP = 5
TILE = 128
BLOCK = 256
CHUNK = 192
REACH = (64, 128)

norm_eps = 1e-05
clip_limit = 1.0
beta_first = 0.5
beta_second = 0.5
adam_eps = 1e-08
matrix_decay = 0.01
masked_score = -1e30
step_rates = (0.03, 0.2, 0.03, 0.015, 0.3, 0.3, 0.3)
bf16 = jnp.bfloat16
f32 = jnp.float32

KERNEL_FLOPS = 7 * 10**9

NN = ((1,), (0,))
NT = ((1,), (1,))
TN = ((0,), (0,))


def dot(a, b, dims):
    return lax.dot_general(a, b, (dims, ((), ())), preferred_element_type=f32)


def shape(dims, dtype):
    return jax.ShapeDtypeStruct(dims, dtype)


def cost():
    return pl.CostEstimate(flops=KERNEL_FLOPS, bytes_accessed=0, transcendentals=0)


def call(body, outs, words, arrays, after=(), limit=16, scratch=()):
    count = len(after)

    def kernel(*refs):
        body(*refs[: len(words)], *refs[len(words) + count :])

    in_vmem = pl.BlockSpec(memory_space=pltpu.VMEM)
    in_specs = [pl.BlockSpec(memory_space=pltpu.SMEM)] * len(words)
    in_specs += [pl.BlockSpec(memory_space=pl.ANY)] * count + [in_vmem] * len(arrays)
    return pl.pallas_call(
        kernel,
        out_shape=outs,
        in_specs=in_specs,
        out_specs=(in_vmem,) * len(outs) if isinstance(outs, tuple) else in_vmem,
        scratch_shapes=list(scratch),
        compiler_params=pltpu.CompilerParams(vmem_limit_bytes=limit * 2**20),
        cost_estimate=cost(),
        name=getattr(body, "func", body).__name__,
    )(*words, *after, *arrays)


def core_index():
    return lax.rem(lax.axis_index("tensor"), 2)


def dp_bit(bit):
    return lax.rem(lax.div(lax.axis_index("dp"), bit), 2)


def rows_sum(v):
    return jnp.sum(v, axis=0, keepdims=True)


def whole_sum(v):
    return jnp.sum(rows_sum(v), axis=1, keepdims=True)


def norm_parts(stream):
    center = stream - jnp.mean(stream, axis=-1, keepdims=True)
    spread = jnp.mean(center * center, axis=-1, keepdims=True)
    scale = lax.rsqrt(spread + norm_eps)
    return center * scale, scale


def norm_back(scaled, xhat, scale):
    mean = jnp.mean(scaled, axis=-1, keepdims=True)
    return scale * (scaled - mean - xhat * jnp.mean(scaled * xhat, axis=-1, keepdims=True))


def adamw_step(weight, moment_old, square_old, gradient, step_rate, decay_value, clip_factor):
    correct_one = 1.0 - beta_first**STEP
    correct_two = 1.0 - beta_second**STEP
    clipped = gradient * clip_factor
    moment_new = beta_first * moment_old + (1.0 - beta_first) * clipped
    square_new = beta_second * square_old + (1.0 - beta_second) * clipped * clipped
    divisor = jnp.sqrt(square_new / correct_two) + adam_eps
    weight_new = weight - step_rate * (moment_new / correct_one / divisor + decay_value * weight)
    return (weight_new, moment_new, square_new)


def swap_bit(v, axis, size, bit):
    return lax.ppermute(v, axis, [(i, i ^ bit) for i in range(size)])


def over_core(v):
    return swap_bit(v, "tensor", 4, 1)


def over_chip(v):
    return swap_bit(v, "tensor", 4, 2)


def dp_sum(v, n):
    bit = 1
    while bit < n:
        v = v + swap_bit(v, "dp", n, bit)
        bit *= 2
    return v


def merge_kernel(r, bit, own_ref, other_ref, *out_refs):
    mine = dp_bit(bit)
    for g in range(own_ref.shape[0] // r):
        for ref, side in ((own_ref, mine), (other_ref, 1 - mine)):
            start = pl.multiple_of((2 * g + side) * r, 16)
            column = 0
            for out_ref in out_refs:
                stop = column + out_ref.shape[1]
                out_ref[pl.ds(start, r), :] = ref[g * r : (g + 1) * r, column:stop]
                column = stop


def merged(own, other, r, bit, after=(), widths=None):
    rows, width = own.shape
    widths = widths or (width,)
    if r % 16:
        own, other = (v.reshape(rows // r, r, width) for v in (own, other))
        sides = [jnp.where(dp_bit(bit) == 0, own, other), jnp.where(dp_bit(bit) == 0, other, own)]
        both = jnp.stack(sides, axis=1).reshape(2 * rows, width)
        return tuple(jnp.split(both, [sum(widths[:i]) for i in range(1, len(widths))], axis=1))
    outs = tuple(shape((2 * rows, w), bf16) for w in widths)
    return call(functools.partial(merge_kernel, r, bit), outs, (), (own, other), after, 8)


def split_kernel(r, bit, keep_ref, moved_ref, away_ref, own_ref):
    mine = dp_bit(bit)
    for g in range(away_ref.shape[0] // r):
        for out_ref, side in ((away_ref, 1 - mine), (own_ref, mine)):
            here = pl.ds(pl.multiple_of((2 * g + side) * r, 16), r)
            total = keep_ref[here, :].astype(f32) + moved_ref[here, :].astype(f32)
            out_ref[g * r : (g + 1) * r, :] = total.astype(out_ref.dtype)


def split(keep, moved, r, bit, after=()):
    half, width = keep.shape[0] // 2, keep.shape[1]
    if r % 16:
        total = (keep.astype(f32) + moved.astype(f32)).reshape(half // r, 2, r, width)
        pieces = [lax.dynamic_index_in_dim(total, i, 1, False) for i in (1 - dp_bit(bit), dp_bit(bit))]
        away, own = (v.reshape(half, width) for v in pieces)
        return away.astype(bf16), own
    outs = (shape((half, width), bf16), shape((half, width), f32))
    return call(functools.partial(split_kernel, r, bit), outs, (), (keep, moved), after, 8)


def add_kernel(keep_ref, moved_ref, out_ref):
    out_ref[...] = (keep_ref[...].astype(f32) + moved_ref[...].astype(f32)).astype(bf16)


def add(keep, moved, after=()):
    return call(add_kernel, shape(keep.shape, bf16), (), (keep, moved), after, 8)


def pack_kernel(qkv_ref, proj_ref, qk_ref, vp_ref):
    qk_ref[...] = jnp.concatenate([qkv_ref[0], qkv_ref[1]], axis=1).astype(bf16)
    vp_ref[...] = jnp.concatenate([qkv_ref[2], proj_ref[...].T], axis=1).astype(bf16)


def pair_kernel(left_ref, right_ref, out_ref):
    width = left_ref.shape[1]
    out_ref[:, :width] = left_ref[...]
    out_ref[:, width:] = right_ref[...]


def upstream_kernel(lengths_one, lengths_two, cot_ref, *out_refs):
    rows = cot_ref.shape[1]
    for b, (lengths_ref, out_ref) in enumerate(zip((lengths_one, lengths_two), out_refs)):
        valid = lax.broadcasted_iota(jnp.int32, (rows, 1), 0) < valid_count(lengths_ref)
        out_ref[...] = jnp.where(valid, cot_ref[b].astype(f32), 0.0).astype(bf16)


def cast_kernel(*refs):
    half = len(refs) // 2
    for source, out in zip(refs[:half], refs[half:]):
        out[...] = source[...].astype(bf16)


def segment_grid(lengths_ref, dims, axis, first=0):
    places = first + lax.broadcasted_iota(jnp.int32, dims, axis)
    ids = jnp.zeros(dims, jnp.int32)
    bound = jnp.int32(0)
    for k in range(lengths_ref.shape[1]):
        bound = bound + lengths_ref[0, k]
        ids = ids + (places >= bound).astype(jnp.int32)
    return ids


def same_segment(lengths_ref, start, low, high):
    queries = segment_grid(lengths_ref, (TILE, 1), 0, start)
    return queries == segment_grid(lengths_ref, (1, high - low), 1, low)


def valid_count(lengths_ref):
    total = jnp.int32(0)
    for k in range(lengths_ref.shape[1]):
        total = total + lengths_ref[0, k]
    return total


def first_norm_kernel(lengths_one, lengths_two, inputs_ref, times_one, times_two, vecs_ref, *refs):
    rows = inputs_ref.shape[1]
    for b, (lengths_ref, times_ref) in enumerate(((lengths_one, times_one), (lengths_two, times_two))):
        stream_ref, normed_ref = refs[2 * b : 2 * b + 2]
        depth = times_ref.shape[0]
        ids = segment_grid(lengths_ref, (rows, 1), 0)
        for start in range(0, rows, BLOCK):
            here = slice(start, start + BLOCK)
            lanes = lax.broadcasted_iota(jnp.int32, (BLOCK, depth), 1)
            pick = (ids[here] == lanes).astype(f32).astype(bf16)
            stream = inputs_ref[b, here, :].astype(f32) + dot(pick, times_ref[...], NN)
            stream_ref[here, :] = stream
            xhat, _ = norm_parts(stream)
            normed_ref[here, :] = (xhat * vecs_ref[0:1, :] + vecs_ref[1:2, :]).astype(bf16)


def windows(rows, reach):
    size = min(rows, TILE + 2 * reach)
    out = []
    for start in range(0, rows, TILE):
        low = max(0, start - reach)
        high = min(rows, start + TILE + reach)
        if (high - low) % 128:
            low = min(low, rows - size)
            high = low + size
        out.append((start, low, high))
    return out


def split_heads(low, rows, q_s, k_s, v_s):
    heads = q_s.shape[0]
    width = heads * HD
    for h in range(heads):
        cut = h * HD
        q_s[h, rows, :] = low[:, cut : cut + HD] * jnp.array(HD**-0.5, bf16)
        k_s[h, rows, :] = low[:, width + cut : width + cut + HD]
        v_s[h, rows, :] = low[:, 2 * width + cut : 2 * width + cut + HD]


def forward_kernel(reach, carried, lengths_ref, normed_ref, qk_ref, wv_ref, bias_ref, *refs):
    att_ref, qkv_ref, lse_ref, *pair_refs, q_s, k_s, v_s = refs[carried:]
    rows, width = att_ref.shape
    heads = range(width // HD)
    for start in range(0, rows, BLOCK):
        piece = slice(start, start + BLOCK)
        normed = normed_ref[piece, :]
        pair = dot(normed, qk_ref[...], NN)
        values = dot(normed, wv_ref[...], NN)
        low = (jnp.concatenate([pair, values], axis=1) + bias_ref[...]).astype(bf16)
        qkv_ref[piece, :] = low
        split_heads(low, piece, q_s, k_s, v_s)
    lanes = lax.broadcasted_iota(jnp.int32, (TILE, 128), 1)
    for start, low, high in windows(rows, reach):
        tile = slice(start, start + TILE)
        allowed = same_segment(lengths_ref, start, low, high)
        scores = [dot(q_s[h, tile, :], k_s[h, low:high, :], NT) for h in heads]
        scores = [jnp.where(allowed, s, masked_score) for s in scores]
        peaks = [jnp.max(s, axis=-1, keepdims=True) for s in scores]
        exponents = [jnp.exp(s - p) for s, p in zip(scores, peaks)]
        totals = [jnp.sum(e, axis=-1, keepdims=True) for e in exponents]
        probs = [(e * (1.0 / t)).astype(bf16) for e, t in zip(exponents, totals)]
        outs = [dot(p, v_s[h, low:high, :], NN).astype(bf16) for h, p in enumerate(probs)]
        att_ref[tile, :] = jnp.concatenate(outs, axis=1)
        logs = jnp.zeros((TILE, 128), f32)
        for h in heads:
            logs = jnp.where(lanes == h, peaks[h] + jnp.log(totals[h]), logs)
        lse_ref[tile, :] = logs
    for ref, pair_ref in zip(refs[:carried], pair_refs):
        pair_ref[...] = jnp.concatenate([att_ref[...], ref[...]], axis=1)


def hidden_kernel(lengths_ref, *refs):
    first_refs, att_refs = refs[:2], refs[-11:-9]
    stream_ref, vecs_ref, up_ref, bias_ref = refs[-9:-5]
    middle_ref, normed_ref, active_ref, slope_ref, square_ref = refs[-5:]
    rows, features = stream_ref.shape
    width = first_refs[0].shape[1] // 4
    step = att_refs[0].shape[1] // 2
    total = valid_count(lengths_ref)
    squares = jnp.zeros((1, features), f32)
    for start in range(0, rows, BLOCK):
        here = slice(start, start + BLOCK)
        valid = start + lax.broadcasted_iota(jnp.int32, (BLOCK, 1), 0) < total
        own, over, near, across = (
            dot(a[here, k * step : k * step + width], p[:, (2 * k + 1) * width : (2 * k + 2) * width], NT)
            for a, p in zip(att_refs, first_refs)
            for k in range(2)
        )
        branch = ((own + near) + (over + across)) + vecs_ref[4:5, :]
        kept = jnp.where(valid, branch, 0.0)
        squares = squares + rows_sum(kept * kept)
        middle = stream_ref[here, :] + branch
        middle_ref[here, :] = middle
        xhat, _ = norm_parts(middle)
        normed = (xhat * vecs_ref[2:3, :] + vecs_ref[3:4, :]).astype(bf16)
        normed_ref[here, :] = normed
        hidden = dot(normed, up_ref[...], NN) + bias_ref[...]
        cdf = 0.5 + 0.5 * lax.erf(hidden * 0.5**0.5)
        pdf = jnp.exp(-0.5 * hidden * hidden) * 0.3989422804014327
        active_ref[here, :] = (hidden * cdf).astype(bf16)
        slope_ref[here, :] = cdf + hidden * pdf
    square_ref[...] = squares


def hidden_back_kernel(upstream_ref, slope_ref, up_ref, down_ref, grad_ref, away_ref, keep_ref, offset_ref):
    rows = upstream_ref.shape[0]
    half = rows // 2
    first = (1 - core_index()) * half

    def rows_step(t, offsets):
        here = pl.ds(pl.multiple_of(lax.rem(first + t * CHUNK, rows), CHUNK), CHUNK)
        grad = dot(upstream_ref[here, :], down_ref[...], NN) * slope_ref[here, :]
        low = grad.astype(bf16)
        grad_ref[here, :] = low
        part = dot(low, up_ref[...], NT)

        @pl.when(t * CHUNK < half)
        def _():
            away_ref[pl.ds(pl.multiple_of(t * CHUNK, CHUNK), CHUNK), :] = part.astype(bf16)

        @pl.when(t * CHUNK >= half)
        def _():
            keep_ref[pl.ds(pl.multiple_of(t * CHUNK - half, CHUNK), CHUNK), :] = part

        return offsets + rows_sum(grad)

    offset_ref[...] = lax.fori_loop(0, rows // CHUNK, rows_step, jnp.zeros(offset_ref.shape, f32))


def down_kernel(active_ref, down_ref, away_ref, keep_ref):
    half = active_ref.shape[0] // 2
    core = core_index()
    for out_ref, base in ((away_ref, (1 - core) * half), (keep_ref, core * half)):
        here = pl.ds(pl.multiple_of(base, half), half)
        out_ref[...] = dot(active_ref[here, :], down_ref[...], NT).astype(out_ref.dtype)


def products_kernel(pairs, *refs):
    out_ref = refs[-1]
    for m in range(0, out_ref.shape[0], BLOCK):
        cut = slice(m, m + BLOCK)
        column = 0
        for p in range(pairs):
            left_one, left_two, right_one, right_two = refs[4 * p : 4 * p + 4]
            rows = left_one.shape[0]
            part = dot(left_one[:, cut], right_one[:rows, :], TN) + dot(left_two[:, cut], right_two[:rows, :], TN)
            out_ref[cut, column : column + part.shape[1]] = part.astype(out_ref.dtype)
            column += part.shape[1]


def parted_kernel(r, *refs):
    away_ref, keep_ref, full_s = refs[-3:]
    products_kernel(len(refs) // 4, *refs[:-3], full_s)
    inner = dp_bit(1)
    for o in range(away_ref.shape[0] // r):
        for out_ref, side in ((away_ref, 1 - inner), (keep_ref, inner)):
            start = pl.multiple_of((o * 2 + side) * r, 8)
            out_ref[o * r : (o + 1) * r, :] = full_s[pl.ds(start, r), :].astype(bf16)


def parted(arrays, n, after):
    rows, width = arrays[0].shape[1], sum(v.shape[1] for v in arrays[2::4])
    r = rows // n
    if r % 16:
        kernel = functools.partial(products_kernel, len(arrays) // 4)
        full = call(kernel, shape((rows, width), bf16), (), arrays, after)
        view = full.reshape(n // 2, 2, r, width)
        inner = dp_bit(1)
        pieces = [lax.dynamic_index_in_dim(view, i, 1, False) for i in (1 - inner, inner)]
        return [v.reshape(rows // 2, width) for v in pieces]
    outs = (shape((rows // 2, width), bf16),) * 2
    scratch = [pltpu.VMEM((rows, width), f32)]
    return call(functools.partial(parted_kernel, r), outs, (), arrays, after, 24, scratch)


def backward_kernel(
    reach,
    lengths_ref,
    both_ref,
    other_ref,
    middle_ref,
    upstream_ref,
    vecs_ref,
    qk_ref,
    wv_ref,
    proj_ref,
    qkv_ref,
    lse_ref,
    grad_middle_ref,
    low_ref,
    mixed_ref,
    away_ref,
    keep_ref,
    sums_ref,
    heads_ref,
    q_s,
    k_s,
    v_s,
    g_s,
    dk_s,
    dv_s,
):
    rows, features = middle_ref.shape
    half = rows // 2
    width = qkv_ref.shape[1] // 3
    heads = range(width // HD)
    core = core_index()
    gain = vecs_ref[2:3, :]
    sums = []
    for piece_ref, base in ((both_ref, core * half), (other_ref, (1 - core) * half)):

        def rows_step(t, acc, piece_ref=piece_ref, base=base):
            off = pl.multiple_of(base + t * TILE, TILE)
            here = pl.ds(off, TILE)
            gnt = piece_ref[pl.ds(pl.multiple_of(t * TILE, TILE), TILE), :].astype(f32)
            xhat, scale = norm_parts(middle_ref[here, :])
            upstream = upstream_ref[here, :].astype(f32)
            grad_middle = upstream + norm_back(gnt * gain, xhat, scale)
            grad_middle_ref[here, :] = grad_middle
            low_ref[here, :] = grad_middle.astype(bf16)
            terms = (gnt * xhat, gnt, grad_middle, upstream)
            return tuple(a + rows_sum(v) for a, v in zip(acc, terms))

        start = (jnp.zeros((1, features), f32),) * 4
        sums.append(lax.fori_loop(0, half // TILE, rows_step, start))
    sums_ref[...] = jnp.concatenate([a + b for a, b in zip(*sums)], axis=0)
    for start in range(0, rows, BLOCK):
        piece = slice(start, start + BLOCK)
        split_heads(qkv_ref[piece, :], piece, q_s, k_s, v_s)
        grad_att = dot(low_ref[piece, :], proj_ref[...], NN).astype(bf16)
        for h in heads:
            g_s[h, piece, :] = grad_att[:, h * HD : (h + 1) * HD]
    dk_s[...] = jnp.zeros_like(dk_s)
    dv_s[...] = jnp.zeros_like(dv_s)
    for start, low, high in windows(rows, reach):
        tile = slice(start, start + TILE)
        keys = slice(low, high)
        allowed = same_segment(lengths_ref, start, low, high)
        scores = [dot(q_s[h, tile, :], k_s[h, keys, :], NT) for h in heads]
        grad_probs = [dot(g_s[h, tile, :], v_s[h, keys, :], NT) for h in heads]
        probs = [jnp.exp(jnp.where(allowed, s, masked_score) - lse_ref[tile, h : h + 1]) for h, s in enumerate(scores)]
        inner = [jnp.sum(p * g, axis=-1, keepdims=True) for p, g in zip(probs, grad_probs)]
        grads = [(p * (g - i)).astype(bf16) for p, g, i in zip(probs, grad_probs, inner)]
        lows = [p.astype(bf16) for p in probs]
        dqs = [(dot(g, k_s[h, keys, :], NN) * HD**-0.5).astype(bf16) for h, g in enumerate(grads)]
        mixed_ref[tile, :width] = jnp.concatenate(dqs, axis=1)
        dks = [dot(g, q_s[h, tile, :], TN) for h, g in enumerate(grads)]
        dvs = [dot(p, g_s[h, tile, :], TN) for h, p in enumerate(lows)]
        for h in heads:
            dk_s[h, keys, :] += dks[h]
            dv_s[h, keys, :] += dvs[h]
    for start in range(0, rows, BLOCK):
        piece = slice(start, start + BLOCK)
        both = [ref[h, piece, :].astype(bf16) for ref in (dk_s, dv_s) for h in heads]
        mixed_ref[piece, width:] = jnp.concatenate(both, axis=1)
    heads_ref[...] = rows_sum(mixed_ref[...].astype(f32))
    for out_ref, base in ((away_ref, (1 - core) * half), (keep_ref, core * half)):
        here = pl.ds(pl.multiple_of(base, half), half)
        part = dot(mixed_ref[here, : 2 * width], qk_ref[...], NT)
        part = part + dot(mixed_ref[here, 2 * width :], wv_ref[...], NT)
        out_ref[...] = part.astype(out_ref.dtype)


def input_grad_kernel(both_ref, other_ref, stream_ref, middle_ref, vecs_ref, *refs):
    out_ref, sums_ref = refs[-2:]
    rows, features = stream_ref.shape
    half = rows // 2
    core = core_index()
    gain = vecs_ref[0:1, :]
    sums = []
    for piece_ref, base in ((both_ref, core * half), (other_ref, (1 - core) * half)):

        def rows_step(t, acc, piece_ref=piece_ref, base=base):
            here = pl.ds(pl.multiple_of(base + t * TILE, TILE), TILE)
            grad = piece_ref[pl.ds(pl.multiple_of(t * TILE, TILE), TILE), :].astype(f32)
            xhat, scale = norm_parts(stream_ref[here, :])
            out_ref[0, here, :] = middle_ref[here, :] + norm_back(grad * gain, xhat, scale)
            return (acc[0] + rows_sum(grad * xhat), acc[1] + rows_sum(grad))

        start = (jnp.zeros((1, features), f32),) * 2
        sums.append(lax.fori_loop(0, half // TILE, rows_step, start))
    sums_ref[...] = jnp.concatenate([a + b for a, b in zip(*sums)], axis=0)


def input_grad_call(which, both, other, stream, middle, vecs, filled, after):
    rows, features = stream.shape
    count = len(after)

    def kernel(*refs):
        input_grad_kernel(*refs[count:])

    whole = pl.BlockSpec(memory_space=pltpu.VMEM)
    anywhere = pl.BlockSpec(memory_space=pl.ANY)
    return pl.pallas_call(
        kernel,
        grid=(1,),
        out_shape=(shape((2, rows, features), f32), shape((2, features), f32)),
        in_specs=[anywhere] * count + [whole] * 5 + [anywhere] * len(filled),
        out_specs=(pl.BlockSpec((1, rows, features), lambda i: (which, 0, 0)), whole),
        input_output_aliases={count + 5: 0} if filled else {},
        compiler_params=pltpu.CompilerParams(vmem_limit_bytes=24 * 2**20),
        cost_estimate=cost(),
    )(*after, both, other, stream, middle, vecs, *filled)


def output_kernel(lengths_one, lengths_two, *refs):
    vecs_ref, branch_one, branch_two, out_ref, sums_ref = refs[6:]
    features = out_ref.shape[2]
    half = out_ref.shape[1] // 2
    core = core_index()
    sums = []
    count = jnp.int32(0)
    for b, lengths_ref in enumerate((lengths_one, lengths_two)):
        total = valid_count(lengths_ref)
        count = count + total
        both_ref, other_ref, middle_ref = refs[3 * b : 3 * b + 3]
        for piece_ref, base in ((both_ref, core * half), (other_ref, (1 - core) * half)):

            def rows_step(t, acc, piece_ref=piece_ref, base=base, middle_ref=middle_ref, total=total, b=b):
                off = pl.multiple_of(base + t * TILE, TILE)
                here = pl.ds(off, TILE)
                two = piece_ref[pl.ds(pl.multiple_of(t * TILE, TILE), TILE), :].astype(f32) + vecs_ref[5:6, :]
                whole = middle_ref[here, :] + two
                out_ref[b, here, :] = whole.astype(bf16)
                valid = off + lax.broadcasted_iota(jnp.int32, (TILE, 1), 0) < total
                terms = [jnp.where(valid, v, 0.0) for v in (whole, two)]
                return tuple(a + rows_sum(v * v) for a, v in zip(acc, terms))

            start = (jnp.zeros((1, features), f32),) * 2
            sums.append(lax.fori_loop(0, half // TILE, rows_step, start))
    whole, two = ((a + b) + (c + d) for a, b, c, d in zip(*sums))
    lines = [jnp.sum(v, axis=1, keepdims=True) for v in (whole, branch_one[...] + branch_two[...], two)]
    lines.append(jnp.full((1, 1), count.astype(f32), f32))
    for i in range(8):
        sums_ref[i : i + 1, :] = jnp.broadcast_to(lines[min(i, 3)], (1, 128))


def message_kernel(*refs):
    out_ref, grads_ref = refs[-2:]
    norm_one, norm_two, sums_one, sums_two, off_one, off_two, heads_one, heads_two = refs[-10:-2]
    pairs = refs[:-10]
    width = heads_one.shape[1] // 3
    column = 0
    squares = jnp.zeros((1, 1), f32)
    for keep_ref, moved_ref in zip(pairs[::2], pairs[1::2]):
        grad = keep_ref[...].astype(f32) + moved_ref[...].astype(f32)
        stop = column + grad.shape[1]
        grads_ref[:, column:stop] = grad
        squares = squares + whole_sum(grad * grad)
        column = stop
    out_ref[...] = jnp.zeros_like(out_ref)
    out_ref[0:2, :] = norm_one[...] + norm_two[...]
    out_ref[2:6, :] = sums_one[...] + sums_two[...]
    out_ref[6:7, :] = off_one[...] + off_two[...]
    heads = heads_one[...] + heads_two[...]
    out_ref[8:9, :width] = heads[:, :width]
    out_ref[9:10, :width] = heads[:, 2 * width :]
    out_ref[10:11, :] = jnp.broadcast_to(squares, (1, out_ref.shape[1]))


def partial_kernel(message_ref, out_ref):
    squares = whole_sum(message_ref[8:10, :] * message_ref[8:10, :])
    squares = squares + whole_sum(message_ref[6:7, :] * message_ref[6:7, :])
    out_ref[...] = jnp.broadcast_to(squares + message_ref[10:11, 0:1], out_ref.shape)


def adamw_kernel(partial_ref, moved_ref, message_ref, grads_ref, *refs):
    count = 21
    sources, targets, norm_ref = refs[:count], refs[count : 2 * count], refs[2 * count]
    inputs, outputs = refs[2 * count + 1 : 3 * count + 1], refs[3 * count + 1 : 4 * count + 1]
    read_sems, write_sems = refs[4 * count + 1 :]
    reads = [pltpu.make_async_copy(sources[i], inputs[i], read_sems.at[i]) for i in range(count)]
    writes = [pltpu.make_async_copy(outputs[i], targets[i], write_sems.at[i]) for i in range(count)]
    for copy in reads:
        copy.start()
    width = inputs[0].shape[2]
    hidden = inputs[6].shape[1]
    vecs = message_ref[0:6, :]
    norm = jnp.sqrt(partial_ref[0:1, 0:1] + moved_ref[0:1, 0:1] + whole_sum(vecs * vecs))
    norm_ref[...] = jnp.broadcast_to(norm, norm_ref.shape)
    clip = jnp.minimum(1.0, clip_limit / (norm + 1e-06))

    def step(p, gradient, at=Ellipsis):
        weight, moment, square = (ref[at] for ref in inputs[3 * p : 3 * p + 3])
        decay = matrix_decay if p < 4 else 0.0
        values = adamw_step(weight, moment, square, gradient, step_rates[p], decay, clip)
        for ref, value in zip(outputs[3 * p : 3 * p + 3], values):
            ref[at] = value

    start = 4 * width
    parts = (
        tuple((grads_ref[:, j * width : (j + 1) * width], j) for j in range(3)),
        ((grads_ref[:, 3 * width : start].T,),),
        ((grads_ref[:, start : start + hidden],),),
        ((grads_ref[:, start + hidden :],),),
        ((vecs,),),
        ((message_ref[8:10, : inputs[15].shape[1]],),),
        ((message_ref[6:7, :],),),
    )
    for p, steps in enumerate(parts):
        for copy in reads[3 * p : 3 * p + 3]:
            copy.wait()
        for arguments in steps:
            step(p, *arguments)
        for copy in writes[3 * p : 3 * p + 3]:
            copy.start()
    for copy in writes:
        copy.wait()


def adamw_call(partial, moved, message, grads, state):
    in_vmem = pl.BlockSpec(memory_space=pltpu.VMEM)
    anywhere = pl.BlockSpec(memory_space=pltpu.MemorySpace.HBM)
    count = len(state)
    return pl.pallas_call(
        adamw_kernel,
        out_shape=tuple(shape(v.shape, f32) for v in state) + (shape((1, 128), f32),),
        in_specs=[in_vmem] * 4 + [anywhere] * count,
        out_specs=(anywhere,) * count + (in_vmem,),
        scratch_shapes=[pltpu.VMEM(v.shape, f32) for v in state] * 2 + [pltpu.SemaphoreType.DMA((count,))] * 2,
        compiler_params=pltpu.CompilerParams(vmem_limit_bytes=24 * 2**20),
        cost_estimate=cost(),
    )(partial, moved, message, grads, *state)


def build(n):
    top = n // 2

    def local(
        inputs,
        time_first,
        time_second,
        lengths_first,
        lengths_second,
        cotangent,
        w_qkv,
        m_qkv,
        v_qkv,
        w_proj,
        m_proj,
        v_proj,
        w_up,
        m_up,
        v_up,
        w_down,
        m_down,
        v_down,
        w_vecs,
        m_vecs,
        v_vecs,
        b_heads,
        m_heads,
        v_heads,
        b_hidden,
        m_hidden,
        v_hidden,
    ):
        rows, features = inputs.shape[1], inputs.shape[2]
        r, _, width = w_qkv.shape
        hidden = w_up.shape[1]
        heads = width // HD
        half = rows // 2
        lengths = (lengths_first, lengths_second)
        whole_f = shape((rows, features), f32)
        whole_b = shape((rows, features), bf16)
        hidden_b = shape((rows, hidden), bf16)
        half_b = shape((half, features), bf16)
        half_f = shape((half, features), f32)
        line = shape((1, features), f32)

        def swap(v, bit):
            return swap_bit(v, "dp", n, bit)

        def gathered(shard, bit, stop, after=()):
            while bit > stop:
                (shard,) = merged(shard, swap(shard, bit), r, bit, after)
                after = ()
                bit //= 2
            return shard

        qk, vp = call(
            pack_kernel, (shape((r, 2 * width), bf16),) * 2, (), (w_qkv.transpose(1, 0, 2), w_proj), (), 8
        )
        times = [jnp.pad(t[0], ((0, 16 - t.shape[1]), (0, 0))) for t in (time_first, time_second)]
        stream_one, normed_one, stream_two, normed_two = call(
            first_norm_kernel, (whole_f, whole_b) * 2, lengths, (inputs, *times, w_vecs), (qk,), 24
        )
        stream, normed = (stream_one, stream_two), (normed_one, normed_two)
        qk = gathered(qk, top, top // 2, (normed_two,))
        vp = gathered(vp, top, top // 2, (qk,))
        upstream = call(upstream_kernel, (whole_b,) * 2, lengths, (cotangent,), (vp,))
        qk = gathered(qk, top // 2, 1, (upstream[1],))
        (up,) = call(cast_kernel, (shape((r, hidden), bf16),), (), (w_up,), (qk,), 8)
        vp = gathered(vp, top // 2, 1, (up,))
        (qk,) = merged(qk, swap(qk, 1), r, 1, (vp,))
        (down,) = call(cast_kernel, (shape((r, hidden), bf16),), (), (w_down.T,), (qk,), 8)
        up = gathered(up, top, top // 2, (down,))
        wv, proj = merged(vp, swap(vp, 1), r, 1, (up,), (width, width))

        def spread(v, after=()):
            moved = over_chip(v)
            pair = call(pair_kernel, shape((rows, 2 * v.shape[1]), bf16), (), (v, moved), after, 8)
            return [pair, over_core(pair)]

        bias = jnp.concatenate([b_heads[0], jnp.zeros_like(b_heads[0]), b_heads[1]])[None]
        head_low = pltpu.VMEM((heads, rows, HD), bf16)
        head_full = pltpu.VMEM((heads, rows, HD), f32)
        after = (wv,)
        att, sent, qkv, lse = [], [], [], []
        for b in range(2):
            carried = (proj,) if b == 0 else ()
            a, q, l, *pair = call(
                functools.partial(forward_kernel, REACH[b], len(carried)),
                (
                    shape((rows, width), bf16),
                    shape((rows, 3 * width), bf16),
                    shape((rows, 128), f32),
                    *(shape((rows, 2 * width), bf16) for _ in carried),
                ),
                (lengths[b],),
                (normed[b], qk, wv, bias, *carried),
                after,
                12,
                [head_low] * 3,
            )
            att.append(a)
            sent.append(pair[0] if pair else a)
            qkv.append(q)
            lse.append(l)
            after = (l,)
            if b == 0:
                down = gathered(down, top, top // 2, after)
                up = gathered(up, top // 2, 1, (down,))
                after = (up,)
        down = gathered(down, top // 2, 1, after)
        (up,) = merged(up, swap(up, 1), r, 1, (down,))
        att_all = [spread(sent[0], (up,))]
        att_all.append(spread(sent[1]))
        after = (att_all[0][0],)

        names = [[] for _ in range(9)]
        for b in range(2):
            outs = call(
                hidden_kernel,
                (whole_f, whole_b, hidden_b, shape((rows, hidden), f32), line),
                (lengths[b],),
                (*att_all[0], *(att_all[1] if b else ()), stream[b], w_vecs, up, b_hidden[None]),
                after,
            )
            for kept, v in zip(names, outs):
                kept.append(v)
            after = (outs[-1],)
        (down,) = merged(down, swap(down, 1), r, 1, after)
        low = []
        after = (down,)
        for b in range(2):
            outs = call(
                hidden_back_kernel,
                (hidden_b, half_b, half_f, shape((1, hidden), f32)),
                (),
                (upstream[b], names[3][b], up, down),
                after,
            )
            for kept, v in zip(names[5:], outs):
                kept.append(v)
            after = (outs[-1],)
        middle, normed_mid, active, slope, branch_square, grad_hidden, away, keep, offsets = names
        low.append(add(keep[0], over_core(away[0]), after))
        after = (low[0],)

        bulk = parted((*normed_mid, *grad_hidden, *upstream, *active), n, after)
        bulk_moved = swap(bulk[0], 1)
        low.append(add(keep[1], over_core(away[1]), (bulk[0],)))
        both = add(low[0], over_chip(low[0]), (low[1],))
        gnt = [(both, over_core(both))]
        parts = [call(down_kernel, (half_b, half_f), (), (active[0], down), (both,))]
        after = (parts[0][0],)

        grad_middle, middle_low, grad_mixed, sums, head_sums, back_low = [], [], [], [], [], []
        for b in range(2):
            outs = call(
                functools.partial(backward_kernel, REACH[b]),
                (
                    whole_f,
                    whole_b,
                    shape((rows, 3 * width), bf16),
                    half_b,
                    half_f,
                    shape((4, features), f32),
                    shape((1, 3 * width), f32),
                ),
                (lengths[b],),
                (*gnt[b], middle[b], upstream[b], w_vecs, qk, wv, proj, qkv[b], lse[b]),
                after,
                24,
                [head_low] * 4 + [head_full] * 2,
            )
            grad_middle.append(outs[0])
            middle_low.append(outs[1])
            grad_mixed.append(outs[2])
            sums.append(outs[5])
            head_sums.append(outs[6])
            after = (outs[6],)
            if b == 0:
                both = add(low[1], over_chip(low[1]), after)
                gnt.append((both, over_core(both)))
                bulk = split(bulk[1], bulk_moved, r, 2, (both,))
                bulk_moved = swap(bulk[0], 2)
                after = (bulk[0],)
            else:
                parts.append(call(down_kernel, (half_b, half_f), (), (active[1], down), after))
                after = (parts[1][0],)
            back_low.append(add(outs[4], over_core(outs[3]), after))
            after = (back_low[b],)

        first = parted((*normed, *grad_mixed, *middle_low, *att), n, after)
        first_moved = swap(first[0], 1)
        both = add(back_low[0], over_chip(back_low[0]), (first[0],))
        piece = (both, over_core(both))
        after = (both,)
        bit = 4
        while bit < n:
            bulk = split(bulk[1], bulk_moved, r, bit, after)
            bulk_moved = swap(bulk[0], bit)
            after = (bulk[0],)
            bit *= 2
        input_grad, pair = input_grad_call(0, *piece, stream[0], grad_middle[0], w_vecs, (), after)
        norm_sums = [pair]
        first = split(first[1], first_moved, r, 2, (pair,))
        first_moved = swap(first[0], 2)
        part = [add(parts[0][1], over_core(parts[0][0]), (first[0],))]
        both = add(back_low[1], over_chip(back_low[1]), (part[0],))
        piece = (both, over_core(both))
        after = (both,)
        bit = 4
        while bit < n:
            first = split(first[1], first_moved, r, bit, after)
            first_moved = swap(first[0], bit)
            after = (first[0],)
            bit *= 2
        part.append(add(parts[1][1], over_core(parts[1][0]), after))
        input_grad, pair = input_grad_call(
            1, *piece, stream[1], grad_middle[1], w_vecs, (input_grad,), (part[1],)
        )
        norm_sums.append(pair)

        message, grads = call(
            message_kernel,
            (shape((16, features), f32), shape((r, 4 * width + 2 * hidden), f32)),
            (),
            (first[1], first_moved, bulk[1], bulk_moved, *norm_sums, *sums, *offsets, *head_sums),
            (pair,),
            16,
        )
        two = []
        for b in range(2):
            both = add(part[b], over_chip(part[b]), (message,))
            two += [both, over_core(both), middle[b]]
        block_out, out_sums = call(
            output_kernel,
            (shape((2, rows, features), bf16), shape((8, 128), f32)),
            lengths,
            (*two, w_vecs, *branch_square),
            (message,),
        )
        message = dp_sum(message, n)
        partial = call(partial_kernel, shape((8, 128), f32), (), (message,), (), 8)
        partial = partial + over_core(partial)
        state = (
            *(v.transpose(1, 0, 2) for v in (w_qkv, m_qkv, v_qkv)),
            *(w_proj, m_proj, v_proj),
            *(w_up, m_up, v_up),
            *(v.T for v in (w_down, m_down, v_down)),
            *(w_vecs, m_vecs, v_vecs),
            *(b_heads, m_heads, v_heads),
            *(b_hidden[None], m_hidden[None], v_hidden[None]),
        )
        *updated, grad_norm = adamw_call(partial, over_chip(partial), message, grads, state)
        out_sums = dp_sum(out_sums, n)
        return (
            block_out,
            input_grad,
            grad_norm[0, :1],
            jnp.sqrt(out_sums[:3, 0] / (out_sums[3, 0] * features)),
            *(v.transpose(1, 0, 2) for v in updated[:3]),
            *updated[3:9],
            *(v.T for v in updated[9:12]),
            *updated[12:18],
            *(v.reshape(hidden) for v in updated[18:]),
        )

    return local


def solution(mesh):
    rows = P(None, "dp", None)
    group = P("dp", None, None)
    qkv, proj, up = P("dp", None, "tensor"), P("tensor", "dp"), P("dp", "tensor")
    params = [qkv] * 3 + [proj] * 3 + [up] * 3 + [proj] * 3 + [P()] * 3
    params += [P(None, "tensor")] * 3 + [P("tensor")] * 3
    return jax.shard_map(
        build(mesh.shape["dp"]),
        mesh=mesh,
        in_specs=(rows, group, group, P("dp", None), P("dp", None), rows, *params),
        out_specs=(rows, rows, P(), P(), *params),
        check_vma=False,
    )
```

```python
import functools

import jax
import jax.numpy as jnp
from jax import lax
from jax.experimental import pallas as pl
from jax.experimental.pallas import tpu as pltpu
from jax.sharding import PartitionSpec as P

HD = 64
STEP = 5
TILE = 128
BLOCK = 256
CHUNK = 192
REACH = (64, 128)

norm_eps = 1e-05
clip_limit = 1.0
beta_first = 0.5
beta_second = 0.5
adam_eps = 1e-08
matrix_decay = 0.01
masked_score = -1e30
step_rates = (0.03, 0.2, 0.03, 0.015, 0.3, 0.3, 0.3)
bf16 = jnp.bfloat16
f32 = jnp.float32

KERNEL_FLOPS = 7 * 10**9

NN = ((1,), (0,))
NT = ((1,), (1,))
TN = ((0,), (0,))


def dot(a, b, dims):
    return lax.dot_general(a, b, (dims, ((), ())), preferred_element_type=f32)


def shape(dims, dtype):
    return jax.ShapeDtypeStruct(dims, dtype)


def cost(weight=1):
    return pl.CostEstimate(flops=weight * KERNEL_FLOPS, bytes_accessed=0, transcendentals=0)


def call(body, outs, words, arrays, after=(), limit=16, scratch=(), weight=1):
    count = len(after)

    def kernel(*refs):
        body(*refs[: len(words)], *refs[len(words) + count :])

    in_vmem = pl.BlockSpec(memory_space=pltpu.VMEM)
    in_specs = [pl.BlockSpec(memory_space=pltpu.SMEM)] * len(words)
    in_specs += [pl.BlockSpec(memory_space=pl.ANY)] * count + [in_vmem] * len(arrays)
    return pl.pallas_call(
        kernel,
        out_shape=outs,
        in_specs=in_specs,
        out_specs=(in_vmem,) * len(outs) if isinstance(outs, tuple) else in_vmem,
        scratch_shapes=list(scratch),
        compiler_params=pltpu.CompilerParams(vmem_limit_bytes=limit * 2**20),
        cost_estimate=cost(weight),
        name=getattr(body, "func", body).__name__,
    )(*words, *after, *arrays)


def core_index():
    return lax.rem(lax.axis_index("tensor"), 2)


def dp_bit(bit):
    return lax.rem(lax.div(lax.axis_index("dp"), bit), 2)


def rows_sum(v):
    return jnp.sum(v, axis=0, keepdims=True)


def whole_sum(v):
    return jnp.sum(rows_sum(v), axis=1, keepdims=True)


def norm_parts(stream):
    center = stream - jnp.mean(stream, axis=-1, keepdims=True)
    spread = jnp.mean(center * center, axis=-1, keepdims=True)
    scale = lax.rsqrt(spread + norm_eps)
    return center * scale, scale


def norm_back(scaled, xhat, scale):
    mean = jnp.mean(scaled, axis=-1, keepdims=True)
    return scale * (scaled - mean - xhat * jnp.mean(scaled * xhat, axis=-1, keepdims=True))


def adamw_step(weight, moment_old, square_old, gradient, step_rate, decay_value, clip_factor):
    correct_one = 1.0 - beta_first**STEP
    correct_two = 1.0 - beta_second**STEP
    clipped = gradient * clip_factor
    moment_new = beta_first * moment_old + (1.0 - beta_first) * clipped
    square_new = beta_second * square_old + (1.0 - beta_second) * clipped * clipped
    divisor = jnp.sqrt(square_new / correct_two) + adam_eps
    weight_new = weight - step_rate * (moment_new / correct_one / divisor + decay_value * weight)
    return (weight_new, moment_new, square_new)


def swap_bit(v, axis, size, bit):
    return lax.ppermute(v, axis, [(i, i ^ bit) for i in range(size)])


def over_core(v):
    return swap_bit(v, "tensor", 4, 1)


def over_chip(v):
    return swap_bit(v, "tensor", 4, 2)


def merge_kernel(r, bit, own_ref, other_ref, *out_refs):
    mine = dp_bit(bit)
    for g in range(own_ref.shape[0] // r):
        for ref, side in ((own_ref, mine), (other_ref, 1 - mine)):
            start = pl.multiple_of((2 * g + side) * r, 16)
            column = 0
            for out_ref in out_refs:
                stop = column + out_ref.shape[1]
                out_ref[pl.ds(start, r), :] = ref[g * r : (g + 1) * r, column:stop]
                column = stop


def merged(own, other, r, bit, after=(), widths=None, weight=1):
    rows, width = own.shape
    widths = widths or (width,)
    if r % 16:
        own, other = (v.reshape(rows // r, r, width) for v in (own, other))
        sides = [jnp.where(dp_bit(bit) == 0, own, other), jnp.where(dp_bit(bit) == 0, other, own)]
        both = jnp.stack(sides, axis=1).reshape(2 * rows, width)
        return tuple(jnp.split(both, [sum(widths[:i]) for i in range(1, len(widths))], axis=1))
    outs = tuple(shape((2 * rows, w), bf16) for w in widths)
    return call(functools.partial(merge_kernel, r, bit), outs, (), (own, other), after, 8, weight=weight)


def split_kernel(r, bit, keep_ref, moved_ref, away_ref, own_ref):
    mine = dp_bit(bit)
    for g in range(away_ref.shape[0] // r):
        for out_ref, side in ((away_ref, 1 - mine), (own_ref, mine)):
            here = pl.ds(pl.multiple_of((2 * g + side) * r, 16), r)
            total = keep_ref[here, :].astype(f32) + moved_ref[here, :].astype(f32)
            out_ref[g * r : (g + 1) * r, :] = total.astype(out_ref.dtype)


def split(keep, moved, r, bit, after=()):
    half, width = keep.shape[0] // 2, keep.shape[1]
    if r % 16:
        total = (keep.astype(f32) + moved.astype(f32)).reshape(half // r, 2, r, width)
        pieces = [lax.dynamic_index_in_dim(total, i, 1, False) for i in (1 - dp_bit(bit), dp_bit(bit))]
        away, own = (v.reshape(half, width) for v in pieces)
        return away.astype(bf16), own
    outs = (shape((half, width), bf16), shape((half, width), f32))
    return call(functools.partial(split_kernel, r, bit), outs, (), (keep, moved), after, 8)


def sum_kernel(own_ref, moved_ref, out_ref):
    out_ref[...] = own_ref[...] + moved_ref[...]


def add_kernel(keep_ref, moved_ref, out_ref):
    out_ref[...] = (keep_ref[...].astype(f32) + moved_ref[...].astype(f32)).astype(bf16)


def add(keep, moved, after=()):
    return call(add_kernel, shape(keep.shape, bf16), (), (keep, moved), after, 8)


def pack_kernel(qkv_ref, proj_ref, qk_ref, vp_ref):
    qk_ref[...] = jnp.concatenate([qkv_ref[0], qkv_ref[1]], axis=1).astype(bf16)
    vp_ref[...] = jnp.concatenate([qkv_ref[2], proj_ref[...].T], axis=1).astype(bf16)


def pair_kernel(left_ref, right_ref, out_ref):
    width = left_ref.shape[1]
    out_ref[:, :width] = left_ref[...]
    out_ref[:, width:] = right_ref[...]


def upstream_kernel(lengths_one, lengths_two, cot_ref, *out_refs):
    rows = cot_ref.shape[1]
    for b, (lengths_ref, out_ref) in enumerate(zip((lengths_one, lengths_two), out_refs)):
        valid = lax.broadcasted_iota(jnp.int32, (rows, 1), 0) < valid_count(lengths_ref)
        out_ref[...] = jnp.where(valid, cot_ref[b].astype(f32), 0.0).astype(bf16)


def cast_kernel(*refs):
    half = len(refs) // 2
    for source, out in zip(refs[:half], refs[half:]):
        out[...] = source[...].astype(bf16)


def segment_grid(lengths_ref, dims, axis, first=0):
    places = first + lax.broadcasted_iota(jnp.int32, dims, axis)
    ids = jnp.zeros(dims, jnp.int32)
    bound = jnp.int32(0)
    for k in range(lengths_ref.shape[1]):
        bound = bound + lengths_ref[0, k]
        ids = ids + (places >= bound).astype(jnp.int32)
    return ids


def same_segment(lengths_ref, start, low, high):
    queries = segment_grid(lengths_ref, (TILE, 1), 0, start)
    return queries == segment_grid(lengths_ref, (1, high - low), 1, low)


def valid_count(lengths_ref):
    total = jnp.int32(0)
    for k in range(lengths_ref.shape[1]):
        total = total + lengths_ref[0, k]
    return total


def first_norm_kernel(lengths_one, lengths_two, inputs_ref, times_one, times_two, vecs_ref, *refs):
    rows = inputs_ref.shape[1]
    for b, (lengths_ref, times_ref) in enumerate(((lengths_one, times_one), (lengths_two, times_two))):
        stream_ref, normed_ref = refs[2 * b : 2 * b + 2]
        depth = times_ref.shape[0]
        ids = segment_grid(lengths_ref, (rows, 1), 0)
        for start in range(0, rows, BLOCK):
            here = slice(start, start + BLOCK)
            lanes = lax.broadcasted_iota(jnp.int32, (BLOCK, depth), 1)
            pick = (ids[here] == lanes).astype(f32).astype(bf16)
            stream = inputs_ref[b, here, :].astype(f32) + dot(pick, times_ref[...], NN)
            stream_ref[here, :] = stream
            xhat, _ = norm_parts(stream)
            normed_ref[here, :] = (xhat * vecs_ref[0:1, :] + vecs_ref[1:2, :]).astype(bf16)


def windows(rows, reach):
    size = min(rows, TILE + 2 * reach)
    out = []
    for start in range(0, rows, TILE):
        low = max(0, start - reach)
        high = min(rows, start + TILE + reach)
        if (high - low) % 128:
            low = min(low, rows - size)
            high = low + size
        out.append((start, low, high))
    return out


def split_heads(low, rows, q_s, k_s, v_s):
    heads = q_s.shape[0]
    width = heads * HD
    for h in range(heads):
        cut = h * HD
        q_s[h, rows, :] = low[:, cut : cut + HD] * jnp.array(HD**-0.5, bf16)
        k_s[h, rows, :] = low[:, width + cut : width + cut + HD]
        v_s[h, rows, :] = low[:, 2 * width + cut : 2 * width + cut + HD]


def forward_kernel(reach, carried, lengths_ref, normed_ref, qk_ref, wv_ref, bias_ref, *refs):
    att_ref, qkv_ref, lse_ref, *pair_refs, q_s, k_s, v_s = refs[carried:]
    rows, width = att_ref.shape
    heads = range(width // HD)
    for start in range(0, rows, BLOCK):
        piece = slice(start, start + BLOCK)
        normed = normed_ref[piece, :]
        pair = dot(normed, qk_ref[...], NN)
        values = dot(normed, wv_ref[...], NN)
        low = (jnp.concatenate([pair, values], axis=1) + bias_ref[...]).astype(bf16)
        qkv_ref[piece, :] = low
        split_heads(low, piece, q_s, k_s, v_s)
    lanes = lax.broadcasted_iota(jnp.int32, (TILE, 128), 1)
    for start, low, high in windows(rows, reach):
        tile = slice(start, start + TILE)
        allowed = same_segment(lengths_ref, start, low, high)
        scores = [dot(q_s[h, tile, :], k_s[h, low:high, :], NT) for h in heads]
        scores = [jnp.where(allowed, s, masked_score) for s in scores]
        peaks = [jnp.max(s, axis=-1, keepdims=True) for s in scores]
        exponents = [jnp.exp(s - p) for s, p in zip(scores, peaks)]
        totals = [jnp.sum(e, axis=-1, keepdims=True) for e in exponents]
        probs = [(e * (1.0 / t)).astype(bf16) for e, t in zip(exponents, totals)]
        outs = [dot(p, v_s[h, low:high, :], NN).astype(bf16) for h, p in enumerate(probs)]
        att_ref[tile, :] = jnp.concatenate(outs, axis=1)
        logs = jnp.zeros((TILE, 128), f32)
        for h in heads:
            logs = jnp.where(lanes == h, peaks[h] + jnp.log(totals[h]), logs)
        lse_ref[tile, :] = logs
    for ref, pair_ref in zip(refs[:carried], pair_refs):
        pair_ref[...] = jnp.concatenate([att_ref[...], ref[...]], axis=1)


def hidden_kernel(lengths_ref, *refs):
    first_refs, att_refs = refs[:2], refs[-11:-9]
    stream_ref, vecs_ref, up_ref, bias_ref = refs[-9:-5]
    middle_ref, normed_ref, active_ref, slope_ref, square_ref = refs[-5:]
    rows, features = stream_ref.shape
    width = first_refs[0].shape[1] // 4
    step = att_refs[0].shape[1] // 2
    total = valid_count(lengths_ref)
    squares = jnp.zeros((1, features), f32)
    for start in range(0, rows, BLOCK):
        here = slice(start, start + BLOCK)
        valid = start + lax.broadcasted_iota(jnp.int32, (BLOCK, 1), 0) < total
        own, over, near, across = (
            dot(a[here, k * step : k * step + width], p[:, (2 * k + 1) * width : (2 * k + 2) * width], NT)
            for a, p in zip(att_refs, first_refs)
            for k in range(2)
        )
        branch = ((own + near) + (over + across)) + vecs_ref[4:5, :]
        kept = jnp.where(valid, branch, 0.0)
        squares = squares + rows_sum(kept * kept)
        middle = stream_ref[here, :] + branch
        middle_ref[here, :] = middle
        xhat, _ = norm_parts(middle)
        normed = (xhat * vecs_ref[2:3, :] + vecs_ref[3:4, :]).astype(bf16)
        normed_ref[here, :] = normed
        hidden = dot(normed, up_ref[...], NN) + bias_ref[...]
        cdf = 0.5 + 0.5 * lax.erf(hidden * 0.5**0.5)
        pdf = jnp.exp(-0.5 * hidden * hidden) * 0.3989422804014327
        active_ref[here, :] = (hidden * cdf).astype(bf16)
        slope_ref[here, :] = cdf + hidden * pdf
    square_ref[...] = squares


def hidden_back_kernel(upstream_ref, slope_ref, up_ref, down_ref, grad_ref, away_ref, keep_ref, offset_ref):
    rows = upstream_ref.shape[0]
    half = rows // 2
    first = (1 - core_index()) * half

    def rows_step(t, offsets):
        here = pl.ds(pl.multiple_of(lax.rem(first + t * CHUNK, rows), CHUNK), CHUNK)
        grad = dot(upstream_ref[here, :], down_ref[...], NN) * slope_ref[here, :]
        low = grad.astype(bf16)
        grad_ref[here, :] = low
        part = dot(low, up_ref[...], NT)

        @pl.when(t * CHUNK < half)
        def _():
            away_ref[pl.ds(pl.multiple_of(t * CHUNK, CHUNK), CHUNK), :] = part.astype(bf16)

        @pl.when(t * CHUNK >= half)
        def _():
            keep_ref[pl.ds(pl.multiple_of(t * CHUNK - half, CHUNK), CHUNK), :] = part

        return offsets + rows_sum(grad)

    offset_ref[...] = lax.fori_loop(0, rows // CHUNK, rows_step, jnp.zeros(offset_ref.shape, f32))


def down_kernel(side, active_ref, down_ref, out_ref):
    half = active_ref.shape[0] // 2
    core = core_index()
    base = (core if side else 1 - core) * half
    here = pl.ds(pl.multiple_of(base, half), half)
    out_ref[...] = dot(active_ref[here, :], down_ref[...], NT).astype(out_ref.dtype)


def products_kernel(pairs, *refs):
    out_ref = refs[-1]
    for m in range(0, out_ref.shape[0], BLOCK):
        cut = slice(m, m + BLOCK)
        column = 0
        for p in range(pairs):
            left_one, left_two, right_one, right_two = refs[4 * p : 4 * p + 4]
            rows = left_one.shape[0]
            part = dot(left_one[:, cut], right_one[:rows, :], TN) + dot(left_two[:, cut], right_two[:rows, :], TN)
            out_ref[cut, column : column + part.shape[1]] = part.astype(out_ref.dtype)
            column += part.shape[1]


def parted_kernel(r, *refs):
    away_ref, keep_ref, full_s = refs[-3:]
    products_kernel(len(refs) // 4, *refs[:-3], full_s)
    inner = dp_bit(1)
    for o in range(away_ref.shape[0] // r):
        for out_ref, side in ((away_ref, 1 - inner), (keep_ref, inner)):
            start = pl.multiple_of((o * 2 + side) * r, 8)
            out_ref[o * r : (o + 1) * r, :] = full_s[pl.ds(start, r), :].astype(bf16)


def parted(arrays, n, after):
    rows, width = arrays[0].shape[1], sum(v.shape[1] for v in arrays[2::4])
    r = rows // n
    if r % 16:
        kernel = functools.partial(products_kernel, len(arrays) // 4)
        full = call(kernel, shape((rows, width), bf16), (), arrays, after)
        view = full.reshape(n // 2, 2, r, width)
        inner = dp_bit(1)
        pieces = [lax.dynamic_index_in_dim(view, i, 1, False) for i in (1 - inner, inner)]
        return [v.reshape(rows // 2, width) for v in pieces]
    outs = (shape((rows // 2, width), bf16),) * 2
    scratch = [pltpu.VMEM((rows, width), f32)]
    return call(functools.partial(parted_kernel, r), outs, (), arrays, after, 24, scratch)


def backward_kernel(
    reach,
    lengths_ref,
    both_ref,
    other_ref,
    middle_ref,
    upstream_ref,
    vecs_ref,
    qk_ref,
    wv_ref,
    proj_ref,
    qkv_ref,
    lse_ref,
    grad_middle_ref,
    low_ref,
    mixed_ref,
    away_ref,
    keep_ref,
    sums_ref,
    heads_ref,
    q_s,
    k_s,
    v_s,
    g_s,
    dk_s,
    dv_s,
):
    rows, features = middle_ref.shape
    half = rows // 2
    width = qkv_ref.shape[1] // 3
    heads = range(width // HD)
    core = core_index()
    gain = vecs_ref[2:3, :]
    sums = []
    for piece_ref, base in ((both_ref, core * half), (other_ref, (1 - core) * half)):

        def rows_step(t, acc, piece_ref=piece_ref, base=base):
            off = pl.multiple_of(base + t * TILE, TILE)
            here = pl.ds(off, TILE)
            gnt = piece_ref[pl.ds(pl.multiple_of(t * TILE, TILE), TILE), :].astype(f32)
            xhat, scale = norm_parts(middle_ref[here, :])
            upstream = upstream_ref[here, :].astype(f32)
            grad_middle = upstream + norm_back(gnt * gain, xhat, scale)
            grad_middle_ref[here, :] = grad_middle
            low_ref[here, :] = grad_middle.astype(bf16)
            terms = (gnt * xhat, gnt, grad_middle, upstream)
            return tuple(a + rows_sum(v) for a, v in zip(acc, terms))

        start = (jnp.zeros((1, features), f32),) * 4
        sums.append(lax.fori_loop(0, half // TILE, rows_step, start))
    sums_ref[...] = jnp.concatenate([a + b for a, b in zip(*sums)], axis=0)
    for start in range(0, rows, BLOCK):
        piece = slice(start, start + BLOCK)
        split_heads(qkv_ref[piece, :], piece, q_s, k_s, v_s)
        grad_att = dot(low_ref[piece, :], proj_ref[...], NN).astype(bf16)
        for h in heads:
            g_s[h, piece, :] = grad_att[:, h * HD : (h + 1) * HD]
    dk_s[...] = jnp.zeros_like(dk_s)
    dv_s[...] = jnp.zeros_like(dv_s)
    for start, low, high in windows(rows, reach):
        tile = slice(start, start + TILE)
        keys = slice(low, high)
        allowed = same_segment(lengths_ref, start, low, high)
        scores = [dot(q_s[h, tile, :], k_s[h, keys, :], NT) for h in heads]
        grad_probs = [dot(g_s[h, tile, :], v_s[h, keys, :], NT) for h in heads]
        probs = [jnp.exp(jnp.where(allowed, s, masked_score) - lse_ref[tile, h : h + 1]) for h, s in enumerate(scores)]
        inner = [jnp.sum(p * g, axis=-1, keepdims=True) for p, g in zip(probs, grad_probs)]
        grads = [(p * (g - i)).astype(bf16) for p, g, i in zip(probs, grad_probs, inner)]
        lows = [p.astype(bf16) for p in probs]
        dqs = [(dot(g, k_s[h, keys, :], NN) * HD**-0.5).astype(bf16) for h, g in enumerate(grads)]
        mixed_ref[tile, :width] = jnp.concatenate(dqs, axis=1)
        dks = [dot(g, q_s[h, tile, :], TN) for h, g in enumerate(grads)]
        dvs = [dot(p, g_s[h, tile, :], TN) for h, p in enumerate(lows)]
        for h in heads:
            dk_s[h, keys, :] += dks[h]
            dv_s[h, keys, :] += dvs[h]
    for start in range(0, rows, BLOCK):
        piece = slice(start, start + BLOCK)
        both = [ref[h, piece, :].astype(bf16) for ref in (dk_s, dv_s) for h in heads]
        mixed_ref[piece, width:] = jnp.concatenate(both, axis=1)
    heads_ref[...] = rows_sum(mixed_ref[...].astype(f32))
    for out_ref, base in ((away_ref, (1 - core) * half), (keep_ref, core * half)):
        here = pl.ds(pl.multiple_of(base, half), half)
        part = dot(mixed_ref[here, : 2 * width], qk_ref[...], NT)
        part = part + dot(mixed_ref[here, 2 * width :], wv_ref[...], NT)
        out_ref[...] = part.astype(out_ref.dtype)


def input_grad_kernel(both_ref, other_ref, stream_ref, middle_ref, vecs_ref, *refs):
    out_ref, sums_ref = refs[-2:]
    rows, features = stream_ref.shape
    half = rows // 2
    core = core_index()
    gain = vecs_ref[0:1, :]
    sums = []
    for piece_ref, base in ((both_ref, core * half), (other_ref, (1 - core) * half)):

        def rows_step(t, acc, piece_ref=piece_ref, base=base):
            here = pl.ds(pl.multiple_of(base + t * TILE, TILE), TILE)
            grad = piece_ref[pl.ds(pl.multiple_of(t * TILE, TILE), TILE), :].astype(f32)
            xhat, scale = norm_parts(stream_ref[here, :])
            out_ref[0, here, :] = middle_ref[here, :] + norm_back(grad * gain, xhat, scale)
            return (acc[0] + rows_sum(grad * xhat), acc[1] + rows_sum(grad))

        start = (jnp.zeros((1, features), f32),) * 2
        sums.append(lax.fori_loop(0, half // TILE, rows_step, start))
    sums_ref[...] = jnp.concatenate([a + b for a, b in zip(*sums)], axis=0)


def input_grad_call(which, both, other, stream, middle, vecs, filled, after):
    rows, features = stream.shape
    count = len(after)

    def kernel(*refs):
        input_grad_kernel(*refs[count:])

    whole = pl.BlockSpec(memory_space=pltpu.VMEM)
    anywhere = pl.BlockSpec(memory_space=pl.ANY)
    return pl.pallas_call(
        kernel,
        grid=(1,),
        out_shape=(shape((2, rows, features), f32), shape((2, features), f32)),
        in_specs=[anywhere] * count + [whole] * 5 + [anywhere] * len(filled),
        out_specs=(pl.BlockSpec((1, rows, features), lambda i: (which, 0, 0)), whole),
        input_output_aliases={count + 5: 0} if filled else {},
        compiler_params=pltpu.CompilerParams(vmem_limit_bytes=24 * 2**20),
        cost_estimate=cost(),
    )(*after, both, other, stream, middle, vecs, *filled)


def output_kernel(lengths_one, lengths_two, *refs):
    vecs_ref, branch_one, branch_two, out_ref, sums_ref = refs[6:]
    features = out_ref.shape[2]
    half = out_ref.shape[1] // 2
    core = core_index()
    sums = []
    count = jnp.int32(0)
    for b, lengths_ref in enumerate((lengths_one, lengths_two)):
        total = valid_count(lengths_ref)
        count = count + total
        both_ref, other_ref, middle_ref = refs[3 * b : 3 * b + 3]
        for piece_ref, base in ((both_ref, core * half), (other_ref, (1 - core) * half)):

            def rows_step(t, acc, piece_ref=piece_ref, base=base, middle_ref=middle_ref, total=total, b=b):
                off = pl.multiple_of(base + t * TILE, TILE)
                here = pl.ds(off, TILE)
                two = piece_ref[pl.ds(pl.multiple_of(t * TILE, TILE), TILE), :].astype(f32) + vecs_ref[5:6, :]
                whole = middle_ref[here, :] + two
                out_ref[b, here, :] = whole.astype(bf16)
                valid = off + lax.broadcasted_iota(jnp.int32, (TILE, 1), 0) < total
                terms = [jnp.where(valid, v, 0.0) for v in (whole, two)]
                return tuple(a + rows_sum(v * v) for a, v in zip(acc, terms))

            start = (jnp.zeros((1, features), f32),) * 2
            sums.append(lax.fori_loop(0, half // TILE, rows_step, start))
    whole, two = ((a + b) + (c + d) for a, b, c, d in zip(*sums))
    lines = [jnp.sum(v, axis=1, keepdims=True) for v in (whole, branch_one[...] + branch_two[...], two)]
    lines.append(jnp.full((1, 1), count.astype(f32), f32))
    for i in range(8):
        sums_ref[i : i + 1, :] = jnp.broadcast_to(lines[min(i, 3)], (1, 128))


def message_kernel(*refs):
    out_ref, grads_ref = refs[-2:]
    norm_one, norm_two, sums_one, sums_two, off_one, off_two, heads_one, heads_two = refs[-10:-2]
    pairs = refs[:-10]
    width = heads_one.shape[1] // 3
    column = 0
    squares = jnp.zeros((1, 1), f32)
    for keep_ref, moved_ref in zip(pairs[::2], pairs[1::2]):
        grad = keep_ref[...].astype(f32) + moved_ref[...].astype(f32)
        stop = column + grad.shape[1]
        grads_ref[:, column:stop] = grad
        squares = squares + whole_sum(grad * grad)
        column = stop
    out_ref[...] = jnp.zeros_like(out_ref)
    out_ref[0:2, :] = norm_one[...] + norm_two[...]
    out_ref[2:6, :] = sums_one[...] + sums_two[...]
    out_ref[6:7, :] = off_one[...] + off_two[...]
    heads = heads_one[...] + heads_two[...]
    out_ref[8:9, :width] = heads[:, :width]
    out_ref[9:10, :width] = heads[:, 2 * width :]
    out_ref[10:11, :] = jnp.broadcast_to(squares, (1, out_ref.shape[1]))


def partial_kernel(message_ref, out_ref):
    squares = whole_sum(message_ref[8:10, :] * message_ref[8:10, :])
    squares = squares + whole_sum(message_ref[6:7, :] * message_ref[6:7, :])
    out_ref[...] = jnp.broadcast_to(squares + message_ref[10:11, 0:1], out_ref.shape)


def rms_kernel(features, sums_ref, out_ref):
    values = jnp.sqrt(sums_ref[...] / (sums_ref[3:4, :] * features))
    for i in range(3):
        out_ref[i] = jnp.max(values[i : i + 1, :])


def rms_call(sums, features):
    return pl.pallas_call(
        functools.partial(rms_kernel, features),
        out_shape=shape((3,), f32),
        in_specs=[pl.BlockSpec(memory_space=pltpu.VMEM)],
        out_specs=pl.BlockSpec(memory_space=pltpu.SMEM),
        compiler_params=pltpu.CompilerParams(vmem_limit_bytes=8 * 2**20),
        cost_estimate=cost(),
        name="rms_kernel",
    )(sums)


def adamw_kernel(partial_ref, moved_ref, message_ref, grads_ref, *refs):
    count = 21
    sources, targets, norm_ref = refs[:count], refs[count : 2 * count], refs[2 * count]
    inputs, outputs = refs[2 * count + 1 : 3 * count + 1], refs[3 * count + 1 : 4 * count + 1]
    read_sems, write_sems = refs[4 * count + 1 :]
    reads = [pltpu.make_async_copy(sources[i], inputs[i], read_sems.at[i]) for i in range(count)]
    writes = [pltpu.make_async_copy(outputs[i], targets[i], write_sems.at[i]) for i in range(count)]
    for copy in reads:
        copy.start()
    width = inputs[0].shape[2]
    hidden = inputs[6].shape[1]
    vecs = message_ref[0:6, :]
    norm = jnp.sqrt(partial_ref[0:1, 0:1] + moved_ref[0:1, 0:1] + whole_sum(vecs * vecs))
    norm_ref[0] = jnp.max(norm)
    clip = jnp.minimum(1.0, clip_limit / (norm + 1e-06))

    def step(p, gradient, at=Ellipsis):
        weight, moment, square = (ref[at] for ref in inputs[3 * p : 3 * p + 3])
        decay = matrix_decay if p < 4 else 0.0
        factor = clip if gradient.ndim == 2 else jnp.max(clip)
        values = adamw_step(weight, moment, square, gradient, step_rates[p], decay, factor)
        for ref, value in zip(outputs[3 * p : 3 * p + 3], values):
            ref[at] = value

    start = 4 * width
    parts = (
        tuple((grads_ref[:, j * width : (j + 1) * width], j) for j in range(3)),
        ((grads_ref[:, 3 * width : start].T,),),
        ((grads_ref[:, start : start + hidden],),),
        ((grads_ref[:, start + hidden :],),),
        ((vecs,),),
        ((message_ref[8:10, : inputs[15].shape[1]],),),
        ((message_ref[6, :],),),
    )
    for p, steps in enumerate(parts):
        for copy in reads[3 * p : 3 * p + 3]:
            copy.wait()
        for arguments in steps:
            step(p, *arguments)
        for copy in writes[3 * p : 3 * p + 3]:
            copy.start()
    for copy in writes:
        copy.wait()


def adamw_call(partial, moved, message, grads, state):
    in_vmem = pl.BlockSpec(memory_space=pltpu.VMEM)
    anywhere = pl.BlockSpec(memory_space=pltpu.MemorySpace.HBM)
    count = len(state)
    return pl.pallas_call(
        adamw_kernel,
        out_shape=tuple(shape(v.shape, f32) for v in state) + (shape((1,), f32),),
        in_specs=[in_vmem] * 4 + [anywhere] * count,
        out_specs=(anywhere,) * count + (pl.BlockSpec(memory_space=pltpu.SMEM),),
        scratch_shapes=[pltpu.VMEM(v.shape, f32) for v in state] * 2 + [pltpu.SemaphoreType.DMA((count,))] * 2,
        compiler_params=pltpu.CompilerParams(vmem_limit_bytes=24 * 2**20),
        cost_estimate=cost(),
    )(partial, moved, message, grads, *state)


def build(n):
    top = n // 2

    def local(
        inputs,
        time_first,
        time_second,
        lengths_first,
        lengths_second,
        cotangent,
        w_qkv,
        m_qkv,
        v_qkv,
        w_proj,
        m_proj,
        v_proj,
        w_up,
        m_up,
        v_up,
        w_down,
        m_down,
        v_down,
        w_vecs,
        m_vecs,
        v_vecs,
        b_heads,
        m_heads,
        v_heads,
        b_hidden,
        m_hidden,
        v_hidden,
    ):
        rows, features = inputs.shape[1], inputs.shape[2]
        r, _, width = w_qkv.shape
        hidden = w_up.shape[1]
        heads = width // HD
        half = rows // 2
        lengths = (lengths_first, lengths_second)
        whole_f = shape((rows, features), f32)
        whole_b = shape((rows, features), bf16)
        hidden_b = shape((rows, hidden), bf16)
        half_b = shape((half, features), bf16)
        half_f = shape((half, features), f32)
        line = shape((1, features), f32)

        def swap(v, bit):
            return swap_bit(v, "dp", n, bit)

        def gathered(shard, bit, stop, after=()):
            while bit > stop:
                (shard,) = merged(shard, swap(shard, bit), r, bit, after)
                after = ()
                bit //= 2
            return shard

        qk, vp = call(
            pack_kernel, (shape((r, 2 * width), bf16),) * 2, (), (w_qkv.transpose(1, 0, 2), w_proj), (), 8
        )
        times = [jnp.pad(t[0], ((0, 16 - t.shape[1]), (0, 0))) for t in (time_first, time_second)]
        stream_one, normed_one, stream_two, normed_two = call(
            first_norm_kernel, (whole_f, whole_b) * 2, lengths, (inputs, *times, w_vecs), (qk,), 24
        )
        stream, normed = (stream_one, stream_two), (normed_one, normed_two)
        qk = gathered(qk, top, top // 2, (normed_two,))
        vp = gathered(vp, top, top // 2, (qk,))
        qk = gathered(qk, top // 2, 1, (vp,))
        (up,) = call(cast_kernel, (shape((r, hidden), bf16),), (), (w_up,), (qk,), 8)
        vp = gathered(vp, top // 2, 1, (up,))
        (qk,) = merged(qk, swap(qk, 1), r, 1, (vp,))
        (down,) = call(cast_kernel, (shape((r, hidden), bf16),), (), (w_down.T,), (qk,), 8)
        up = gathered(up, top, top // 2, (down,))
        wv, proj = merged(vp, swap(vp, 1), r, 1, (up,), (width, width))

        def spread(v, after=()):
            moved = over_chip(v)
            pair = call(pair_kernel, shape((rows, 2 * v.shape[1]), bf16), (), (v, moved), after, 8)
            return [pair, over_core(pair)]

        bias = jnp.concatenate([b_heads[0], jnp.zeros_like(b_heads[0]), b_heads[1]])[None]
        head_low = pltpu.VMEM((heads, rows, HD), bf16)
        head_full = pltpu.VMEM((heads, rows, HD), f32)
        after = (wv,)
        att, sent, qkv, lse = [], [], [], []
        for b in range(2):
            carried = (proj,) if b == 0 else ()
            a, q, l, *pair = call(
                functools.partial(forward_kernel, REACH[b], len(carried)),
                (
                    shape((rows, width), bf16),
                    shape((rows, 3 * width), bf16),
                    shape((rows, 128), f32),
                    *(shape((rows, 2 * width), bf16) for _ in carried),
                ),
                (lengths[b],),
                (normed[b], qk, wv, bias, *carried),
                after,
                12,
                [head_low] * 3,
            )
            att.append(a)
            sent.append(pair[0] if pair else a)
            qkv.append(q)
            lse.append(l)
            after = (l,)
            if b == 0:
                down = gathered(down, top, top // 2, after)
                up = gathered(up, top // 2, 1, (down,))
                down = gathered(down, top // 2, 1, (up,))
                after = (down,)
        att_first = spread(sent[0], after)
        (up,) = merged(up, swap(up, 1), r, 1, (att_first[0],), weight=4)
        after = (up,)

        names = [[] for _ in range(9)]
        att_own = []
        for b in range(2):
            outs = call(
                hidden_kernel,
                (whole_f, whole_b, hidden_b, shape((rows, hidden), f32), line),
                (lengths[b],),
                (*att_first, *att_own, stream[b], w_vecs, up, b_hidden[None]),
                after,
            )
            for kept, v in zip(names, outs):
                kept.append(v)
            after = (outs[-1],)
            if b == 0:
                att_own = spread(sent[1], after)
                upstream = call(upstream_kernel, (whole_b,) * 2, lengths, (cotangent,), (att_own[0],))
                after = (upstream[1],)
        (down,) = merged(down, swap(down, 1), r, 1, after)
        low, parts = [], [[], []]

        def down_part(b, side, after):
            out = (half_b, half_f)[side]
            part = call(functools.partial(down_kernel, side), out, (), (active[b], down), after)
            parts[b].append(part)
            return part

        after = (down,)
        for b in range(2):
            outs = call(
                hidden_back_kernel,
                (hidden_b, half_b, half_f, shape((1, hidden), f32)),
                (),
                (upstream[b], names[3][b], up, down),
                after,
            )
            for kept, v in zip(names[5:], outs):
                kept.append(v)
            middle, normed_mid, active, slope, branch_square, grad_hidden, away, keep, offsets = names
            if b == 0:
                after = (down_part(0, 0, (outs[-1],)),)
            else:
                bulk = parted((*normed_mid, *grad_hidden, *upstream, *active), n, (outs[-1],))
                bulk_moved = swap(bulk[0], 1)
                after = (bulk[0],)
            low.append(add(keep[b], over_core(away[b]), after))
            after = (low[b],)
        both = add(low[0], over_chip(low[0]), after)
        gnt = [(both, over_core(both))]
        after = (down_part(0, 1, (both,)),)

        grad_middle, middle_low, grad_mixed, sums, head_sums, back_low = [], [], [], [], [], []
        for b in range(2):
            outs = call(
                functools.partial(backward_kernel, REACH[b]),
                (
                    whole_f,
                    whole_b,
                    shape((rows, 3 * width), bf16),
                    half_b,
                    half_f,
                    shape((4, features), f32),
                    shape((1, 3 * width), f32),
                ),
                (lengths[b],),
                (*gnt[b], middle[b], upstream[b], w_vecs, qk, wv, proj, qkv[b], lse[b]),
                after,
                24,
                [head_low] * 4 + [head_full] * 2,
            )
            grad_middle.append(outs[0])
            middle_low.append(outs[1])
            grad_mixed.append(outs[2])
            sums.append(outs[5])
            head_sums.append(outs[6])
            after = (outs[6],)
            if b == 0:
                both = add(low[1], over_chip(low[1]), after)
                gnt.append((both, over_core(both)))
                after = (down_part(1, 0, (both,)),)
            else:
                bulk = split(bulk[1], bulk_moved, r, 2, after)
                bulk_moved = swap(bulk[0], 2)
                after = (down_part(1, 1, (bulk[0],)),)
            back_low.append(add(outs[4], over_core(outs[3]), after))
            after = (back_low[b],)

        first = parted((*normed, *grad_mixed, *middle_low, *att), n, after)
        first_moved = swap(first[0], 1)
        both = add(back_low[0], over_chip(back_low[0]), (first[0],))
        piece = (both, over_core(both))
        part = [add(parts[0][1], over_core(parts[0][0]), (both,))]
        after = (part[0],)
        bit = 4
        while bit < n:
            bulk = split(bulk[1], bulk_moved, r, bit, after)
            bulk_moved = swap(bulk[0], bit)
            after = (bulk[0],)
            bit *= 2
        input_grad, pair = input_grad_call(0, *piece, stream[0], grad_middle[0], w_vecs, (), after)
        norm_sums = [pair]
        first = split(first[1], first_moved, r, 2, (pair,))
        first_moved = swap(first[0], 2)
        both = add(back_low[1], over_chip(back_low[1]), (first[0],))
        piece = (both, over_core(both))
        part.append(add(parts[1][1], over_core(parts[1][0]), (both,)))
        after = (part[1],)
        bit = 4
        while bit < n:
            first = split(first[1], first_moved, r, bit, after)
            first_moved = swap(first[0], bit)
            after = (first[0],)
            bit *= 2
        input_grad, pair = input_grad_call(
            1, *piece, stream[1], grad_middle[1], w_vecs, (input_grad,), after
        )
        norm_sums.append(pair)
        both = add(part[0], over_chip(part[0]), (pair,))
        two = [both, over_core(both), middle[0]]

        message, grads = call(
            message_kernel,
            (shape((16, features), f32), shape((r, 4 * width + 2 * hidden), f32)),
            (),
            (first[1], first_moved, bulk[1], bulk_moved, *norm_sums, *sums, *offsets, *head_sums),
            (both,),
            16,
        )
        both = add(part[1], over_chip(part[1]), (message,))
        two += [both, over_core(both), middle[1]]

        def hop(v, moved, after=()):
            return call(sum_kernel, shape(v.shape, f32), (), (v, moved), after, 8)

        message = hop(message, swap(message, 1), (both,))
        block_out, out_sums = call(
            output_kernel,
            (shape((2, rows, features), bf16), shape((8, 128), f32)),
            lengths,
            (*two, w_vecs, *branch_square),
            (message,),
        )
        after = (out_sums,)
        bit = 2
        while bit < n:
            message = hop(message, swap(message, bit), after)
            after = ()
            bit *= 2
        partial = call(partial_kernel, shape((8, 128), f32), (), (message,), (), 8)
        out_sums = hop(out_sums, swap(out_sums, 1), (partial,))
        partial = hop(partial, over_core(partial), (out_sums,))
        out_sums = hop(out_sums, swap(out_sums, 2), (partial,))
        state = (
            *(v.transpose(1, 0, 2) for v in (w_qkv, m_qkv, v_qkv)),
            *(w_proj, m_proj, v_proj),
            *(w_up, m_up, v_up),
            *(v.T for v in (w_down, m_down, v_down)),
            *(w_vecs, m_vecs, v_vecs),
            *(b_heads, m_heads, v_heads),
            *(b_hidden, m_hidden, v_hidden),
        )
        *updated, grad_norm = adamw_call(partial, over_chip(partial), message, grads, state)
        bit = 4
        while bit < n:
            out_sums = hop(out_sums, swap(out_sums, bit))
            bit *= 2
        stream_rms = rms_call(out_sums, features)
        return (
            block_out,
            input_grad,
            grad_norm,
            stream_rms,
            *(v.transpose(1, 0, 2) for v in updated[:3]),
            *updated[3:9],
            *(v.T for v in updated[9:12]),
            *updated[12:18],
            *updated[18:],
        )

    return local


def solution(mesh):
    rows = P(None, "dp", None)
    group = P("dp", None, None)
    qkv, proj, up = P("dp", None, "tensor"), P("tensor", "dp"), P("dp", "tensor")
    params = [qkv] * 3 + [proj] * 3 + [up] * 3 + [proj] * 3 + [P()] * 3
    params += [P(None, "tensor")] * 3 + [P("tensor")] * 3
    return jax.shard_map(
        build(mesh.shape["dp"]),
        mesh=mesh,
        in_specs=(rows, group, group, P("dp", None), P("dp", None), rows, *params),
        out_specs=(rows, rows, P(), P(), *params),
        check_vma=False,
    )
```

```python
import functools

import jax
import jax.numpy as jnp
from jax import lax
from jax.experimental import pallas as pl
from jax.experimental.pallas import tpu as pltpu
from jax.sharding import PartitionSpec as P

HD = 64
STEP = 5
TILE = 128
BLOCK = 256
CHUNK = 384
REACH = (64, 128)

norm_eps = 1e-05
clip_limit = 1.0
beta_first = 0.5
beta_second = 0.5
adam_eps = 1e-08
matrix_decay = 0.01
masked_score = -1e30
step_rates = (0.03, 0.2, 0.03, 0.015, 0.3, 0.3, 0.3)
bf16 = jnp.bfloat16
f32 = jnp.float32

KERNEL_FLOPS = 7 * 10**9

NN = ((1,), (0,))
NT = ((1,), (1,))
TN = ((0,), (0,))


def dot(a, b, dims):
    return lax.dot_general(a, b, (dims, ((), ())), preferred_element_type=f32)


def shape(dims, dtype):
    return jax.ShapeDtypeStruct(dims, dtype)


def cost(weight=1):
    return pl.CostEstimate(flops=weight * KERNEL_FLOPS, bytes_accessed=0, transcendentals=0)


def call(body, outs, words, arrays, after=(), limit=16, scratch=(), weight=1):
    count = len(after)

    def kernel(*refs):
        body(*refs[: len(words)], *refs[len(words) + count :])

    in_vmem = pl.BlockSpec(memory_space=pltpu.VMEM)
    in_specs = [pl.BlockSpec(memory_space=pltpu.SMEM)] * len(words)
    in_specs += [pl.BlockSpec(memory_space=pl.ANY)] * count + [in_vmem] * len(arrays)
    return pl.pallas_call(
        kernel,
        out_shape=outs,
        in_specs=in_specs,
        out_specs=(in_vmem,) * len(outs) if isinstance(outs, tuple) else in_vmem,
        scratch_shapes=list(scratch),
        compiler_params=pltpu.CompilerParams(vmem_limit_bytes=limit * 2**20),
        cost_estimate=cost(weight),
        name=getattr(body, "func", body).__name__,
    )(*words, *after, *arrays)


def core_index():
    return lax.rem(lax.axis_index("tensor"), 2)


def dp_bit(bit):
    return lax.rem(lax.div(lax.axis_index("dp"), bit), 2)


def rows_sum(v):
    return jnp.sum(v, axis=0, keepdims=True)


def whole_sum(v):
    return jnp.sum(rows_sum(v), axis=1, keepdims=True)


def norm_parts(stream):
    center = stream - jnp.mean(stream, axis=-1, keepdims=True)
    spread = jnp.mean(center * center, axis=-1, keepdims=True)
    scale = lax.rsqrt(spread + norm_eps)
    return center * scale, scale


def norm_back(scaled, xhat, scale):
    mean = jnp.mean(scaled, axis=-1, keepdims=True)
    return scale * (scaled - mean - xhat * jnp.mean(scaled * xhat, axis=-1, keepdims=True))


def adamw_step(weight, moment_old, square_old, gradient, step_rate, decay_value, clip_factor):
    correct_one = 1.0 - beta_first**STEP
    correct_two = 1.0 - beta_second**STEP
    clipped = gradient * clip_factor
    moment_new = beta_first * moment_old + (1.0 - beta_first) * clipped
    square_new = beta_second * square_old + (1.0 - beta_second) * clipped * clipped
    divisor = jnp.sqrt(square_new / correct_two) + adam_eps
    weight_new = weight - step_rate * (moment_new / correct_one / divisor + decay_value * weight)
    return (weight_new, moment_new, square_new)


def swap_bit(v, axis, size, bit):
    return lax.ppermute(v, axis, [(i, i ^ bit) for i in range(size)])


def over_core(v):
    return swap_bit(v, "tensor", 4, 1)


def over_chip(v):
    return swap_bit(v, "tensor", 4, 2)


def merge_kernel(r, bit, own_ref, other_ref, *out_refs):
    mine = dp_bit(bit)
    for g in range(own_ref.shape[0] // r):
        for ref, side in ((own_ref, mine), (other_ref, 1 - mine)):
            start = pl.multiple_of((2 * g + side) * r, 16)
            column = 0
            for out_ref in out_refs:
                stop = column + out_ref.shape[1]
                out_ref[pl.ds(start, r), :] = ref[g * r : (g + 1) * r, column:stop]
                column = stop


def merged(own, other, r, bit, after=(), widths=None, weight=1):
    rows, width = own.shape
    widths = widths or (width,)
    if r % 16:
        own, other = (v.reshape(rows // r, r, width) for v in (own, other))
        sides = [jnp.where(dp_bit(bit) == 0, own, other), jnp.where(dp_bit(bit) == 0, other, own)]
        both = jnp.stack(sides, axis=1).reshape(2 * rows, width)
        return tuple(jnp.split(both, [sum(widths[:i]) for i in range(1, len(widths))], axis=1))
    outs = tuple(shape((2 * rows, w), bf16) for w in widths)
    return call(functools.partial(merge_kernel, r, bit), outs, (), (own, other), after, 8, weight=weight)


def split_kernel(r, bit, keep_ref, moved_ref, away_ref, own_ref):
    mine = dp_bit(bit)
    for g in range(away_ref.shape[0] // r):
        for out_ref, side in ((away_ref, 1 - mine), (own_ref, mine)):
            here = pl.ds(pl.multiple_of((2 * g + side) * r, 16), r)
            total = keep_ref[here, :].astype(f32) + moved_ref[here, :].astype(f32)
            out_ref[g * r : (g + 1) * r, :] = total.astype(out_ref.dtype)


def split(keep, moved, r, bit, after=()):
    half, width = keep.shape[0] // 2, keep.shape[1]
    if r % 16:
        total = (keep.astype(f32) + moved.astype(f32)).reshape(half // r, 2, r, width)
        pieces = [lax.dynamic_index_in_dim(total, i, 1, False) for i in (1 - dp_bit(bit), dp_bit(bit))]
        away, own = (v.reshape(half, width) for v in pieces)
        return away.astype(bf16), own
    outs = (shape((half, width), bf16), shape((half, width), f32))
    return call(functools.partial(split_kernel, r, bit), outs, (), (keep, moved), after, 8)


def sum_kernel(own_ref, moved_ref, *refs):
    *more_refs, out_ref = refs
    total = own_ref[...] + moved_ref[...]
    for ref in more_refs:
        total = total + ref[...]
    out_ref[...] = total


def add_kernel(keep_ref, moved_ref, out_ref):
    out_ref[...] = (keep_ref[...].astype(f32) + moved_ref[...].astype(f32)).astype(bf16)


def add(keep, moved, after=()):
    return call(add_kernel, shape(keep.shape, bf16), (), (keep, moved), after, 8)


def pack_kernel(qkv_ref, proj_ref, qk_ref, vp_ref):
    qk_ref[...] = jnp.concatenate([qkv_ref[0], qkv_ref[1]], axis=1).astype(bf16)
    vp_ref[...] = jnp.concatenate([qkv_ref[2], proj_ref[...].T], axis=1).astype(bf16)


def pair_kernel(left_ref, right_ref, out_ref):
    width = left_ref.shape[1]
    out_ref[:, :width] = left_ref[...]
    out_ref[:, width:] = right_ref[...]


def upstream_kernel(lengths_one, lengths_two, cot_ref, *out_refs):
    rows = cot_ref.shape[1]
    for b, (lengths_ref, out_ref) in enumerate(zip((lengths_one, lengths_two), out_refs)):
        valid = lax.broadcasted_iota(jnp.int32, (rows, 1), 0) < valid_count(lengths_ref)
        out_ref[...] = jnp.where(valid, cot_ref[b].astype(f32), 0.0).astype(bf16)


def cast_kernel(*refs):
    half = len(refs) // 2
    for source, out in zip(refs[:half], refs[half:]):
        out[...] = source[...].astype(bf16)


def segment_grid(lengths_ref, dims, axis, first=0):
    places = first + lax.broadcasted_iota(jnp.int32, dims, axis)
    ids = jnp.zeros(dims, jnp.int32)
    bound = jnp.int32(0)
    for k in range(lengths_ref.shape[1]):
        bound = bound + lengths_ref[0, k]
        ids = ids + (places >= bound).astype(jnp.int32)
    return ids


def same_segment(lengths_ref, start, low, high):
    queries = segment_grid(lengths_ref, (TILE, 1), 0, start)
    return queries == segment_grid(lengths_ref, (1, high - low), 1, low)


def valid_count(lengths_ref):
    total = jnp.int32(0)
    for k in range(lengths_ref.shape[1]):
        total = total + lengths_ref[0, k]
    return total


def first_norm_kernel(lengths_one, lengths_two, inputs_ref, times_one, times_two, vecs_ref, *refs):
    rows = inputs_ref.shape[1]
    for b, (lengths_ref, times_ref) in enumerate(((lengths_one, times_one), (lengths_two, times_two))):
        stream_ref, normed_ref = refs[2 * b : 2 * b + 2]
        depth = times_ref.shape[0]
        ids = segment_grid(lengths_ref, (rows, 1), 0)
        for start in range(0, rows, BLOCK):
            here = slice(start, start + BLOCK)
            lanes = lax.broadcasted_iota(jnp.int32, (BLOCK, depth), 1)
            pick = (ids[here] == lanes).astype(f32).astype(bf16)
            stream = inputs_ref[b, here, :].astype(f32) + dot(pick, times_ref[...], NN)
            stream_ref[here, :] = stream
            xhat, _ = norm_parts(stream)
            normed_ref[here, :] = (xhat * vecs_ref[0:1, :] + vecs_ref[1:2, :]).astype(bf16)


def windows(rows, reach):
    size = min(rows, TILE + 2 * reach)
    out = []
    for start in range(0, rows, TILE):
        low = max(0, start - reach)
        high = min(rows, start + TILE + reach)
        if (high - low) % 128:
            low = min(low, rows - size)
            high = low + size
        out.append((start, low, high))
    return out


def split_heads(low, rows, q_s, k_s, v_s):
    heads = q_s.shape[0]
    width = heads * HD
    for h in range(heads):
        cut = h * HD
        q_s[h, rows, :] = low[:, cut : cut + HD] * jnp.array(HD**-0.5, bf16)
        k_s[h, rows, :] = low[:, width + cut : width + cut + HD]
        v_s[h, rows, :] = low[:, 2 * width + cut : 2 * width + cut + HD]


def forward_kernel(reach, carried, lengths_ref, normed_ref, qk_ref, wv_ref, bias_ref, *refs):
    att_ref, qkv_ref, lse_ref, *pair_refs, q_s, k_s, v_s = refs[carried:]
    rows, width = att_ref.shape
    heads = range(width // HD)
    for start in range(0, rows, BLOCK):
        piece = slice(start, start + BLOCK)
        normed = normed_ref[piece, :]
        pair = dot(normed, qk_ref[...], NN)
        values = dot(normed, wv_ref[...], NN)
        low = (jnp.concatenate([pair, values], axis=1) + bias_ref[...]).astype(bf16)
        qkv_ref[piece, :] = low
        split_heads(low, piece, q_s, k_s, v_s)
    lanes = lax.broadcasted_iota(jnp.int32, (TILE, 128), 1)
    for start, low, high in windows(rows, reach):
        tile = slice(start, start + TILE)
        allowed = same_segment(lengths_ref, start, low, high)
        scores = [dot(q_s[h, tile, :], k_s[h, low:high, :], NT) for h in heads]
        scores = [jnp.where(allowed, s, masked_score) for s in scores]
        peaks = [jnp.max(s, axis=-1, keepdims=True) for s in scores]
        exponents = [jnp.exp(s - p) for s, p in zip(scores, peaks)]
        totals = [jnp.sum(e, axis=-1, keepdims=True) for e in exponents]
        probs = [(e * (1.0 / t)).astype(bf16) for e, t in zip(exponents, totals)]
        outs = [dot(p, v_s[h, low:high, :], NN).astype(bf16) for h, p in enumerate(probs)]
        att_ref[tile, :] = jnp.concatenate(outs, axis=1)
        logs = jnp.zeros((TILE, 128), f32)
        for h in heads:
            logs = jnp.where(lanes == h, peaks[h] + jnp.log(totals[h]), logs)
        lse_ref[tile, :] = logs
    for ref, pair_ref in zip(refs[:carried], pair_refs):
        pair_ref[...] = jnp.concatenate([att_ref[...], ref[...]], axis=1)


def hidden_kernel(lengths_ref, *refs):
    first_refs, att_refs = refs[:2], refs[-11:-9]
    stream_ref, vecs_ref, up_ref, bias_ref = refs[-9:-5]
    middle_ref, normed_ref, active_ref, slope_ref, square_ref = refs[-5:]
    rows, features = stream_ref.shape
    width = first_refs[0].shape[1] // 4
    step = att_refs[0].shape[1] // 2
    total = valid_count(lengths_ref)
    squares = jnp.zeros((1, features), f32)
    for start in range(0, rows, CHUNK):
        here = slice(start, start + CHUNK)
        valid = start + lax.broadcasted_iota(jnp.int32, (CHUNK, 1), 0) < total
        own, over, near, across = (
            dot(a[here, k * step : k * step + width], p[:, (2 * k + 1) * width : (2 * k + 2) * width], NT)
            for a, p in zip(att_refs, first_refs)
            for k in range(2)
        )
        branch = ((own + near) + (over + across)) + vecs_ref[4:5, :]
        kept = jnp.where(valid, branch, 0.0)
        squares = squares + rows_sum(kept * kept)
        middle = stream_ref[here, :] + branch
        middle_ref[here, :] = middle
        xhat, _ = norm_parts(middle)
        normed = (xhat * vecs_ref[2:3, :] + vecs_ref[3:4, :]).astype(bf16)
        normed_ref[here, :] = normed
        hidden = dot(normed, up_ref[...], NN) + bias_ref[...]
        cdf = 0.5 + 0.5 * lax.erf(hidden * 0.5**0.5)
        pdf = jnp.exp(-0.5 * hidden * hidden) * 0.3989422804014327
        active_ref[here, :] = (hidden * cdf).astype(bf16)
        slope_ref[here, :] = cdf + hidden * pdf
    square_ref[...] = squares


def hidden_back_kernel(upstream_ref, slope_ref, up_ref, down_ref, grad_ref, away_ref, keep_ref, offset_ref):
    rows = upstream_ref.shape[0]
    half = rows // 2
    first = (1 - core_index()) * half

    def rows_step(t, offsets):
        here = pl.ds(pl.multiple_of(lax.rem(first + t * CHUNK, rows), CHUNK), CHUNK)
        grad = dot(upstream_ref[here, :], down_ref[...], NN) * slope_ref[here, :]
        low = grad.astype(bf16)
        grad_ref[here, :] = low
        part = dot(low, up_ref[...], NT)

        @pl.when(t * CHUNK < half)
        def _():
            away_ref[pl.ds(pl.multiple_of(t * CHUNK, CHUNK), CHUNK), :] = part.astype(bf16)

        @pl.when(t * CHUNK >= half)
        def _():
            keep_ref[pl.ds(pl.multiple_of(t * CHUNK - half, CHUNK), CHUNK), :] = part

        return offsets + rows_sum(grad)

    offset_ref[...] = lax.fori_loop(0, rows // CHUNK, rows_step, jnp.zeros(offset_ref.shape, f32))


def down_kernel(side, active_ref, down_ref, out_ref):
    half = active_ref.shape[0] // 2
    core = core_index()
    base = (core if side else 1 - core) * half
    here = pl.ds(pl.multiple_of(base, half), half)
    out_ref[...] = dot(active_ref[here, :], down_ref[...], NT).astype(out_ref.dtype)


def products_kernel(pairs, *refs):
    out_ref = refs[-1]
    for m in range(0, out_ref.shape[0], BLOCK):
        cut = slice(m, m + BLOCK)
        column = 0
        for p in range(pairs):
            left_one, left_two, right_one, right_two = refs[4 * p : 4 * p + 4]
            rows = left_one.shape[0]
            part = dot(left_one[:, cut], right_one[:rows, :], TN) + dot(left_two[:, cut], right_two[:rows, :], TN)
            out_ref[cut, column : column + part.shape[1]] = part.astype(out_ref.dtype)
            column += part.shape[1]


def parted_kernel(r, *refs):
    away_ref, keep_ref, full_s = refs[-3:]
    products_kernel(len(refs) // 4, *refs[:-3], full_s)
    inner = dp_bit(1)
    for o in range(away_ref.shape[0] // r):
        for out_ref, side in ((away_ref, 1 - inner), (keep_ref, inner)):
            start = pl.multiple_of((o * 2 + side) * r, 8)
            out_ref[o * r : (o + 1) * r, :] = full_s[pl.ds(start, r), :].astype(bf16)


def parted(arrays, n, after):
    rows, width = arrays[0].shape[1], sum(v.shape[1] for v in arrays[2::4])
    r = rows // n
    if r % 16:
        kernel = functools.partial(products_kernel, len(arrays) // 4)
        full = call(kernel, shape((rows, width), bf16), (), arrays, after)
        view = full.reshape(n // 2, 2, r, width)
        inner = dp_bit(1)
        pieces = [lax.dynamic_index_in_dim(view, i, 1, False) for i in (1 - inner, inner)]
        return [v.reshape(rows // 2, width) for v in pieces]
    outs = (shape((rows // 2, width), bf16),) * 2
    scratch = [pltpu.VMEM((rows, width), f32)]
    return call(functools.partial(parted_kernel, r), outs, (), arrays, after, 24, scratch)


def backward_kernel(
    reach,
    lengths_ref,
    both_ref,
    other_ref,
    middle_ref,
    upstream_ref,
    vecs_ref,
    qk_ref,
    wv_ref,
    proj_ref,
    qkv_ref,
    lse_ref,
    grad_middle_ref,
    low_ref,
    mixed_ref,
    away_ref,
    keep_ref,
    sums_ref,
    heads_ref,
    q_s,
    k_s,
    v_s,
    g_s,
    dk_s,
    dv_s,
):
    rows, features = middle_ref.shape
    half = rows // 2
    width = qkv_ref.shape[1] // 3
    heads = range(width // HD)
    core = core_index()
    gain = vecs_ref[2:3, :]
    sums = []
    for piece_ref, base in ((both_ref, core * half), (other_ref, (1 - core) * half)):

        def rows_step(t, acc, piece_ref=piece_ref, base=base):
            off = pl.multiple_of(base + t * TILE, TILE)
            here = pl.ds(off, TILE)
            gnt = piece_ref[pl.ds(pl.multiple_of(t * TILE, TILE), TILE), :].astype(f32)
            xhat, scale = norm_parts(middle_ref[here, :])
            upstream = upstream_ref[here, :].astype(f32)
            grad_middle = upstream + norm_back(gnt * gain, xhat, scale)
            grad_middle_ref[here, :] = grad_middle
            low_ref[here, :] = grad_middle.astype(bf16)
            terms = (gnt * xhat, gnt, grad_middle, upstream)
            return tuple(a + rows_sum(v) for a, v in zip(acc, terms))

        start = (jnp.zeros((1, features), f32),) * 4
        sums.append(lax.fori_loop(0, half // TILE, rows_step, start))
    sums_ref[...] = jnp.concatenate([a + b for a, b in zip(*sums)], axis=0)
    for start in range(0, rows, BLOCK):
        piece = slice(start, start + BLOCK)
        split_heads(qkv_ref[piece, :], piece, q_s, k_s, v_s)
        grad_att = dot(low_ref[piece, :], proj_ref[...], NN).astype(bf16)
        for h in heads:
            g_s[h, piece, :] = grad_att[:, h * HD : (h + 1) * HD]
    dk_s[...] = jnp.zeros_like(dk_s)
    dv_s[...] = jnp.zeros_like(dv_s)
    for start, low, high in windows(rows, reach):
        tile = slice(start, start + TILE)
        keys = slice(low, high)
        allowed = same_segment(lengths_ref, start, low, high)
        scores = [dot(q_s[h, tile, :], k_s[h, keys, :], NT) for h in heads]
        grad_probs = [dot(g_s[h, tile, :], v_s[h, keys, :], NT) for h in heads]
        probs = [jnp.exp(jnp.where(allowed, s, masked_score) - lse_ref[tile, h : h + 1]) for h, s in enumerate(scores)]
        inner = [jnp.sum(p * g, axis=-1, keepdims=True) for p, g in zip(probs, grad_probs)]
        grads = [(p * (g - i)).astype(bf16) for p, g, i in zip(probs, grad_probs, inner)]
        lows = [p.astype(bf16) for p in probs]
        dqs = [(dot(g, k_s[h, keys, :], NN) * HD**-0.5).astype(bf16) for h, g in enumerate(grads)]
        mixed_ref[tile, :width] = jnp.concatenate(dqs, axis=1)
        dks = [dot(g, q_s[h, tile, :], TN) for h, g in enumerate(grads)]
        dvs = [dot(p, g_s[h, tile, :], TN) for h, p in enumerate(lows)]
        for h in heads:
            dk_s[h, keys, :] += dks[h]
            dv_s[h, keys, :] += dvs[h]
    for start in range(0, rows, BLOCK):
        piece = slice(start, start + BLOCK)
        both = [ref[h, piece, :].astype(bf16) for ref in (dk_s, dv_s) for h in heads]
        mixed_ref[piece, width:] = jnp.concatenate(both, axis=1)
    heads_ref[...] = rows_sum(mixed_ref[...].astype(f32))
    for out_ref, base in ((away_ref, (1 - core) * half), (keep_ref, core * half)):
        here = pl.ds(pl.multiple_of(base, half), half)
        part = dot(mixed_ref[here, : 2 * width], qk_ref[...], NT)
        part = part + dot(mixed_ref[here, 2 * width :], wv_ref[...], NT)
        out_ref[...] = part.astype(out_ref.dtype)


def input_grad_kernel(both_ref, other_ref, stream_ref, middle_ref, vecs_ref, *refs):
    out_ref, sums_ref = refs[-2:]
    rows, features = stream_ref.shape
    half = rows // 2
    core = core_index()
    gain = vecs_ref[0:1, :]
    sums = []
    for piece_ref, base in ((both_ref, core * half), (other_ref, (1 - core) * half)):

        def rows_step(t, acc, piece_ref=piece_ref, base=base):
            here = pl.ds(pl.multiple_of(base + t * TILE, TILE), TILE)
            grad = piece_ref[pl.ds(pl.multiple_of(t * TILE, TILE), TILE), :].astype(f32)
            xhat, scale = norm_parts(stream_ref[here, :])
            out_ref[0, here, :] = middle_ref[here, :] + norm_back(grad * gain, xhat, scale)
            return (acc[0] + rows_sum(grad * xhat), acc[1] + rows_sum(grad))

        start = (jnp.zeros((1, features), f32),) * 2
        sums.append(lax.fori_loop(0, half // TILE, rows_step, start))
    sums_ref[...] = jnp.concatenate([a + b for a, b in zip(*sums)], axis=0)


def input_grad_call(which, both, other, stream, middle, vecs, filled, after):
    rows, features = stream.shape
    count = len(after)

    def kernel(*refs):
        input_grad_kernel(*refs[count:])

    whole = pl.BlockSpec(memory_space=pltpu.VMEM)
    anywhere = pl.BlockSpec(memory_space=pl.ANY)
    return pl.pallas_call(
        kernel,
        grid=(1,),
        out_shape=(shape((2, rows, features), f32), shape((2, features), f32)),
        in_specs=[anywhere] * count + [whole] * 5 + [anywhere] * len(filled),
        out_specs=(pl.BlockSpec((1, rows, features), lambda i: (which, 0, 0)), whole),
        input_output_aliases={count + 5: 0} if filled else {},
        compiler_params=pltpu.CompilerParams(vmem_limit_bytes=24 * 2**20),
        cost_estimate=cost(),
    )(*after, both, other, stream, middle, vecs, *filled)


def output_kernel(lengths_ref, both_ref, other_ref, middle_ref, vecs_ref, branch_ref, *refs):
    out_ref, sums_ref = refs[-2:]
    rows, features = middle_ref.shape
    half = rows // 2
    core = core_index()
    total = valid_count(lengths_ref)
    sums = []
    for piece_ref, base in ((both_ref, core * half), (other_ref, (1 - core) * half)):

        def rows_step(t, acc, piece_ref=piece_ref, base=base):
            off = pl.multiple_of(base + t * TILE, TILE)
            here = pl.ds(off, TILE)
            two = piece_ref[pl.ds(pl.multiple_of(t * TILE, TILE), TILE), :].astype(f32) + vecs_ref[5:6, :]
            whole = middle_ref[here, :] + two
            out_ref[0, here, :] = whole.astype(bf16)
            valid = off + lax.broadcasted_iota(jnp.int32, (TILE, 1), 0) < total
            terms = [jnp.where(valid, v, 0.0) for v in (whole, two)]
            return tuple(a + rows_sum(v * v) for a, v in zip(acc, terms))

        start = (jnp.zeros((1, features), f32),) * 2
        sums.append(lax.fori_loop(0, half // TILE, rows_step, start))
    whole, two = (a + b for a, b in zip(*sums))
    lines = [jnp.sum(v, axis=1, keepdims=True) for v in (whole, branch_ref[...], two)]
    lines.append(jnp.full((1, 1), total.astype(f32), f32))
    for i in range(8):
        line = jnp.broadcast_to(lines[min(i, 3)], (1, 128))
        for ref in refs[:-2][1:]:
            line = line + ref[i : i + 1, :]
        sums_ref[i : i + 1, :] = line


def output_call(which, lengths, both, other, middle, vecs, branch, filled, after):
    rows, features = middle.shape
    count = len(after)

    def kernel(lengths_ref, *refs):
        output_kernel(lengths_ref, *refs[count:])

    whole = pl.BlockSpec(memory_space=pltpu.VMEM)
    anywhere = pl.BlockSpec(memory_space=pl.ANY)
    more = [anywhere, whole] if filled else []
    return pl.pallas_call(
        kernel,
        grid=(1,),
        out_shape=(shape((2, rows, features), bf16), shape((8, 128), f32)),
        in_specs=[pl.BlockSpec(memory_space=pltpu.SMEM)] + [anywhere] * count + [whole] * 5 + more,
        out_specs=(pl.BlockSpec((1, rows, features), lambda i: (which, 0, 0)), whole),
        input_output_aliases={1 + count + 5: 0} if filled else {},
        compiler_params=pltpu.CompilerParams(vmem_limit_bytes=16 * 2**20),
        cost_estimate=cost(),
        name="output_kernel",
    )(lengths, *after, both, other, middle, vecs, branch, *filled)


def message_kernel(norm_one, norm_two, sums_one, sums_two, off_one, off_two, heads_one, heads_two, out_ref):
    width = heads_one.shape[1] // 3
    out_ref[...] = jnp.zeros_like(out_ref)
    out_ref[0:2, :] = norm_one[...] + norm_two[...]
    out_ref[2:6, :] = sums_one[...] + sums_two[...]
    out_ref[6:7, :] = off_one[...] + off_two[...]
    heads = heads_one[...] + heads_two[...]
    out_ref[8:9, :width] = heads[:, :width]
    out_ref[9:10, :width] = heads[:, 2 * width :]


def shards_kernel(*refs):
    *pairs, grads_ref, out_ref = refs
    column = 0
    squares = jnp.zeros((1, 1), f32)
    for keep_ref, moved_ref in zip(pairs[::2], pairs[1::2]):
        grad = keep_ref[...].astype(f32) + moved_ref[...].astype(f32)
        stop = column + grad.shape[1]
        grads_ref[:, column:stop] = grad
        squares = squares + whole_sum(grad * grad)
        column = stop
    out_ref[...] = jnp.broadcast_to(squares, out_ref.shape)


def partial_kernel(message_ref, out_ref):
    squares = whole_sum(message_ref[8:10, :] * message_ref[8:10, :])
    squares = squares + whole_sum(message_ref[6:7, :] * message_ref[6:7, :])
    out_ref[...] = jnp.broadcast_to(squares, out_ref.shape)


def rms_kernel(features, sums_ref, out_ref):
    values = jnp.sqrt(sums_ref[...] / (sums_ref[3:4, :] * features))
    for i in range(3):
        out_ref[i] = jnp.max(values[i : i + 1, :])


def rms_call(sums, features):
    return pl.pallas_call(
        functools.partial(rms_kernel, features),
        out_shape=shape((3,), f32),
        in_specs=[pl.BlockSpec(memory_space=pltpu.VMEM)],
        out_specs=pl.BlockSpec(memory_space=pltpu.SMEM),
        compiler_params=pltpu.CompilerParams(vmem_limit_bytes=8 * 2**20),
        cost_estimate=cost(),
        name="rms_kernel",
    )(sums)


def adamw_kernel(partial_ref, moved_ref, message_ref, grads_ref, *refs):
    count = 21
    inputs, targets, norm_ref = refs[:count], refs[count : 2 * count], refs[2 * count]
    outputs, write_sems = refs[2 * count + 1 : 3 * count + 1], refs[3 * count + 1]
    writes = [pltpu.make_async_copy(outputs[i], targets[i], write_sems.at[i]) for i in range(count)]
    width = inputs[0].shape[2]
    hidden = inputs[6].shape[1]
    vecs = message_ref[0:6, :]
    norm = jnp.sqrt(partial_ref[0:1, 0:1] + moved_ref[0:1, 0:1] + whole_sum(vecs * vecs))
    norm_ref[0] = jnp.max(norm)
    clip = jnp.minimum(1.0, clip_limit / (norm + 1e-06))

    def step(p, gradient, at=Ellipsis):
        weight, moment, square = (ref[at] for ref in inputs[3 * p : 3 * p + 3])
        decay = matrix_decay if p < 4 else 0.0
        factor = clip if gradient.ndim == 2 else jnp.max(clip)
        values = adamw_step(weight, moment, square, gradient, step_rates[p], decay, factor)
        for ref, value in zip(outputs[3 * p : 3 * p + 3], values):
            ref[at] = value

    start = 4 * width
    parts = (
        tuple((grads_ref[:, j * width : (j + 1) * width], j) for j in range(3)),
        ((grads_ref[:, 3 * width : start].T,),),
        ((grads_ref[:, start : start + hidden],),),
        ((grads_ref[:, start + hidden :],),),
        ((vecs,),),
        ((message_ref[8:10, : inputs[15].shape[1]],),),
        ((message_ref[6, :],),),
    )
    for p, steps in enumerate(parts):
        for arguments in steps:
            step(p, *arguments)
        for copy in writes[3 * p : 3 * p + 3]:
            copy.start()
    for copy in writes:
        copy.wait()


def adamw_call(partial, moved, message, grads, state, after):
    in_vmem = pl.BlockSpec(memory_space=pltpu.VMEM)
    anywhere = pl.BlockSpec(memory_space=pltpu.MemorySpace.HBM)
    count = len(state)

    def kernel(*refs):
        adamw_kernel(*refs[len(after) :])

    return pl.pallas_call(
        kernel,
        out_shape=tuple(shape(v.shape, f32) for v in state) + (shape((1,), f32),),
        in_specs=[pl.BlockSpec(memory_space=pl.ANY)] * len(after) + [in_vmem] * (4 + count),
        out_specs=(anywhere,) * count + (pl.BlockSpec(memory_space=pltpu.SMEM),),
        scratch_shapes=[pltpu.VMEM(v.shape, f32) for v in state] + [pltpu.SemaphoreType.DMA((count,))],
        compiler_params=pltpu.CompilerParams(vmem_limit_bytes=24 * 2**20),
        cost_estimate=cost(),
        name="adamw_kernel",
    )(*after, partial, moved, message, grads, *state)


def build(n):
    top = n // 2

    def local(
        inputs,
        time_first,
        time_second,
        lengths_first,
        lengths_second,
        cotangent,
        w_qkv,
        m_qkv,
        v_qkv,
        w_proj,
        m_proj,
        v_proj,
        w_up,
        m_up,
        v_up,
        w_down,
        m_down,
        v_down,
        w_vecs,
        m_vecs,
        v_vecs,
        b_heads,
        m_heads,
        v_heads,
        b_hidden,
        m_hidden,
        v_hidden,
    ):
        rows, features = inputs.shape[1], inputs.shape[2]
        r, _, width = w_qkv.shape
        hidden = w_up.shape[1]
        heads = width // HD
        half = rows // 2
        lengths = (lengths_first, lengths_second)
        whole_f = shape((rows, features), f32)
        whole_b = shape((rows, features), bf16)
        hidden_b = shape((rows, hidden), bf16)
        half_b = shape((half, features), bf16)
        half_f = shape((half, features), f32)
        line = shape((1, features), f32)

        def swap(v, bit):
            return swap_bit(v, "dp", n, bit)

        def gathered(shard, bit, stop, after=()):
            while bit > stop:
                (shard,) = merged(shard, swap(shard, bit), r, bit, after)
                after = ()
                bit //= 2
            return shard

        qk, vp = call(
            pack_kernel, (shape((r, 2 * width), bf16),) * 2, (), (w_qkv.transpose(1, 0, 2), w_proj), (), 8
        )
        times = [jnp.pad(t[0], ((0, 16 - t.shape[1]), (0, 0))) for t in (time_first, time_second)]
        stream_one, normed_one, stream_two, normed_two = call(
            first_norm_kernel, (whole_f, whole_b) * 2, lengths, (inputs, *times, w_vecs), (qk,), 24
        )
        stream, normed = (stream_one, stream_two), (normed_one, normed_two)
        qk = gathered(qk, top, top // 2, (normed_two,))
        vp = gathered(vp, top, top // 2, (qk,))
        qk = gathered(qk, top // 2, 1, (vp,))
        (up,) = call(cast_kernel, (shape((r, hidden), bf16),), (), (w_up,), (qk,), 8)
        vp = gathered(vp, top // 2, 1, (up,))
        (qk,) = merged(qk, swap(qk, 1), r, 1, (vp,))
        (down,) = call(cast_kernel, (shape((r, hidden), bf16),), (), (w_down.T,), (qk,), 8)
        up = gathered(up, top, top // 2, (down,))
        wv, proj = merged(vp, swap(vp, 1), r, 1, (up,), (width, width))

        def spread(v, after=()):
            moved = over_chip(v)
            pair = call(pair_kernel, shape((rows, 2 * v.shape[1]), bf16), (), (v, moved), after, 8)
            return [pair, over_core(pair)]

        bias = jnp.concatenate([b_heads[0], jnp.zeros_like(b_heads[0]), b_heads[1]])[None]
        head_low = pltpu.VMEM((heads, rows, HD), bf16)
        head_full = pltpu.VMEM((heads, rows, HD), f32)
        after = (wv,)
        att, sent, qkv, lse = [], [], [], []
        for b in range(2):
            carried = (proj,) if b == 0 else ()
            a, q, l, *pair = call(
                functools.partial(forward_kernel, REACH[b], len(carried)),
                (
                    shape((rows, width), bf16),
                    shape((rows, 3 * width), bf16),
                    shape((rows, 128), f32),
                    *(shape((rows, 2 * width), bf16) for _ in carried),
                ),
                (lengths[b],),
                (normed[b], qk, wv, bias, *carried),
                after,
                12,
                [head_low] * 3,
            )
            att.append(a)
            sent.append(pair[0] if pair else a)
            qkv.append(q)
            lse.append(l)
            after = (l,)
            if b == 0:
                down = gathered(down, top, top // 2, after)
                up = gathered(up, top // 2, 1, (down,))
                down = gathered(down, top // 2, 1, (up,))
                after = (down,)
        att_first = spread(sent[0], after)
        (up,) = merged(up, swap(up, 1), r, 1, (att_first[0],), weight=4)
        after = (up,)

        names = [[] for _ in range(9)]
        att_own = []
        for b in range(2):
            outs = call(
                hidden_kernel,
                (whole_f, whole_b, hidden_b, shape((rows, hidden), f32), line),
                (lengths[b],),
                (*att_first, *att_own, stream[b], w_vecs, up, b_hidden[None]),
                after,
            )
            for kept, v in zip(names, outs):
                kept.append(v)
            after = (outs[-1],)
            if b == 0:
                att_own = spread(sent[1], after)
                upstream = call(upstream_kernel, (whole_b,) * 2, lengths, (cotangent,), (att_own[0],))
                after = (upstream[1],)
        (down,) = merged(down, swap(down, 1), r, 1, after)
        low, parts = [], [[], []]

        def down_part(b, side, after):
            out = (half_b, half_f)[side]
            part = call(functools.partial(down_kernel, side), out, (), (active[b], down), after)
            parts[b].append(part)
            return part

        after = (down,)
        for b in range(2):
            outs = call(
                hidden_back_kernel,
                (hidden_b, half_b, half_f, shape((1, hidden), f32)),
                (),
                (upstream[b], names[3][b], up, down),
                after,
            )
            for kept, v in zip(names[5:], outs):
                kept.append(v)
            middle, normed_mid, active, slope, branch_square, grad_hidden, away, keep, offsets = names
            if b == 0:
                after = (down_part(0, 0, (outs[-1],)),)
            else:
                bulk = parted((*normed_mid, *grad_hidden, *upstream, *active), n, (outs[-1],))
                bulk_moved = swap(bulk[0], 1)
                after = (bulk[0],)
            low.append(add(keep[b], over_core(away[b]), after))
            after = (low[b],)
        both = add(low[0], over_chip(low[0]), after)
        gnt = [(both, over_core(both))]
        after = (down_part(0, 1, (both,)),)

        grad_middle, middle_low, grad_mixed, sums, head_sums, back_low = [], [], [], [], [], []
        for b in range(2):
            outs = call(
                functools.partial(backward_kernel, REACH[b]),
                (
                    whole_f,
                    whole_b,
                    shape((rows, 3 * width), bf16),
                    half_b,
                    half_f,
                    shape((4, features), f32),
                    shape((1, 3 * width), f32),
                ),
                (lengths[b],),
                (*gnt[b], middle[b], upstream[b], w_vecs, qk, wv, proj, qkv[b], lse[b]),
                after,
                24,
                [head_low] * 4 + [head_full] * 2,
            )
            grad_middle.append(outs[0])
            middle_low.append(outs[1])
            grad_mixed.append(outs[2])
            sums.append(outs[5])
            head_sums.append(outs[6])
            after = (outs[6],)
            if b == 0:
                both = add(low[1], over_chip(low[1]), after)
                gnt.append((both, over_core(both)))
                after = (down_part(1, 0, (both,)),)
            else:
                bulk = split(bulk[1], bulk_moved, r, 2, after)
                bulk_moved = swap(bulk[0], 2)
                after = (down_part(1, 1, (bulk[0],)),)
            back_low.append(add(outs[4], over_core(outs[3]), after))
            after = (back_low[b],)

        chunk = parted((*normed, *grad_mixed, *middle_low, *att), n, after)
        chunks = [[*chunk, swap(chunk[0], 1)]]
        after = (chunk[0],)

        def halved(chunk, bit, after):
            away, kept = split(chunk[1], chunk[2], r, bit, after)
            return [away, kept, swap(away, bit)]

        both = add(back_low[0], over_chip(back_low[0]), after)
        piece = (both, over_core(both))
        part = [add(parts[0][1], over_core(parts[0][0]), (both,))]
        after = (part[0],)
        bulk = [*bulk, bulk_moved]
        bit = 4
        while bit < n:
            bulk = halved(bulk, bit, after)
            after = (bulk[0],)
            bit *= 2
        input_grad, pair = input_grad_call(0, *piece, stream[0], grad_middle[0], w_vecs, (), after)
        norm_sums = [pair]
        after = (pair,)
        for i in range(len(chunks)):
            chunks[i] = halved(chunks[i], 2, after)
            after = (chunks[i][0],)
        both = add(back_low[1], over_chip(back_low[1]), after)
        piece = (both, over_core(both))
        part.append(add(parts[1][1], over_core(parts[1][0]), (both,)))
        input_grad, pair = input_grad_call(
            1, *piece, stream[1], grad_middle[1], w_vecs, (input_grad,), (part[1],)
        )
        norm_sums.append(pair)

        def hop(v, moved, after=(), more=()):
            return call(sum_kernel, shape(v.shape, f32), (), (v, moved, *more), after, 8)

        message = call(
            message_kernel, shape((16, features), f32), (), (*norm_sums, *sums, *offsets, *head_sums), (), 8
        )
        after = (message,)
        bit = 4
        while bit < n:
            for i in range(len(chunks)):
                chunks[i] = halved(chunks[i], bit, after)
                after = (chunks[i][0],)
            bit *= 2
        message = hop(message, swap(message, 1), after)
        both = add(part[0], over_chip(part[0]), (message,))
        two = (both, over_core(both))
        message = hop(message, swap(message, 2), (both,))
        filled = output_call(0, lengths[0], *two, middle[0], w_vecs, branch_square[0], (), (message,))
        grads, squares = call(
            shards_kernel,
            (shape((r, 4 * width + 2 * hidden), f32), shape((8, 128), f32)),
            (),
            tuple(v for chunk in (*chunks, bulk) for v in chunk[1:]),
            (filled[1],),
        )
        after = (squares,)
        bit = 4
        while bit < n:
            message = hop(message, swap(message, bit), after)
            after = ()
            bit *= 2
        partial = call(partial_kernel, shape((8, 128), f32), (), (message,), (), 8)
        both = add(part[1], over_chip(part[1]), (partial,))
        two = (both, over_core(both))
        squares = hop(squares, swap(squares, 1), (both,))
        block_out, out_sums = output_call(
            1, lengths[1], *two, middle[1], w_vecs, branch_square[1], tuple(filled), (squares,)
        )
        after = (out_sums,)
        bit = 2
        while bit < n:
            more = (partial,) if 2 * bit == n else ()
            squares = hop(squares, swap(squares, bit), after, more)
            after = ()
            bit *= 2
        out_sums = hop(out_sums, swap(out_sums, 1), (squares,))
        partial = hop(squares, over_core(squares), (out_sums,))
        out_sums = hop(out_sums, swap(out_sums, 2), (partial,))
        bit = 4
        last = out_sums
        state = (
            *(v.transpose(1, 0, 2) for v in (w_qkv, m_qkv, v_qkv)),
            *(w_proj, m_proj, v_proj),
            *(w_up, m_up, v_up),
            *(v.T for v in (w_down, m_down, v_down)),
            *(w_vecs, m_vecs, v_vecs),
            *(b_heads, m_heads, v_heads),
            *(b_hidden, m_hidden, v_hidden),
        )
        *updated, grad_norm = adamw_call(partial, over_chip(partial), message, grads, state, (last,))
        while bit < n:
            out_sums = hop(out_sums, swap(out_sums, bit), (grad_norm,))
            bit *= 2
        stream_rms = rms_call(out_sums, features)
        return (
            block_out,
            input_grad,
            grad_norm,
            stream_rms,
            *(v.transpose(1, 0, 2) for v in updated[:3]),
            *updated[3:9],
            *(v.T for v in updated[9:12]),
            *updated[12:18],
            *updated[18:],
        )

    return local


def solution(mesh):
    rows = P(None, "dp", None)
    group = P("dp", None, None)
    qkv, proj, up = P("dp", None, "tensor"), P("tensor", "dp"), P("dp", "tensor")
    params = [qkv] * 3 + [proj] * 3 + [up] * 3 + [proj] * 3 + [P()] * 3
    params += [P(None, "tensor")] * 3 + [P("tensor")] * 3
    return jax.shard_map(
        build(mesh.shape["dp"]),
        mesh=mesh,
        in_specs=(rows, group, group, P("dp", None), P("dp", None), rows, *params),
        out_specs=(rows, rows, P(), P(), *params),
        check_vma=False,
    )
```

```python
import functools

import jax
import jax.numpy as jnp
from jax import lax
from jax.experimental import pallas as pl
from jax.experimental.pallas import tpu as pltpu
from jax.sharding import PartitionSpec as P

HD = 64
STEP = 5
TILE = 128
BLOCK = 256
CHUNK = 384
REACH = (64, 128)

norm_eps = 1e-05
clip_limit = 1.0
beta_first = 0.5
beta_second = 0.5
adam_eps = 1e-08
matrix_decay = 0.01
masked_score = -1e30
step_rates = (0.03, 0.2, 0.03, 0.015, 0.3, 0.3, 0.3)
bf16 = jnp.bfloat16
f32 = jnp.float32

KERNEL_FLOPS = 7 * 10**9

NN = ((1,), (0,))
NT = ((1,), (1,))
TN = ((0,), (0,))


def dot(a, b, dims):
    return lax.dot_general(a, b, (dims, ((), ())), preferred_element_type=f32)


def shape(dims, dtype):
    return jax.ShapeDtypeStruct(dims, dtype)


def cost(weight=1):
    return pl.CostEstimate(flops=weight * KERNEL_FLOPS, bytes_accessed=0, transcendentals=0)


def call(body, outs, words, arrays, after=(), limit=16, scratch=(), weight=1):
    count = len(after)

    def kernel(*refs):
        body(*refs[: len(words)], *refs[len(words) + count :])

    in_vmem = pl.BlockSpec(memory_space=pltpu.VMEM)
    in_specs = [pl.BlockSpec(memory_space=pltpu.SMEM)] * len(words)
    in_specs += [pl.BlockSpec(memory_space=pl.ANY)] * count + [in_vmem] * len(arrays)
    return pl.pallas_call(
        kernel,
        out_shape=outs,
        in_specs=in_specs,
        out_specs=(in_vmem,) * len(outs) if isinstance(outs, tuple) else in_vmem,
        scratch_shapes=list(scratch),
        compiler_params=pltpu.CompilerParams(vmem_limit_bytes=limit * 2**20),
        cost_estimate=cost(weight),
        name=getattr(body, "func", body).__name__,
    )(*words, *after, *arrays)


def core_index():
    return lax.rem(lax.axis_index("tensor"), 2)


def dp_bit(bit):
    return lax.rem(lax.div(lax.axis_index("dp"), bit), 2)


def rows_sum(v):
    return jnp.sum(v, axis=0, keepdims=True)


def whole_sum(v):
    return jnp.sum(rows_sum(v), axis=1, keepdims=True)


def norm_parts(stream):
    center = stream - jnp.mean(stream, axis=-1, keepdims=True)
    spread = jnp.mean(center * center, axis=-1, keepdims=True)
    scale = lax.rsqrt(spread + norm_eps)
    return center * scale, scale


def norm_back(scaled, xhat, scale):
    mean = jnp.mean(scaled, axis=-1, keepdims=True)
    return scale * (scaled - mean - xhat * jnp.mean(scaled * xhat, axis=-1, keepdims=True))


def adamw_step(weight, moment_old, square_old, gradient, step_rate, decay_value, clip_factor):
    correct_one = 1.0 - beta_first**STEP
    correct_two = 1.0 - beta_second**STEP
    clipped = gradient * clip_factor
    moment_new = beta_first * moment_old + (1.0 - beta_first) * clipped
    square_new = beta_second * square_old + (1.0 - beta_second) * clipped * clipped
    divisor = jnp.sqrt(square_new / correct_two) + adam_eps
    weight_new = weight - step_rate * (moment_new / correct_one / divisor + decay_value * weight)
    return (weight_new, moment_new, square_new)


def swap_bit(v, axis, size, bit):
    return lax.ppermute(v, axis, [(i, i ^ bit) for i in range(size)])


def over_core(v):
    return swap_bit(v, "tensor", 4, 1)


def over_chip(v):
    return swap_bit(v, "tensor", 4, 2)


def merge_kernel(r, bit, own_ref, other_ref, *out_refs):
    mine = dp_bit(bit)
    for g in range(own_ref.shape[0] // r):
        for ref, side in ((own_ref, mine), (other_ref, 1 - mine)):
            start = pl.multiple_of((2 * g + side) * r, 16)
            column = 0
            for out_ref in out_refs:
                stop = column + out_ref.shape[1]
                out_ref[pl.ds(start, r), :] = ref[g * r : (g + 1) * r, column:stop]
                column = stop


def merged(own, other, r, bit, after=(), widths=None, weight=1):
    rows, width = own.shape
    widths = widths or (width,)
    if r % 16:
        own, other = (v.reshape(rows // r, r, width) for v in (own, other))
        sides = [jnp.where(dp_bit(bit) == 0, own, other), jnp.where(dp_bit(bit) == 0, other, own)]
        both = jnp.stack(sides, axis=1).reshape(2 * rows, width)
        return tuple(jnp.split(both, [sum(widths[:i]) for i in range(1, len(widths))], axis=1))
    outs = tuple(shape((2 * rows, w), bf16) for w in widths)
    return call(functools.partial(merge_kernel, r, bit), outs, (), (own, other), after, 8, weight=weight)


def split_kernel(r, bit, keep_ref, moved_ref, away_ref, own_ref):
    mine = dp_bit(bit)
    for g in range(away_ref.shape[0] // r):
        for out_ref, side in ((away_ref, 1 - mine), (own_ref, mine)):
            here = pl.ds(pl.multiple_of((2 * g + side) * r, 16), r)
            total = keep_ref[here, :].astype(f32) + moved_ref[here, :].astype(f32)
            out_ref[g * r : (g + 1) * r, :] = total.astype(out_ref.dtype)


def split(keep, moved, r, bit, after=()):
    half, width = keep.shape[0] // 2, keep.shape[1]
    if r % 16:
        total = (keep.astype(f32) + moved.astype(f32)).reshape(half // r, 2, r, width)
        pieces = [lax.dynamic_index_in_dim(total, i, 1, False) for i in (1 - dp_bit(bit), dp_bit(bit))]
        away, own = (v.reshape(half, width) for v in pieces)
        return away.astype(bf16), own
    outs = (shape((half, width), bf16), shape((half, width), f32))
    return call(functools.partial(split_kernel, r, bit), outs, (), (keep, moved), after, 8)


def sum_kernel(own_ref, moved_ref, *refs):
    *more_refs, out_ref = refs
    total = own_ref[...] + moved_ref[...]
    for ref in more_refs:
        total = total + ref[...]
    out_ref[...] = total


def add_kernel(keep_ref, moved_ref, out_ref):
    out_ref[...] = (keep_ref[...].astype(f32) + moved_ref[...].astype(f32)).astype(bf16)


def add(keep, moved, after=()):
    return call(add_kernel, shape(keep.shape, bf16), (), (keep, moved), after, 8)


def pack_kernel(qkv_ref, proj_ref, qk_ref, vp_ref):
    qk_ref[...] = jnp.concatenate([qkv_ref[0], qkv_ref[1]], axis=1).astype(bf16)
    vp_ref[...] = jnp.concatenate([qkv_ref[2], proj_ref[...].T], axis=1).astype(bf16)


def pair_kernel(left_ref, right_ref, out_ref):
    width = left_ref.shape[1]
    out_ref[:, :width] = left_ref[...]
    out_ref[:, width:] = right_ref[...]


def upstream_kernel(lengths_one, lengths_two, cot_ref, *out_refs):
    rows = cot_ref.shape[1]
    for b, (lengths_ref, out_ref) in enumerate(zip((lengths_one, lengths_two), out_refs)):
        valid = lax.broadcasted_iota(jnp.int32, (rows, 1), 0) < valid_count(lengths_ref)
        out_ref[...] = jnp.where(valid, cot_ref[b].astype(f32), 0.0).astype(bf16)


def cast_kernel(*refs):
    half = len(refs) // 2
    for source, out in zip(refs[:half], refs[half:]):
        out[...] = source[...].astype(bf16)


def segment_grid(lengths_ref, dims, axis, first=0):
    places = first + lax.broadcasted_iota(jnp.int32, dims, axis)
    ids = jnp.zeros(dims, jnp.int32)
    bound = jnp.int32(0)
    for k in range(lengths_ref.shape[1]):
        bound = bound + lengths_ref[0, k]
        ids = ids + (places >= bound).astype(jnp.int32)
    return ids


def same_segment(lengths_ref, start, low, high):
    queries = segment_grid(lengths_ref, (TILE, 1), 0, start)
    return queries == segment_grid(lengths_ref, (1, high - low), 1, low)


def valid_count(lengths_ref):
    total = jnp.int32(0)
    for k in range(lengths_ref.shape[1]):
        total = total + lengths_ref[0, k]
    return total


def first_norm_kernel(lengths_one, lengths_two, inputs_ref, times_one, times_two, vecs_ref, *refs):
    rows = inputs_ref.shape[1]
    for b, (lengths_ref, times_ref) in enumerate(((lengths_one, times_one), (lengths_two, times_two))):
        stream_ref, normed_ref = refs[2 * b : 2 * b + 2]
        depth = times_ref.shape[0]
        ids = segment_grid(lengths_ref, (rows, 1), 0)
        for start in range(0, rows, BLOCK):
            here = slice(start, start + BLOCK)
            lanes = lax.broadcasted_iota(jnp.int32, (BLOCK, depth), 1)
            pick = (ids[here] == lanes).astype(f32).astype(bf16)
            stream = inputs_ref[b, here, :].astype(f32) + dot(pick, times_ref[...], NN)
            stream_ref[here, :] = stream
            xhat, _ = norm_parts(stream)
            normed_ref[here, :] = (xhat * vecs_ref[0:1, :] + vecs_ref[1:2, :]).astype(bf16)


def windows(rows, reach):
    size = min(rows, TILE + 2 * reach)
    out = []
    for start in range(0, rows, TILE):
        low = max(0, start - reach)
        high = min(rows, start + TILE + reach)
        if (high - low) % 128:
            low = min(low, rows - size)
            high = low + size
        out.append((start, low, high))
    return out


def split_heads(low, rows, q_s, k_s, v_s):
    heads = q_s.shape[0]
    width = heads * HD
    for h in range(heads):
        cut = h * HD
        q_s[h, rows, :] = low[:, cut : cut + HD] * jnp.array(HD**-0.5, bf16)
        k_s[h, rows, :] = low[:, width + cut : width + cut + HD]
        v_s[h, rows, :] = low[:, 2 * width + cut : 2 * width + cut + HD]


def forward_kernel(reach, carried, lengths_ref, normed_ref, qk_ref, wv_ref, bias_ref, *refs):
    att_ref, qkv_ref, lse_ref, *pair_refs, q_s, k_s, v_s = refs[carried:]
    rows, width = att_ref.shape
    heads = range(width // HD)
    for start in range(0, rows, BLOCK):
        piece = slice(start, start + BLOCK)
        normed = normed_ref[piece, :]
        pair = dot(normed, qk_ref[...], NN)
        values = dot(normed, wv_ref[...], NN)
        low = (jnp.concatenate([pair, values], axis=1) + bias_ref[...]).astype(bf16)
        qkv_ref[piece, :] = low
        split_heads(low, piece, q_s, k_s, v_s)
    lanes = lax.broadcasted_iota(jnp.int32, (TILE, 128), 1)
    for start, low, high in windows(rows, reach):
        tile = slice(start, start + TILE)
        allowed = same_segment(lengths_ref, start, low, high)
        scores = [dot(q_s[h, tile, :], k_s[h, low:high, :], NT) for h in heads]
        scores = [jnp.where(allowed, s, masked_score) for s in scores]
        peaks = [jnp.max(s, axis=-1, keepdims=True) for s in scores]
        exponents = [jnp.exp(s - p) for s, p in zip(scores, peaks)]
        totals = [jnp.sum(e, axis=-1, keepdims=True) for e in exponents]
        probs = [(e * (1.0 / t)).astype(bf16) for e, t in zip(exponents, totals)]
        outs = [dot(p, v_s[h, low:high, :], NN).astype(bf16) for h, p in enumerate(probs)]
        att_ref[tile, :] = jnp.concatenate(outs, axis=1)
        logs = jnp.zeros((TILE, 128), f32)
        for h in heads:
            logs = jnp.where(lanes == h, peaks[h] + jnp.log(totals[h]), logs)
        lse_ref[tile, :] = logs
    for ref, pair_ref in zip(refs[:carried], pair_refs):
        pair_ref[...] = jnp.concatenate([att_ref[...], ref[...]], axis=1)


def hidden_kernel(lengths_ref, *refs):
    first_refs, att_refs = refs[:2], refs[-11:-9]
    stream_ref, vecs_ref, up_ref, bias_ref = refs[-9:-5]
    middle_ref, normed_ref, active_ref, slope_ref, square_ref = refs[-5:]
    rows, features = stream_ref.shape
    width = first_refs[0].shape[1] // 4
    step = att_refs[0].shape[1] // 2
    total = valid_count(lengths_ref)
    squares = jnp.zeros((1, features), f32)
    for start in range(0, rows, CHUNK):
        here = slice(start, start + CHUNK)
        valid = start + lax.broadcasted_iota(jnp.int32, (CHUNK, 1), 0) < total
        own, over, near, across = (
            dot(a[here, k * step : k * step + width], p[:, (2 * k + 1) * width : (2 * k + 2) * width], NT)
            for a, p in zip(att_refs, first_refs)
            for k in range(2)
        )
        branch = ((own + near) + (over + across)) + vecs_ref[4:5, :]
        kept = jnp.where(valid, branch, 0.0)
        squares = squares + rows_sum(kept * kept)
        middle = stream_ref[here, :] + branch
        middle_ref[here, :] = middle
        xhat, _ = norm_parts(middle)
        normed = (xhat * vecs_ref[2:3, :] + vecs_ref[3:4, :]).astype(bf16)
        normed_ref[here, :] = normed
        hidden = dot(normed, up_ref[...], NN) + bias_ref[...]
        cdf = 0.5 + 0.5 * lax.erf(hidden * 0.5**0.5)
        pdf = jnp.exp(-0.5 * hidden * hidden) * 0.3989422804014327
        active_ref[here, :] = (hidden * cdf).astype(bf16)
        slope_ref[here, :] = cdf + hidden * pdf
    square_ref[...] = squares


def hidden_back_kernel(upstream_ref, slope_ref, up_ref, down_ref, grad_ref, away_ref, keep_ref, offset_ref):
    rows = upstream_ref.shape[0]
    half = rows // 2
    first = (1 - core_index()) * half

    def rows_step(t, offsets):
        here = pl.ds(pl.multiple_of(lax.rem(first + t * CHUNK, rows), CHUNK), CHUNK)
        grad = dot(upstream_ref[here, :], down_ref[...], NN) * slope_ref[here, :]
        low = grad.astype(bf16)
        grad_ref[here, :] = low
        part = dot(low, up_ref[...], NT)

        @pl.when(t * CHUNK < half)
        def _():
            away_ref[pl.ds(pl.multiple_of(t * CHUNK, CHUNK), CHUNK), :] = part.astype(bf16)

        @pl.when(t * CHUNK >= half)
        def _():
            keep_ref[pl.ds(pl.multiple_of(t * CHUNK - half, CHUNK), CHUNK), :] = part

        return offsets + rows_sum(grad)

    offset_ref[...] = lax.fori_loop(0, rows // CHUNK, rows_step, jnp.zeros(offset_ref.shape, f32))


def down_kernel(side, active_ref, down_ref, out_ref):
    half = active_ref.shape[0] // 2
    core = core_index()
    base = (core if side else 1 - core) * half
    here = pl.ds(pl.multiple_of(base, half), half)
    out_ref[...] = dot(active_ref[here, :], down_ref[...], NT).astype(out_ref.dtype)


def products_kernel(pairs, *refs):
    out_ref = refs[-1]
    for m in range(0, out_ref.shape[0], BLOCK):
        cut = slice(m, m + BLOCK)
        column = 0
        for p in range(pairs):
            left_one, left_two, right_one, right_two = refs[4 * p : 4 * p + 4]
            rows = left_one.shape[0]
            part = dot(left_one[:, cut], right_one[:rows, :], TN) + dot(left_two[:, cut], right_two[:rows, :], TN)
            out_ref[cut, column : column + part.shape[1]] = part.astype(out_ref.dtype)
            column += part.shape[1]


def parted_kernel(r, *refs):
    away_ref, keep_ref, full_s = refs[-3:]
    products_kernel(len(refs) // 4, *refs[:-3], full_s)
    inner = dp_bit(1)
    for o in range(away_ref.shape[0] // r):
        for out_ref, side in ((away_ref, 1 - inner), (keep_ref, inner)):
            start = pl.multiple_of((o * 2 + side) * r, 8)
            out_ref[o * r : (o + 1) * r, :] = full_s[pl.ds(start, r), :].astype(bf16)


def parted(arrays, n, after):
    rows, width = arrays[0].shape[1], sum(v.shape[1] for v in arrays[2::4])
    r = rows // n
    if r % 16:
        kernel = functools.partial(products_kernel, len(arrays) // 4)
        full = call(kernel, shape((rows, width), bf16), (), arrays, after)
        view = full.reshape(n // 2, 2, r, width)
        inner = dp_bit(1)
        pieces = [lax.dynamic_index_in_dim(view, i, 1, False) for i in (1 - inner, inner)]
        return [v.reshape(rows // 2, width) for v in pieces]
    outs = (shape((rows // 2, width), bf16),) * 2
    scratch = [pltpu.VMEM((rows, width), f32)]
    return call(functools.partial(parted_kernel, r), outs, (), arrays, after, 24, scratch)


def backward_kernel(
    reach,
    lengths_ref,
    both_ref,
    other_ref,
    middle_ref,
    upstream_ref,
    vecs_ref,
    qk_ref,
    wv_ref,
    proj_ref,
    qkv_ref,
    lse_ref,
    grad_middle_ref,
    low_ref,
    mixed_ref,
    away_ref,
    keep_ref,
    sums_ref,
    heads_ref,
    q_s,
    k_s,
    v_s,
    g_s,
    dk_s,
    dv_s,
):
    rows, features = middle_ref.shape
    half = rows // 2
    width = qkv_ref.shape[1] // 3
    heads = range(width // HD)
    core = core_index()
    gain = vecs_ref[2:3, :]
    sums = []
    for piece_ref, base in ((both_ref, core * half), (other_ref, (1 - core) * half)):

        def rows_step(t, acc, piece_ref=piece_ref, base=base):
            off = pl.multiple_of(base + t * TILE, TILE)
            here = pl.ds(off, TILE)
            gnt = piece_ref[pl.ds(pl.multiple_of(t * TILE, TILE), TILE), :].astype(f32)
            xhat, scale = norm_parts(middle_ref[here, :])
            upstream = upstream_ref[here, :].astype(f32)
            grad_middle = upstream + norm_back(gnt * gain, xhat, scale)
            grad_middle_ref[here, :] = grad_middle
            low_ref[here, :] = grad_middle.astype(bf16)
            terms = (gnt * xhat, gnt, grad_middle, upstream)
            return tuple(a + rows_sum(v) for a, v in zip(acc, terms))

        start = (jnp.zeros((1, features), f32),) * 4
        sums.append(lax.fori_loop(0, half // TILE, rows_step, start))
    sums_ref[...] = jnp.concatenate([a + b for a, b in zip(*sums)], axis=0)
    for start in range(0, rows, BLOCK):
        piece = slice(start, start + BLOCK)
        split_heads(qkv_ref[piece, :], piece, q_s, k_s, v_s)
        grad_att = dot(low_ref[piece, :], proj_ref[...], NN).astype(bf16)
        for h in heads:
            g_s[h, piece, :] = grad_att[:, h * HD : (h + 1) * HD]
    dk_s[...] = jnp.zeros_like(dk_s)
    dv_s[...] = jnp.zeros_like(dv_s)
    for start, low, high in windows(rows, reach):
        tile = slice(start, start + TILE)
        keys = slice(low, high)
        allowed = same_segment(lengths_ref, start, low, high)
        scores = [dot(q_s[h, tile, :], k_s[h, keys, :], NT) for h in heads]
        grad_probs = [dot(g_s[h, tile, :], v_s[h, keys, :], NT) for h in heads]
        probs = [jnp.exp(jnp.where(allowed, s, masked_score) - lse_ref[tile, h : h + 1]) for h, s in enumerate(scores)]
        inner = [jnp.sum(p * g, axis=-1, keepdims=True) for p, g in zip(probs, grad_probs)]
        grads = [(p * (g - i)).astype(bf16) for p, g, i in zip(probs, grad_probs, inner)]
        lows = [p.astype(bf16) for p in probs]
        dqs = [(dot(g, k_s[h, keys, :], NN) * HD**-0.5).astype(bf16) for h, g in enumerate(grads)]
        mixed_ref[tile, :width] = jnp.concatenate(dqs, axis=1)
        dks = [dot(g, q_s[h, tile, :], TN) for h, g in enumerate(grads)]
        dvs = [dot(p, g_s[h, tile, :], TN) for h, p in enumerate(lows)]
        for h in heads:
            dk_s[h, keys, :] += dks[h]
            dv_s[h, keys, :] += dvs[h]
    for start in range(0, rows, BLOCK):
        piece = slice(start, start + BLOCK)
        both = [ref[h, piece, :].astype(bf16) for ref in (dk_s, dv_s) for h in heads]
        mixed_ref[piece, width:] = jnp.concatenate(both, axis=1)
    heads_ref[...] = rows_sum(mixed_ref[...].astype(f32))
    for out_ref, base in ((away_ref, (1 - core) * half), (keep_ref, core * half)):
        here = pl.ds(pl.multiple_of(base, half), half)
        part = dot(mixed_ref[here, : 2 * width], qk_ref[...], NT)
        part = part + dot(mixed_ref[here, 2 * width :], wv_ref[...], NT)
        out_ref[...] = part.astype(out_ref.dtype)


def input_grad_kernel(both_ref, other_ref, stream_ref, middle_ref, vecs_ref, *refs):
    out_ref, sums_ref = refs[-2:]
    rows, features = stream_ref.shape
    half = rows // 2
    core = core_index()
    gain = vecs_ref[0:1, :]
    sums = []
    for piece_ref, base in ((both_ref, core * half), (other_ref, (1 - core) * half)):

        def rows_step(t, acc, piece_ref=piece_ref, base=base):
            here = pl.ds(pl.multiple_of(base + t * TILE, TILE), TILE)
            grad = piece_ref[pl.ds(pl.multiple_of(t * TILE, TILE), TILE), :].astype(f32)
            xhat, scale = norm_parts(stream_ref[here, :])
            out_ref[0, here, :] = middle_ref[here, :] + norm_back(grad * gain, xhat, scale)
            return (acc[0] + rows_sum(grad * xhat), acc[1] + rows_sum(grad))

        start = (jnp.zeros((1, features), f32),) * 2
        sums.append(lax.fori_loop(0, half // TILE, rows_step, start))
    sums_ref[...] = jnp.concatenate([a + b for a, b in zip(*sums)], axis=0)


def input_grad_call(which, both, other, stream, middle, vecs, filled, after):
    rows, features = stream.shape
    count = len(after)

    def kernel(*refs):
        input_grad_kernel(*refs[count:])

    whole = pl.BlockSpec(memory_space=pltpu.VMEM)
    anywhere = pl.BlockSpec(memory_space=pl.ANY)
    return pl.pallas_call(
        kernel,
        grid=(1,),
        out_shape=(shape((2, rows, features), f32), shape((2, features), f32)),
        in_specs=[anywhere] * count + [whole] * 5 + [anywhere] * len(filled),
        out_specs=(pl.BlockSpec((1, rows, features), lambda i: (which, 0, 0)), whole),
        input_output_aliases={count + 5: 0} if filled else {},
        compiler_params=pltpu.CompilerParams(vmem_limit_bytes=24 * 2**20),
        cost_estimate=cost(),
    )(*after, both, other, stream, middle, vecs, *filled)


def output_kernel(lengths_ref, both_ref, other_ref, middle_ref, vecs_ref, branch_ref, *refs):
    out_ref, sums_ref = refs[-2:]
    rows, features = middle_ref.shape
    half = rows // 2
    core = core_index()
    total = valid_count(lengths_ref)
    sums = []
    for piece_ref, base in ((both_ref, core * half), (other_ref, (1 - core) * half)):

        def rows_step(t, acc, piece_ref=piece_ref, base=base):
            off = pl.multiple_of(base + t * TILE, TILE)
            here = pl.ds(off, TILE)
            two = piece_ref[pl.ds(pl.multiple_of(t * TILE, TILE), TILE), :].astype(f32) + vecs_ref[5:6, :]
            whole = middle_ref[here, :] + two
            out_ref[0, here, :] = whole.astype(bf16)
            valid = off + lax.broadcasted_iota(jnp.int32, (TILE, 1), 0) < total
            terms = [jnp.where(valid, v, 0.0) for v in (whole, two)]
            return tuple(a + rows_sum(v * v) for a, v in zip(acc, terms))

        start = (jnp.zeros((1, features), f32),) * 2
        sums.append(lax.fori_loop(0, half // TILE, rows_step, start))
    whole, two = (a + b for a, b in zip(*sums))
    lines = [jnp.sum(v, axis=1, keepdims=True) for v in (whole, branch_ref[...], two)]
    lines.append(jnp.full((1, 1), total.astype(f32), f32))
    for i in range(8):
        line = jnp.broadcast_to(lines[min(i, 3)], (1, 128))
        for ref in refs[:-2][1:]:
            line = line + ref[i : i + 1, :]
        sums_ref[i : i + 1, :] = line


def output_call(which, lengths, both, other, middle, vecs, branch, filled, after):
    rows, features = middle.shape
    count = len(after)

    def kernel(lengths_ref, *refs):
        output_kernel(lengths_ref, *refs[count:])

    whole = pl.BlockSpec(memory_space=pltpu.VMEM)
    anywhere = pl.BlockSpec(memory_space=pl.ANY)
    more = [anywhere, whole] if filled else []
    return pl.pallas_call(
        kernel,
        grid=(1,),
        out_shape=(shape((2, rows, features), bf16), shape((8, 128), f32)),
        in_specs=[pl.BlockSpec(memory_space=pltpu.SMEM)] + [anywhere] * count + [whole] * 5 + more,
        out_specs=(pl.BlockSpec((1, rows, features), lambda i: (which, 0, 0)), whole),
        input_output_aliases={1 + count + 5: 0} if filled else {},
        compiler_params=pltpu.CompilerParams(vmem_limit_bytes=16 * 2**20),
        cost_estimate=cost(),
        name="output_kernel",
    )(lengths, *after, both, other, middle, vecs, branch, *filled)


def message_kernel(norm_one, norm_two, sums_one, sums_two, off_one, off_two, heads_one, heads_two, out_ref):
    width = heads_one.shape[1] // 3
    out_ref[...] = jnp.zeros_like(out_ref)
    out_ref[0:2, :] = norm_one[...] + norm_two[...]
    out_ref[2:6, :] = sums_one[...] + sums_two[...]
    out_ref[6:7, :] = off_one[...] + off_two[...]
    heads = heads_one[...] + heads_two[...]
    out_ref[8:9, :width] = heads[:, :width]
    out_ref[9:10, :width] = heads[:, 2 * width :]


def shards_kernel(*refs):
    *pairs, grads_ref, out_ref = refs
    column = 0
    squares = jnp.zeros((1, 1), f32)
    for keep_ref, moved_ref in zip(pairs[::2], pairs[1::2]):
        grad = keep_ref[...].astype(f32) + moved_ref[...].astype(f32)
        stop = column + grad.shape[1]
        grads_ref[:, column:stop] = grad
        squares = squares + whole_sum(grad * grad)
        column = stop
    out_ref[...] = jnp.broadcast_to(squares, out_ref.shape)


def partial_kernel(message_ref, out_ref):
    squares = whole_sum(message_ref[8:10, :] * message_ref[8:10, :])
    squares = squares + whole_sum(message_ref[6:7, :] * message_ref[6:7, :])
    out_ref[...] = jnp.broadcast_to(squares, out_ref.shape)


def rms_kernel(features, own_ref, moved_ref, out_ref):
    sums = own_ref[...] + moved_ref[...]
    values = jnp.sqrt(sums / (sums[3:4, :] * features))
    for i in range(3):
        out_ref[i] = jnp.max(values[i : i + 1, :])


def rms_call(own, moved, features, after):
    def kernel(*refs):
        rms_kernel(features, *refs[1:])

    return pl.pallas_call(
        kernel,
        out_shape=shape((3,), f32),
        in_specs=[pl.BlockSpec(memory_space=pl.ANY)] + [pl.BlockSpec(memory_space=pltpu.VMEM)] * 2,
        out_specs=pl.BlockSpec(memory_space=pltpu.SMEM),
        compiler_params=pltpu.CompilerParams(vmem_limit_bytes=8 * 2**20),
        cost_estimate=cost(),
        name="rms_kernel",
    )(after, own, moved)


def adamw_kernel(partial_ref, moved_ref, message_ref, grads_ref, *refs):
    count = 21
    inputs, targets, norm_ref = refs[:count], refs[count : 2 * count], refs[2 * count]
    outputs, write_sems = refs[2 * count + 1 : 3 * count + 1], refs[3 * count + 1]
    writes = [pltpu.make_async_copy(outputs[i], targets[i], write_sems.at[i]) for i in range(count)]
    width = inputs[0].shape[2]
    hidden = inputs[6].shape[1]
    vecs = message_ref[0:6, :]
    norm = jnp.sqrt(partial_ref[0:1, 0:1] + moved_ref[0:1, 0:1] + whole_sum(vecs * vecs))
    norm_ref[0] = jnp.max(norm)
    clip = jnp.minimum(1.0, clip_limit / (norm + 1e-06))

    def step(p, gradient, at=Ellipsis):
        weight, moment, square = (ref[at] for ref in inputs[3 * p : 3 * p + 3])
        decay = matrix_decay if p < 4 else 0.0
        factor = clip if gradient.ndim == 2 else jnp.max(clip)
        values = adamw_step(weight, moment, square, gradient, step_rates[p], decay, factor)
        for ref, value in zip(outputs[3 * p : 3 * p + 3], values):
            ref[at] = value

    start = 4 * width
    parts = (
        tuple((grads_ref[:, j * width : (j + 1) * width], j) for j in range(3)),
        ((grads_ref[:, 3 * width : start].T,),),
        ((grads_ref[:, start : start + hidden],),),
        ((grads_ref[:, start + hidden :],),),
        ((vecs,),),
        ((message_ref[8:10, : inputs[15].shape[1]],),),
        ((message_ref[6, :],),),
    )
    for p, steps in enumerate(parts):
        for arguments in steps:
            step(p, *arguments)
        for copy in writes[3 * p : 3 * p + 3]:
            copy.start()
    for copy in writes:
        copy.wait()


def adamw_call(partial, moved, message, grads, state, after):
    in_vmem = pl.BlockSpec(memory_space=pltpu.VMEM)
    anywhere = pl.BlockSpec(memory_space=pltpu.MemorySpace.HBM)
    count = len(state)

    def kernel(*refs):
        adamw_kernel(*refs[len(after) :])

    return pl.pallas_call(
        kernel,
        out_shape=tuple(shape(v.shape, f32) for v in state) + (shape((1,), f32),),
        in_specs=[pl.BlockSpec(memory_space=pl.ANY)] * len(after) + [in_vmem] * (4 + count),
        out_specs=(anywhere,) * count + (pl.BlockSpec(memory_space=pltpu.SMEM),),
        scratch_shapes=[pltpu.VMEM(v.shape, f32) for v in state] + [pltpu.SemaphoreType.DMA((count,))],
        compiler_params=pltpu.CompilerParams(vmem_limit_bytes=24 * 2**20),
        cost_estimate=cost(),
        name="adamw_kernel",
    )(*after, partial, moved, message, grads, *state)


def build(n):
    top = n // 2

    def local(
        inputs,
        time_first,
        time_second,
        lengths_first,
        lengths_second,
        cotangent,
        w_qkv,
        m_qkv,
        v_qkv,
        w_proj,
        m_proj,
        v_proj,
        w_up,
        m_up,
        v_up,
        w_down,
        m_down,
        v_down,
        w_vecs,
        m_vecs,
        v_vecs,
        b_heads,
        m_heads,
        v_heads,
        b_hidden,
        m_hidden,
        v_hidden,
    ):
        rows, features = inputs.shape[1], inputs.shape[2]
        r, _, width = w_qkv.shape
        hidden = w_up.shape[1]
        heads = width // HD
        half = rows // 2
        lengths = (lengths_first, lengths_second)
        whole_f = shape((rows, features), f32)
        whole_b = shape((rows, features), bf16)
        hidden_b = shape((rows, hidden), bf16)
        half_b = shape((half, features), bf16)
        half_f = shape((half, features), f32)
        line = shape((1, features), f32)

        def swap(v, bit):
            return swap_bit(v, "dp", n, bit)

        def gathered(shard, bit, stop, after=()):
            while bit > stop:
                (shard,) = merged(shard, swap(shard, bit), r, bit, after)
                after = ()
                bit //= 2
            return shard

        qk, vp = call(
            pack_kernel, (shape((r, 2 * width), bf16),) * 2, (), (w_qkv.transpose(1, 0, 2), w_proj), (), 8
        )
        times = [jnp.pad(t[0], ((0, 16 - t.shape[1]), (0, 0))) for t in (time_first, time_second)]
        stream_one, normed_one, stream_two, normed_two = call(
            first_norm_kernel, (whole_f, whole_b) * 2, lengths, (inputs, *times, w_vecs), (qk,), 24
        )
        stream, normed = (stream_one, stream_two), (normed_one, normed_two)
        qk = gathered(qk, top, top // 2, (normed_two,))
        vp = gathered(vp, top, top // 2, (qk,))
        qk = gathered(qk, top // 2, 1, (vp,))
        (up,) = call(cast_kernel, (shape((r, hidden), bf16),), (), (w_up,), (qk,), 8)
        vp = gathered(vp, top // 2, 1, (up,))
        (qk,) = merged(qk, swap(qk, 1), r, 1, (vp,))
        (down,) = call(cast_kernel, (shape((r, hidden), bf16),), (), (w_down.T,), (qk,), 8)
        up = gathered(up, top, top // 2, (down,))
        wv, proj = merged(vp, swap(vp, 1), r, 1, (up,), (width, width))

        def spread(v, after=()):
            moved = over_chip(v)
            pair = call(pair_kernel, shape((rows, 2 * v.shape[1]), bf16), (), (v, moved), after, 8)
            return [pair, over_core(pair)]

        bias = jnp.concatenate([b_heads[0], jnp.zeros_like(b_heads[0]), b_heads[1]])[None]
        head_low = pltpu.VMEM((heads, rows, HD), bf16)
        head_full = pltpu.VMEM((heads, rows, HD), f32)
        after = (wv,)
        att, sent, qkv, lse = [], [], [], []
        for b in range(2):
            carried = (proj,) if b == 0 else ()
            a, q, l, *pair = call(
                functools.partial(forward_kernel, REACH[b], len(carried)),
                (
                    shape((rows, width), bf16),
                    shape((rows, 3 * width), bf16),
                    shape((rows, 128), f32),
                    *(shape((rows, 2 * width), bf16) for _ in carried),
                ),
                (lengths[b],),
                (normed[b], qk, wv, bias, *carried),
                after,
                12,
                [head_low] * 3,
            )
            att.append(a)
            sent.append(pair[0] if pair else a)
            qkv.append(q)
            lse.append(l)
            after = (l,)
            if b == 0:
                down = gathered(down, top, top // 2, after)
                up = gathered(up, top // 2, 1, (down,))
                down = gathered(down, top // 2, 1, (up,))
                after = (down,)
        att_first = spread(sent[0], after)
        (up,) = merged(up, swap(up, 1), r, 1, (att_first[0],), weight=4)
        after = (up,)

        names = [[] for _ in range(9)]
        att_own = []
        for b in range(2):
            outs = call(
                hidden_kernel,
                (whole_f, whole_b, hidden_b, shape((rows, hidden), f32), line),
                (lengths[b],),
                (*att_first, *att_own, stream[b], w_vecs, up, b_hidden[None]),
                after,
            )
            for kept, v in zip(names, outs):
                kept.append(v)
            after = (outs[-1],)
            if b == 0:
                att_own = spread(sent[1], after)
                upstream = call(upstream_kernel, (whole_b,) * 2, lengths, (cotangent,), (att_own[0],))
                after = (upstream[1],)
        (down,) = merged(down, swap(down, 1), r, 1, after)
        low, parts = [], [[], []]

        def down_part(b, side, after):
            out = (half_b, half_f)[side]
            part = call(functools.partial(down_kernel, side), out, (), (active[b], down), after)
            parts[b].insert(0, part)
            return part

        after = (down,)
        for b in range(2):
            outs = call(
                hidden_back_kernel,
                (hidden_b, half_b, half_f, shape((1, hidden), f32)),
                (),
                (upstream[b], names[3][b], up, down),
                after,
            )
            for kept, v in zip(names[5:], outs):
                kept.append(v)
            middle, normed_mid, active, slope, branch_square, grad_hidden, away, keep, offsets = names
            if b == 0:
                after = (down_part(0, 1, (outs[-1],)),)
            else:
                bulk = parted((*normed_mid, *grad_hidden, *upstream, *active), n, (outs[-1],))
                bulk_moved = swap(bulk[0], 1)
                after = (bulk[0],)
            low.append(add(keep[b], over_core(away[b]), after))
            after = (low[b],)
        both = add(low[0], over_chip(low[0]), after)
        gnt = [(both, over_core(both))]
        after = (down_part(1, 1, (both,)),)

        grad_middle, middle_low, grad_mixed, sums, head_sums, back_low = [], [], [], [], [], []
        for b in range(2):
            outs = call(
                functools.partial(backward_kernel, REACH[b]),
                (
                    whole_f,
                    whole_b,
                    shape((rows, 3 * width), bf16),
                    half_b,
                    half_f,
                    shape((4, features), f32),
                    shape((1, 3 * width), f32),
                ),
                (lengths[b],),
                (*gnt[b], middle[b], upstream[b], w_vecs, qk, wv, proj, qkv[b], lse[b]),
                after,
                24,
                [head_low] * 4 + [head_full] * 2,
            )
            grad_middle.append(outs[0])
            middle_low.append(outs[1])
            grad_mixed.append(outs[2])
            sums.append(outs[5])
            head_sums.append(outs[6])
            after = (outs[6],)
            if b == 0:
                both = add(low[1], over_chip(low[1]), after)
                gnt.append((both, over_core(both)))
                after = (both,)
            else:
                bulk = split(bulk[1], bulk_moved, r, 2, after)
                bulk_moved = swap(bulk[0], 2)
                chunk = parted((*normed, *grad_mixed, *middle_low, *att), n, (bulk[0],))
                chunks = [[*chunk, swap(chunk[0], 1)]]
                after = (chunk[0],)
            back_low.append(add(outs[4], over_core(outs[3]), after))
            after = (back_low[b],)

        def halved(chunk, bit, after):
            away, kept = split(chunk[1], chunk[2], r, bit, after)
            return [away, kept, swap(away, bit)]

        moved = down_part(0, 0, after)
        both = add(back_low[0], over_chip(back_low[0]), (moved,))
        piece = (both, over_core(both))
        part = [add(parts[0][1], over_core(parts[0][0]), (both,))]
        after = (part[0],)
        bulk = [*bulk, bulk_moved]
        bit = 4
        while bit < n:
            bulk = halved(bulk, bit, after)
            after = (bulk[0],)
            bit *= 2
        for i in range(len(chunks)):
            chunks[i] = halved(chunks[i], 2, after)
            after = (chunks[i][0],)
        input_grad, pair = input_grad_call(0, *piece, stream[0], grad_middle[0], w_vecs, (), after)
        norm_sums = [pair]
        after = (pair,)
        moved = down_part(1, 0, after)
        both = add(back_low[1], over_chip(back_low[1]), (moved,))
        piece = (both, over_core(both))
        part.append(add(parts[1][1], over_core(parts[1][0]), (both,)))
        input_grad, pair = input_grad_call(
            1, *piece, stream[1], grad_middle[1], w_vecs, (input_grad,), (part[1],)
        )
        norm_sums.append(pair)

        def hop(v, moved, after=(), more=()):
            return call(sum_kernel, shape(v.shape, f32), (), (v, moved, *more), after, 8)

        message = call(
            message_kernel, shape((16, features), f32), (), (*norm_sums, *sums, *offsets, *head_sums), (), 8
        )
        after = (message,)
        bit = 4
        while bit < n:
            for i in range(len(chunks)):
                chunks[i] = halved(chunks[i], bit, after)
                after = (chunks[i][0],)
            bit *= 2
        both = add(part[0], over_chip(part[0]), after)
        two = [(both, over_core(both))]
        message = hop(message, swap(message, 1), (both,))
        filled = output_call(0, lengths[0], *two[0], middle[0], w_vecs, branch_square[0], (), (message,))
        message = hop(message, swap(message, 2), (filled[1],))
        grads, squares = call(
            shards_kernel,
            (shape((r, 4 * width + 2 * hidden), f32), shape((8, 128), f32)),
            (),
            tuple(v for chunk in (*chunks, bulk) for v in chunk[1:]),
            (message,),
        )
        after = (squares,)
        bit = 4
        while bit < n:
            message = hop(message, swap(message, bit), after)
            after = ()
            bit *= 2
        partial = call(partial_kernel, shape((8, 128), f32), (), (message,), (), 8)
        both = add(part[1], over_chip(part[1]), (partial,))
        two.append((both, over_core(both)))
        squares = hop(squares, swap(squares, 1), (both,))
        block_out, out_sums = output_call(
            1, lengths[1], *two[1], middle[1], w_vecs, branch_square[1], tuple(filled), (squares,)
        )
        after = (out_sums,)
        bit = 2
        while bit < n:
            more = (partial,) if 2 * bit == n else ()
            squares = hop(squares, swap(squares, bit), after, more)
            after = ()
            bit *= 2
        out_sums = hop(out_sums, swap(out_sums, 1), (squares,))
        partial = hop(squares, over_core(squares), (out_sums,))
        out_sums = hop(out_sums, swap(out_sums, 2), (partial,))
        bit = 4
        last = out_sums
        state = (
            *(v.transpose(1, 0, 2) for v in (w_qkv, m_qkv, v_qkv)),
            *(w_proj, m_proj, v_proj),
            *(w_up, m_up, v_up),
            *(v.T for v in (w_down, m_down, v_down)),
            *(w_vecs, m_vecs, v_vecs),
            *(b_heads, m_heads, v_heads),
            *(b_hidden, m_hidden, v_hidden),
        )
        *updated, grad_norm = adamw_call(partial, over_chip(partial), message, grads, state, (last,))
        while 2 * bit < n:
            out_sums = hop(out_sums, swap(out_sums, bit), (grad_norm,))
            bit *= 2
        stream_rms = rms_call(out_sums, swap(out_sums, bit), features, grad_norm)
        return (
            block_out,
            input_grad,
            grad_norm,
            stream_rms,
            *(v.transpose(1, 0, 2) for v in updated[:3]),
            *updated[3:9],
            *(v.T for v in updated[9:12]),
            *updated[12:18],
            *updated[18:],
        )

    return local


def solution(mesh):
    rows = P(None, "dp", None)
    group = P("dp", None, None)
    qkv, proj, up = P("dp", None, "tensor"), P("tensor", "dp"), P("dp", "tensor")
    params = [qkv] * 3 + [proj] * 3 + [up] * 3 + [proj] * 3 + [P()] * 3
    params += [P(None, "tensor")] * 3 + [P("tensor")] * 3
    return jax.shard_map(
        build(mesh.shape["dp"]),
        mesh=mesh,
        in_specs=(rows, group, group, P("dp", None), P("dp", None), rows, *params),
        out_specs=(rows, rows, P(), P(), *params),
        check_vma=False,
    )
```

```python
import functools

import jax
import jax.numpy as jnp
from jax import lax
from jax.experimental import pallas as pl
from jax.experimental.pallas import tpu as pltpu
from jax.sharding import PartitionSpec as P

HD = 64
STEP = 5
TILE = 128
BLOCK = 256
CHUNK = 384
REACH = (64, 128)

norm_eps = 1e-05
clip_limit = 1.0
beta_first = 0.5
beta_second = 0.5
adam_eps = 1e-08
matrix_decay = 0.01
masked_score = -1e30
step_rates = (0.03, 0.2, 0.03, 0.015, 0.3, 0.3, 0.3)
bf16 = jnp.bfloat16
f32 = jnp.float32

KERNEL_FLOPS = 7 * 10**9

NN = ((1,), (0,))
NT = ((1,), (1,))
TN = ((0,), (0,))


def dot(a, b, dims):
    return lax.dot_general(a, b, (dims, ((), ())), preferred_element_type=f32)


def shape(dims, dtype):
    return jax.ShapeDtypeStruct(dims, dtype)


def cost(weight=1):
    return pl.CostEstimate(flops=weight * KERNEL_FLOPS, bytes_accessed=0, transcendentals=0)


def call(body, outs, words, arrays, after=(), limit=16, scratch=(), weight=1):
    count = len(after)

    def kernel(*refs):
        body(*refs[: len(words)], *refs[len(words) + count :])

    in_vmem = pl.BlockSpec(memory_space=pltpu.VMEM)
    in_specs = [pl.BlockSpec(memory_space=pltpu.SMEM)] * len(words)
    in_specs += [pl.BlockSpec(memory_space=pl.ANY)] * count + [in_vmem] * len(arrays)
    return pl.pallas_call(
        kernel,
        out_shape=outs,
        in_specs=in_specs,
        out_specs=(in_vmem,) * len(outs) if isinstance(outs, tuple) else in_vmem,
        scratch_shapes=list(scratch),
        compiler_params=pltpu.CompilerParams(vmem_limit_bytes=limit * 2**20),
        cost_estimate=cost(weight),
        name=getattr(body, "func", body).__name__,
    )(*words, *after, *arrays)


def core_index():
    return lax.rem(lax.axis_index("tensor"), 2)


def dp_bit(bit):
    return lax.rem(lax.div(lax.axis_index("dp"), bit), 2)


def rows_sum(v):
    return jnp.sum(v, axis=0, keepdims=True)


def whole_sum(v):
    return jnp.sum(rows_sum(v), axis=1, keepdims=True)


def norm_parts(stream):
    center = stream - jnp.mean(stream, axis=-1, keepdims=True)
    spread = jnp.mean(center * center, axis=-1, keepdims=True)
    scale = lax.rsqrt(spread + norm_eps)
    return center * scale, scale


def norm_back(scaled, xhat, scale):
    mean = jnp.mean(scaled, axis=-1, keepdims=True)
    return scale * (scaled - mean - xhat * jnp.mean(scaled * xhat, axis=-1, keepdims=True))


def adamw_step(weight, moment_old, square_old, gradient, step_rate, decay_value, clip_factor):
    correct_one = 1.0 - beta_first**STEP
    correct_two = 1.0 - beta_second**STEP
    clipped = gradient * clip_factor
    moment_new = beta_first * moment_old + (1.0 - beta_first) * clipped
    square_new = beta_second * square_old + (1.0 - beta_second) * clipped * clipped
    divisor = jnp.sqrt(square_new / correct_two) + adam_eps
    weight_new = weight - step_rate * (moment_new / correct_one / divisor + decay_value * weight)
    return (weight_new, moment_new, square_new)


def swap_bit(v, axis, size, bit):
    return lax.ppermute(v, axis, [(i, i ^ bit) for i in range(size)])


def over_core(v):
    return swap_bit(v, "tensor", 4, 1)


def over_chip(v):
    return swap_bit(v, "tensor", 4, 2)


def merge_kernel(r, bit, own_ref, other_ref, *out_refs):
    mine = dp_bit(bit)
    for g in range(own_ref.shape[0] // r):
        for ref, side in ((own_ref, mine), (other_ref, 1 - mine)):
            start = pl.multiple_of((2 * g + side) * r, 16)
            column = 0
            for out_ref in out_refs:
                stop = column + out_ref.shape[1]
                out_ref[pl.ds(start, r), :] = ref[g * r : (g + 1) * r, column:stop]
                column = stop


def merged(own, other, r, bit, after=(), widths=None, weight=1):
    rows, width = own.shape
    widths = widths or (width,)
    if r % 16:
        own, other = (v.reshape(rows // r, r, width) for v in (own, other))
        sides = [jnp.where(dp_bit(bit) == 0, own, other), jnp.where(dp_bit(bit) == 0, other, own)]
        both = jnp.stack(sides, axis=1).reshape(2 * rows, width)
        return tuple(jnp.split(both, [sum(widths[:i]) for i in range(1, len(widths))], axis=1))
    outs = tuple(shape((2 * rows, w), bf16) for w in widths)
    return call(functools.partial(merge_kernel, r, bit), outs, (), (own, other), after, 8, weight=weight)


def split_kernel(r, bit, keep_ref, moved_ref, away_ref, own_ref):
    mine = dp_bit(bit)
    for g in range(away_ref.shape[0] // r):
        for out_ref, side in ((away_ref, 1 - mine), (own_ref, mine)):
            here = pl.ds(pl.multiple_of((2 * g + side) * r, 16), r)
            total = keep_ref[here, :].astype(f32) + moved_ref[here, :].astype(f32)
            out_ref[g * r : (g + 1) * r, :] = total.astype(out_ref.dtype)


def split(keep, moved, r, bit, after=()):
    half, width = keep.shape[0] // 2, keep.shape[1]
    if r % 16:
        total = (keep.astype(f32) + moved.astype(f32)).reshape(half // r, 2, r, width)
        pieces = [lax.dynamic_index_in_dim(total, i, 1, False) for i in (1 - dp_bit(bit), dp_bit(bit))]
        away, own = (v.reshape(half, width) for v in pieces)
        return away.astype(bf16), own
    outs = (shape((half, width), bf16), shape((half, width), f32))
    return call(functools.partial(split_kernel, r, bit), outs, (), (keep, moved), after, 8)


def sum_kernel(own_ref, moved_ref, *refs):
    *more_refs, out_ref = refs
    total = own_ref[...] + moved_ref[...]
    for ref in more_refs:
        total = total + ref[...]
    out_ref[...] = total


def tree_kernel(*refs):
    *value_refs, more_ref, out_ref = refs
    values = [ref[...] for ref in value_refs]
    while len(values) > 1:
        values = [a + b for a, b in zip(values[::2], values[1::2])]
    out_ref[...] = values[0] + more_ref[...]


def add_kernel(keep_ref, moved_ref, out_ref):
    out_ref[...] = (keep_ref[...].astype(f32) + moved_ref[...].astype(f32)).astype(bf16)


def add(keep, moved, after=()):
    return call(add_kernel, shape(keep.shape, bf16), (), (keep, moved), after, 8)


def pack_kernel(qkv_ref, proj_ref, qk_ref, vp_ref):
    qk_ref[...] = jnp.concatenate([qkv_ref[0], qkv_ref[1]], axis=1).astype(bf16)
    vp_ref[...] = jnp.concatenate([qkv_ref[2], proj_ref[...].T], axis=1).astype(bf16)


def pair_kernel(left_ref, right_ref, out_ref):
    width = left_ref.shape[1]
    out_ref[:, :width] = left_ref[...]
    out_ref[:, width:] = right_ref[...]


def upstream_kernel(lengths_one, lengths_two, cot_ref, *out_refs):
    rows = cot_ref.shape[1]
    for b, (lengths_ref, out_ref) in enumerate(zip((lengths_one, lengths_two), out_refs)):
        valid = lax.broadcasted_iota(jnp.int32, (rows, 1), 0) < valid_count(lengths_ref)
        out_ref[...] = jnp.where(valid, cot_ref[b].astype(f32), 0.0).astype(bf16)


def cast_kernel(*refs):
    half = len(refs) // 2
    for source, out in zip(refs[:half], refs[half:]):
        out[...] = source[...].astype(bf16)


def segment_grid(lengths_ref, dims, axis, first=0):
    places = first + lax.broadcasted_iota(jnp.int32, dims, axis)
    ids = jnp.zeros(dims, jnp.int32)
    bound = jnp.int32(0)
    for k in range(lengths_ref.shape[1]):
        bound = bound + lengths_ref[0, k]
        ids = ids + (places >= bound).astype(jnp.int32)
    return ids


def same_segment(lengths_ref, start, low, high):
    queries = segment_grid(lengths_ref, (TILE, 1), 0, start)
    return queries == segment_grid(lengths_ref, (1, high - low), 1, low)


def valid_count(lengths_ref):
    total = jnp.int32(0)
    for k in range(lengths_ref.shape[1]):
        total = total + lengths_ref[0, k]
    return total


def first_norm_kernel(lengths_one, lengths_two, inputs_ref, times_one, times_two, vecs_ref, *refs):
    rows = inputs_ref.shape[1]
    for b, (lengths_ref, times_ref) in enumerate(((lengths_one, times_one), (lengths_two, times_two))):
        stream_ref, normed_ref = refs[2 * b : 2 * b + 2]
        depth = times_ref.shape[0]
        ids = segment_grid(lengths_ref, (rows, 1), 0)
        for start in range(0, rows, BLOCK):
            here = slice(start, start + BLOCK)
            lanes = lax.broadcasted_iota(jnp.int32, (BLOCK, depth), 1)
            pick = (ids[here] == lanes).astype(f32).astype(bf16)
            stream = inputs_ref[b, here, :].astype(f32) + dot(pick, times_ref[...], NN)
            stream_ref[here, :] = stream
            xhat, _ = norm_parts(stream)
            normed_ref[here, :] = (xhat * vecs_ref[0:1, :] + vecs_ref[1:2, :]).astype(bf16)


def windows(rows, reach):
    size = min(rows, TILE + 2 * reach)
    out = []
    for start in range(0, rows, TILE):
        low = max(0, start - reach)
        high = min(rows, start + TILE + reach)
        if (high - low) % 128:
            low = min(low, rows - size)
            high = low + size
        out.append((start, low, high))
    return out


def split_heads(low, rows, q_s, k_s, v_s):
    heads = q_s.shape[0]
    width = heads * HD
    for h in range(heads):
        cut = h * HD
        q_s[h, rows, :] = low[:, cut : cut + HD] * jnp.array(HD**-0.5, bf16)
        k_s[h, rows, :] = low[:, width + cut : width + cut + HD]
        v_s[h, rows, :] = low[:, 2 * width + cut : 2 * width + cut + HD]


def forward_kernel(reach, carried, lengths_ref, normed_ref, qk_ref, wv_ref, bias_ref, *refs):
    att_ref, qkv_ref, lse_ref, *pair_refs, q_s, k_s, v_s = refs[carried:]
    rows, width = att_ref.shape
    heads = range(width // HD)
    for start in range(0, rows, BLOCK):
        piece = slice(start, start + BLOCK)
        normed = normed_ref[piece, :]
        pair = dot(normed, qk_ref[...], NN)
        values = dot(normed, wv_ref[...], NN)
        low = (jnp.concatenate([pair, values], axis=1) + bias_ref[...]).astype(bf16)
        qkv_ref[piece, :] = low
        split_heads(low, piece, q_s, k_s, v_s)
    lanes = lax.broadcasted_iota(jnp.int32, (TILE, 128), 1)
    for start, low, high in windows(rows, reach):
        tile = slice(start, start + TILE)
        allowed = same_segment(lengths_ref, start, low, high)
        scores = [dot(q_s[h, tile, :], k_s[h, low:high, :], NT) for h in heads]
        scores = [jnp.where(allowed, s, masked_score) for s in scores]
        peaks = [jnp.max(s, axis=-1, keepdims=True) for s in scores]
        exponents = [jnp.exp(s - p) for s, p in zip(scores, peaks)]
        totals = [jnp.sum(e, axis=-1, keepdims=True) for e in exponents]
        probs = [(e * (1.0 / t)).astype(bf16) for e, t in zip(exponents, totals)]
        outs = [dot(p, v_s[h, low:high, :], NN).astype(bf16) for h, p in enumerate(probs)]
        att_ref[tile, :] = jnp.concatenate(outs, axis=1)
        logs = jnp.zeros((TILE, 128), f32)
        for h in heads:
            logs = jnp.where(lanes == h, peaks[h] + jnp.log(totals[h]), logs)
        lse_ref[tile, :] = logs
    for ref, pair_ref in zip(refs[:carried], pair_refs):
        pair_ref[...] = jnp.concatenate([att_ref[...], ref[...]], axis=1)


def hidden_kernel(lengths_ref, *refs):
    first_refs, att_refs = refs[:2], refs[-11:-9]
    stream_ref, vecs_ref, up_ref, bias_ref = refs[-9:-5]
    middle_ref, normed_ref, active_ref, slope_ref, square_ref = refs[-5:]
    rows, features = stream_ref.shape
    width = first_refs[0].shape[1] // 4
    step = att_refs[0].shape[1] // 2
    total = valid_count(lengths_ref)
    squares = jnp.zeros((1, features), f32)
    for start in range(0, rows, CHUNK):
        here = slice(start, start + CHUNK)
        valid = start + lax.broadcasted_iota(jnp.int32, (CHUNK, 1), 0) < total
        own, over, near, across = (
            dot(a[here, k * step : k * step + width], p[:, (2 * k + 1) * width : (2 * k + 2) * width], NT)
            for a, p in zip(att_refs, first_refs)
            for k in range(2)
        )
        branch = ((own + near) + (over + across)) + vecs_ref[4:5, :]
        kept = jnp.where(valid, branch, 0.0)
        squares = squares + rows_sum(kept * kept)
        middle = stream_ref[here, :] + branch
        middle_ref[here, :] = middle
        xhat, _ = norm_parts(middle)
        normed = (xhat * vecs_ref[2:3, :] + vecs_ref[3:4, :]).astype(bf16)
        normed_ref[here, :] = normed
        hidden = dot(normed, up_ref[...], NN) + bias_ref[...]
        cdf = 0.5 + 0.5 * lax.erf(hidden * 0.5**0.5)
        pdf = jnp.exp(-0.5 * hidden * hidden) * 0.3989422804014327
        active_ref[here, :] = (hidden * cdf).astype(bf16)
        slope_ref[here, :] = cdf + hidden * pdf
    square_ref[...] = squares


def hidden_back_kernel(upstream_ref, slope_ref, up_ref, down_ref, grad_ref, away_ref, keep_ref, offset_ref):
    rows = upstream_ref.shape[0]
    half = rows // 2
    first = (1 - core_index()) * half

    def rows_step(t, offsets):
        here = pl.ds(pl.multiple_of(lax.rem(first + t * CHUNK, rows), CHUNK), CHUNK)
        grad = dot(upstream_ref[here, :], down_ref[...], NN) * slope_ref[here, :]
        low = grad.astype(bf16)
        grad_ref[here, :] = low
        part = dot(low, up_ref[...], NT)

        @pl.when(t * CHUNK < half)
        def _():
            away_ref[pl.ds(pl.multiple_of(t * CHUNK, CHUNK), CHUNK), :] = part.astype(bf16)

        @pl.when(t * CHUNK >= half)
        def _():
            keep_ref[pl.ds(pl.multiple_of(t * CHUNK - half, CHUNK), CHUNK), :] = part

        return offsets + rows_sum(grad)

    offset_ref[...] = lax.fori_loop(0, rows // CHUNK, rows_step, jnp.zeros(offset_ref.shape, f32))


def down_kernel(side, active_ref, down_ref, out_ref):
    half = active_ref.shape[0] // 2
    core = core_index()
    base = (core if side else 1 - core) * half
    here = pl.ds(pl.multiple_of(base, half), half)
    out_ref[...] = dot(active_ref[here, :], down_ref[...], NT).astype(out_ref.dtype)


def products_kernel(pairs, *refs):
    out_ref = refs[-1]
    for m in range(0, out_ref.shape[0], BLOCK):
        cut = slice(m, m + BLOCK)
        column = 0
        for p in range(pairs):
            left_one, left_two, right_one, right_two = refs[4 * p : 4 * p + 4]
            rows = left_one.shape[0]
            part = dot(left_one[:, cut], right_one[:rows, :], TN) + dot(left_two[:, cut], right_two[:rows, :], TN)
            out_ref[cut, column : column + part.shape[1]] = part.astype(out_ref.dtype)
            column += part.shape[1]


def parted_kernel(r, *refs):
    away_ref, keep_ref, full_s = refs[-3:]
    products_kernel(len(refs) // 4, *refs[:-3], full_s)
    inner = dp_bit(1)
    for o in range(away_ref.shape[0] // r):
        for out_ref, side in ((away_ref, 1 - inner), (keep_ref, inner)):
            start = pl.multiple_of((o * 2 + side) * r, 8)
            out_ref[o * r : (o + 1) * r, :] = full_s[pl.ds(start, r), :].astype(bf16)


def parted(arrays, n, after):
    rows, width = arrays[0].shape[1], sum(v.shape[1] for v in arrays[2::4])
    r = rows // n
    if r % 16:
        kernel = functools.partial(products_kernel, len(arrays) // 4)
        full = call(kernel, shape((rows, width), bf16), (), arrays, after)
        view = full.reshape(n // 2, 2, r, width)
        inner = dp_bit(1)
        pieces = [lax.dynamic_index_in_dim(view, i, 1, False) for i in (1 - inner, inner)]
        return [v.reshape(rows // 2, width) for v in pieces]
    outs = (shape((rows // 2, width), bf16),) * 2
    scratch = [pltpu.VMEM((rows, width), f32)]
    return call(functools.partial(parted_kernel, r), outs, (), arrays, after, 24, scratch)


def backward_kernel(
    reach,
    lengths_ref,
    both_ref,
    other_ref,
    middle_ref,
    upstream_ref,
    vecs_ref,
    qk_ref,
    wv_ref,
    proj_ref,
    qkv_ref,
    lse_ref,
    grad_middle_ref,
    low_ref,
    mixed_ref,
    away_ref,
    keep_ref,
    sums_ref,
    heads_ref,
    q_s,
    k_s,
    v_s,
    g_s,
    dk_s,
    dv_s,
):
    rows, features = middle_ref.shape
    half = rows // 2
    width = qkv_ref.shape[1] // 3
    heads = range(width // HD)
    core = core_index()
    gain = vecs_ref[2:3, :]
    sums = []
    for piece_ref, base in ((both_ref, core * half), (other_ref, (1 - core) * half)):

        def rows_step(t, acc, piece_ref=piece_ref, base=base):
            off = pl.multiple_of(base + t * TILE, TILE)
            here = pl.ds(off, TILE)
            gnt = piece_ref[pl.ds(pl.multiple_of(t * TILE, TILE), TILE), :].astype(f32)
            xhat, scale = norm_parts(middle_ref[here, :])
            upstream = upstream_ref[here, :].astype(f32)
            grad_middle = upstream + norm_back(gnt * gain, xhat, scale)
            grad_middle_ref[here, :] = grad_middle
            low_ref[here, :] = grad_middle.astype(bf16)
            terms = (gnt * xhat, gnt, grad_middle, upstream)
            return tuple(a + rows_sum(v) for a, v in zip(acc, terms))

        start = (jnp.zeros((1, features), f32),) * 4
        sums.append(lax.fori_loop(0, half // TILE, rows_step, start))
    sums_ref[...] = jnp.concatenate([a + b for a, b in zip(*sums)], axis=0)
    for start in range(0, rows, BLOCK):
        piece = slice(start, start + BLOCK)
        split_heads(qkv_ref[piece, :], piece, q_s, k_s, v_s)
        grad_att = dot(low_ref[piece, :], proj_ref[...], NN).astype(bf16)
        for h in heads:
            g_s[h, piece, :] = grad_att[:, h * HD : (h + 1) * HD]
    dk_s[...] = jnp.zeros_like(dk_s)
    dv_s[...] = jnp.zeros_like(dv_s)
    for start, low, high in windows(rows, reach):
        tile = slice(start, start + TILE)
        keys = slice(low, high)
        allowed = same_segment(lengths_ref, start, low, high)
        scores = [dot(q_s[h, tile, :], k_s[h, keys, :], NT) for h in heads]
        grad_probs = [dot(g_s[h, tile, :], v_s[h, keys, :], NT) for h in heads]
        probs = [jnp.exp(jnp.where(allowed, s, masked_score) - lse_ref[tile, h : h + 1]) for h, s in enumerate(scores)]
        inner = [jnp.sum(p * g, axis=-1, keepdims=True) for p, g in zip(probs, grad_probs)]
        grads = [(p * (g - i)).astype(bf16) for p, g, i in zip(probs, grad_probs, inner)]
        lows = [p.astype(bf16) for p in probs]
        dqs = [(dot(g, k_s[h, keys, :], NN) * HD**-0.5).astype(bf16) for h, g in enumerate(grads)]
        mixed_ref[tile, :width] = jnp.concatenate(dqs, axis=1)
        dks = [dot(g, q_s[h, tile, :], TN) for h, g in enumerate(grads)]
        dvs = [dot(p, g_s[h, tile, :], TN) for h, p in enumerate(lows)]
        for h in heads:
            dk_s[h, keys, :] += dks[h]
            dv_s[h, keys, :] += dvs[h]
    for start in range(0, rows, BLOCK):
        piece = slice(start, start + BLOCK)
        both = [ref[h, piece, :].astype(bf16) for ref in (dk_s, dv_s) for h in heads]
        mixed_ref[piece, width:] = jnp.concatenate(both, axis=1)
    heads_ref[...] = rows_sum(mixed_ref[...].astype(f32))
    for out_ref, base in ((away_ref, (1 - core) * half), (keep_ref, core * half)):
        here = pl.ds(pl.multiple_of(base, half), half)
        part = dot(mixed_ref[here, : 2 * width], qk_ref[...], NT)
        part = part + dot(mixed_ref[here, 2 * width :], wv_ref[...], NT)
        out_ref[...] = part.astype(out_ref.dtype)


def input_grad_kernel(both_ref, other_ref, stream_ref, middle_ref, vecs_ref, *refs):
    out_ref, sums_ref = refs[-2:]
    rows, features = stream_ref.shape
    half = rows // 2
    core = core_index()
    gain = vecs_ref[0:1, :]
    sums = []
    for piece_ref, base in ((both_ref, core * half), (other_ref, (1 - core) * half)):

        def rows_step(t, acc, piece_ref=piece_ref, base=base):
            here = pl.ds(pl.multiple_of(base + t * TILE, TILE), TILE)
            grad = piece_ref[pl.ds(pl.multiple_of(t * TILE, TILE), TILE), :].astype(f32)
            xhat, scale = norm_parts(stream_ref[here, :])
            out_ref[0, here, :] = middle_ref[here, :] + norm_back(grad * gain, xhat, scale)
            return (acc[0] + rows_sum(grad * xhat), acc[1] + rows_sum(grad))

        start = (jnp.zeros((1, features), f32),) * 2
        sums.append(lax.fori_loop(0, half // TILE, rows_step, start))
    sums_ref[...] = jnp.concatenate([a + b for a, b in zip(*sums)], axis=0)


def input_grad_call(which, both, other, stream, middle, vecs, filled, after):
    rows, features = stream.shape
    count = len(after)

    def kernel(*refs):
        input_grad_kernel(*refs[count:])

    whole = pl.BlockSpec(memory_space=pltpu.VMEM)
    anywhere = pl.BlockSpec(memory_space=pl.ANY)
    return pl.pallas_call(
        kernel,
        grid=(1,),
        out_shape=(shape((2, rows, features), f32), shape((2, features), f32)),
        in_specs=[anywhere] * count + [whole] * 5 + [anywhere] * len(filled),
        out_specs=(pl.BlockSpec((1, rows, features), lambda i: (which, 0, 0)), whole),
        input_output_aliases={count + 5: 0} if filled else {},
        compiler_params=pltpu.CompilerParams(vmem_limit_bytes=24 * 2**20),
        cost_estimate=cost(),
    )(*after, both, other, stream, middle, vecs, *filled)


def output_kernel(lengths_ref, both_ref, other_ref, middle_ref, vecs_ref, branch_ref, *refs):
    out_ref, sums_ref = refs[-2:]
    rows, features = middle_ref.shape
    half = rows // 2
    core = core_index()
    total = valid_count(lengths_ref)
    sums = []
    for piece_ref, base in ((both_ref, core * half), (other_ref, (1 - core) * half)):

        def rows_step(t, acc, piece_ref=piece_ref, base=base):
            off = pl.multiple_of(base + t * TILE, TILE)
            here = pl.ds(off, TILE)
            two = piece_ref[pl.ds(pl.multiple_of(t * TILE, TILE), TILE), :].astype(f32) + vecs_ref[5:6, :]
            whole = middle_ref[here, :] + two
            out_ref[0, here, :] = whole.astype(bf16)
            valid = off + lax.broadcasted_iota(jnp.int32, (TILE, 1), 0) < total
            terms = [jnp.where(valid, v, 0.0) for v in (whole, two)]
            return tuple(a + rows_sum(v * v) for a, v in zip(acc, terms))

        start = (jnp.zeros((1, features), f32),) * 2
        sums.append(lax.fori_loop(0, half // TILE, rows_step, start))
    whole, two = (a + b for a, b in zip(*sums))
    lines = [jnp.sum(v, axis=1, keepdims=True) for v in (whole, branch_ref[...], two)]
    lines.append(jnp.full((1, 1), total.astype(f32), f32))
    for i in range(8):
        line = jnp.broadcast_to(lines[min(i, 3)], (1, 128))
        for ref in refs[:-2][1:]:
            line = line + ref[i : i + 1, :]
        sums_ref[i : i + 1, :] = line


def output_call(which, lengths, both, other, middle, vecs, branch, filled, after):
    rows, features = middle.shape
    count = len(after)

    def kernel(lengths_ref, *refs):
        output_kernel(lengths_ref, *refs[count:])

    whole = pl.BlockSpec(memory_space=pltpu.VMEM)
    anywhere = pl.BlockSpec(memory_space=pl.ANY)
    more = [anywhere, whole] if filled else []
    return pl.pallas_call(
        kernel,
        grid=(1,),
        out_shape=(shape((2, rows, features), bf16), shape((8, 128), f32)),
        in_specs=[pl.BlockSpec(memory_space=pltpu.SMEM)] + [anywhere] * count + [whole] * 5 + more,
        out_specs=(pl.BlockSpec((1, rows, features), lambda i: (which, 0, 0)), whole),
        input_output_aliases={1 + count + 5: 0} if filled else {},
        compiler_params=pltpu.CompilerParams(vmem_limit_bytes=16 * 2**20),
        cost_estimate=cost(),
        name="output_kernel",
    )(lengths, *after, both, other, middle, vecs, branch, *filled)


def message_kernel(norm_one, norm_two, sums_one, sums_two, off_one, off_two, heads_one, heads_two, out_ref):
    width = heads_one.shape[1] // 3
    out_ref[...] = jnp.zeros_like(out_ref)
    out_ref[0:2, :] = norm_one[...] + norm_two[...]
    out_ref[2:6, :] = sums_one[...] + sums_two[...]
    out_ref[6:7, :] = off_one[...] + off_two[...]
    heads = heads_one[...] + heads_two[...]
    out_ref[8:9, :width] = heads[:, :width]
    out_ref[9:10, :width] = heads[:, 2 * width :]


def shards_kernel(*refs):
    *pairs, grads_ref, out_ref = refs
    column = 0
    squares = jnp.zeros((1, 1), f32)
    for keep_ref, moved_ref in zip(pairs[::2], pairs[1::2]):
        grad = keep_ref[...].astype(f32) + moved_ref[...].astype(f32)
        stop = column + grad.shape[1]
        grads_ref[:, column:stop] = grad
        squares = squares + whole_sum(grad * grad)
        column = stop
    out_ref[...] = jnp.broadcast_to(squares, out_ref.shape)


def partial_kernel(message_ref, out_ref):
    squares = whole_sum(message_ref[8:10, :] * message_ref[8:10, :])
    squares = squares + whole_sum(message_ref[6:7, :] * message_ref[6:7, :])
    out_ref[...] = jnp.broadcast_to(squares, out_ref.shape)


def rms_kernel(features, own_ref, moved_ref, out_ref):
    sums = own_ref[...] + moved_ref[...]
    values = jnp.sqrt(sums / (sums[3:4, :] * features))
    for i in range(3):
        out_ref[i] = jnp.max(values[i : i + 1, :])


def rms_call(own, moved, features, after):
    def kernel(*refs):
        rms_kernel(features, *refs[1:])

    return pl.pallas_call(
        kernel,
        out_shape=shape((3,), f32),
        in_specs=[pl.BlockSpec(memory_space=pl.ANY)] + [pl.BlockSpec(memory_space=pltpu.VMEM)] * 2,
        out_specs=pl.BlockSpec(memory_space=pltpu.SMEM),
        compiler_params=pltpu.CompilerParams(vmem_limit_bytes=8 * 2**20),
        cost_estimate=cost(),
        name="rms_kernel",
    )(after, own, moved)


def adamw_kernel(partial_ref, moved_ref, message_ref, grads_ref, *refs):
    count = 21
    inputs, targets, norm_ref = refs[:count], refs[count : 2 * count], refs[2 * count]
    outputs, write_sems = refs[2 * count + 1 : 3 * count + 1], refs[3 * count + 1]
    writes = [pltpu.make_async_copy(outputs[i], targets[i], write_sems.at[i]) for i in range(count)]
    width = inputs[0].shape[2]
    hidden = inputs[6].shape[1]
    vecs = message_ref[0:6, :]
    norm = jnp.sqrt(partial_ref[0:1, 0:1] + moved_ref[0:1, 0:1] + whole_sum(vecs * vecs))
    norm_ref[0] = jnp.max(norm)
    clip = jnp.minimum(1.0, clip_limit / (norm + 1e-06))

    def step(p, gradient, at=Ellipsis):
        weight, moment, square = (ref[at] for ref in inputs[3 * p : 3 * p + 3])
        decay = matrix_decay if p < 4 else 0.0
        factor = clip if gradient.ndim == 2 else jnp.max(clip)
        values = adamw_step(weight, moment, square, gradient, step_rates[p], decay, factor)
        for ref, value in zip(outputs[3 * p : 3 * p + 3], values):
            ref[at] = value

    start = 4 * width
    parts = (
        tuple((grads_ref[:, j * width : (j + 1) * width], j) for j in range(3)),
        ((grads_ref[:, 3 * width : start].T,),),
        ((grads_ref[:, start : start + hidden],),),
        ((grads_ref[:, start + hidden :],),),
        ((vecs,),),
        ((message_ref[8:10, : inputs[15].shape[1]],),),
        ((message_ref[6, :],),),
    )
    for p, steps in enumerate(parts):
        for arguments in steps:
            step(p, *arguments)
        for copy in writes[3 * p : 3 * p + 3]:
            copy.start()
    for copy in writes:
        copy.wait()


def adamw_call(partial, moved, message, grads, state, after):
    in_vmem = pl.BlockSpec(memory_space=pltpu.VMEM)
    anywhere = pl.BlockSpec(memory_space=pltpu.MemorySpace.HBM)
    count = len(state)

    def kernel(*refs):
        adamw_kernel(*refs[len(after) :])

    return pl.pallas_call(
        kernel,
        out_shape=tuple(shape(v.shape, f32) for v in state) + (shape((1,), f32),),
        in_specs=[pl.BlockSpec(memory_space=pl.ANY)] * len(after) + [in_vmem] * (4 + count),
        out_specs=(anywhere,) * count + (pl.BlockSpec(memory_space=pltpu.SMEM),),
        scratch_shapes=[pltpu.VMEM(v.shape, f32) for v in state] + [pltpu.SemaphoreType.DMA((count,))],
        compiler_params=pltpu.CompilerParams(vmem_limit_bytes=24 * 2**20),
        cost_estimate=cost(),
        name="adamw_kernel",
    )(*after, partial, moved, message, grads, *state)


def build(n):
    top = n // 2

    def local(
        inputs,
        time_first,
        time_second,
        lengths_first,
        lengths_second,
        cotangent,
        w_qkv,
        m_qkv,
        v_qkv,
        w_proj,
        m_proj,
        v_proj,
        w_up,
        m_up,
        v_up,
        w_down,
        m_down,
        v_down,
        w_vecs,
        m_vecs,
        v_vecs,
        b_heads,
        m_heads,
        v_heads,
        b_hidden,
        m_hidden,
        v_hidden,
    ):
        rows, features = inputs.shape[1], inputs.shape[2]
        r, _, width = w_qkv.shape
        hidden = w_up.shape[1]
        heads = width // HD
        half = rows // 2
        lengths = (lengths_first, lengths_second)
        whole_f = shape((rows, features), f32)
        whole_b = shape((rows, features), bf16)
        hidden_b = shape((rows, hidden), bf16)
        half_b = shape((half, features), bf16)
        half_f = shape((half, features), f32)
        line = shape((1, features), f32)

        def swap(v, bit):
            return swap_bit(v, "dp", n, bit)

        def gathered(shard, bit, stop, after=()):
            while bit > stop:
                (shard,) = merged(shard, swap(shard, bit), r, bit, after)
                after = ()
                bit //= 2
            return shard

        qk, vp = call(
            pack_kernel, (shape((r, 2 * width), bf16),) * 2, (), (w_qkv.transpose(1, 0, 2), w_proj), (), 8
        )
        times = [jnp.pad(t[0], ((0, 16 - t.shape[1]), (0, 0))) for t in (time_first, time_second)]
        stream_one, normed_one, stream_two, normed_two = call(
            first_norm_kernel, (whole_f, whole_b) * 2, lengths, (inputs, *times, w_vecs), (qk,), 24
        )
        stream, normed = (stream_one, stream_two), (normed_one, normed_two)
        qk = gathered(qk, top, top // 2, (normed_two,))
        vp = gathered(vp, top, top // 2, (qk,))
        qk = gathered(qk, top // 2, 1, (vp,))
        (up,) = call(cast_kernel, (shape((r, hidden), bf16),), (), (w_up,), (qk,), 8)
        vp = gathered(vp, top // 2, 1, (up,))
        (qk,) = merged(qk, swap(qk, 1), r, 1, (vp,))
        (down,) = call(cast_kernel, (shape((r, hidden), bf16),), (), (w_down.T,), (qk,), 8)
        up = gathered(up, top, top // 2, (down,))
        wv, proj = merged(vp, swap(vp, 1), r, 1, (up,), (width, width))

        def spread(v, after=()):
            moved = over_chip(v)
            pair = call(pair_kernel, shape((rows, 2 * v.shape[1]), bf16), (), (v, moved), after, 8)
            return [pair, over_core(pair)]

        bias = jnp.concatenate([b_heads[0], jnp.zeros_like(b_heads[0]), b_heads[1]])[None]
        head_low = pltpu.VMEM((heads, rows, HD), bf16)
        head_full = pltpu.VMEM((heads, rows, HD), f32)
        after = (wv,)
        att, sent, qkv, lse = [], [], [], []
        for b in range(2):
            carried = (proj,) if b == 0 else ()
            a, q, l, *pair = call(
                functools.partial(forward_kernel, REACH[b], len(carried)),
                (
                    shape((rows, width), bf16),
                    shape((rows, 3 * width), bf16),
                    shape((rows, 128), f32),
                    *(shape((rows, 2 * width), bf16) for _ in carried),
                ),
                (lengths[b],),
                (normed[b], qk, wv, bias, *carried),
                after,
                12,
                [head_low] * 3,
            )
            att.append(a)
            sent.append(pair[0] if pair else a)
            qkv.append(q)
            lse.append(l)
            after = (l,)
            if b == 0:
                down = gathered(down, top, top // 2, after)
                up = gathered(up, top // 2, 1, (down,))
                down = gathered(down, top // 2, 1, (up,))
                after = (down,)
        att_first = spread(sent[0], after)
        (up,) = merged(up, swap(up, 1), r, 1, (att_first[0],), weight=4)
        after = (up,)

        names = [[] for _ in range(9)]
        att_own = []
        for b in range(2):
            outs = call(
                hidden_kernel,
                (whole_f, whole_b, hidden_b, shape((rows, hidden), f32), line),
                (lengths[b],),
                (*att_first, *att_own, stream[b], w_vecs, up, b_hidden[None]),
                after,
            )
            for kept, v in zip(names, outs):
                kept.append(v)
            after = (outs[-1],)
            if b == 0:
                att_own = spread(sent[1], after)
                upstream = call(upstream_kernel, (whole_b,) * 2, lengths, (cotangent,), (att_own[0],))
                after = (upstream[1],)
        (down,) = merged(down, swap(down, 1), r, 1, after)
        low, parts = [], [[], []]

        def down_part(b, side, after):
            out = (half_b, half_f)[side]
            part = call(functools.partial(down_kernel, side), out, (), (active[b], down), after)
            parts[b].insert(0, part)
            return part

        after = (down,)
        for b in range(2):
            outs = call(
                hidden_back_kernel,
                (hidden_b, half_b, half_f, shape((1, hidden), f32)),
                (),
                (upstream[b], names[3][b], up, down),
                after,
            )
            for kept, v in zip(names[5:], outs):
                kept.append(v)
            middle, normed_mid, active, slope, branch_square, grad_hidden, away, keep, offsets = names
            if b == 0:
                after = (down_part(0, 1, (outs[-1],)),)
            else:
                bulk = parted((*normed_mid, *grad_hidden, *upstream, *active), n, (outs[-1],))
                bulk_moved = swap(bulk[0], 1)
                after = (bulk[0],)
            low.append(add(keep[b], over_core(away[b]), after))
            after = (low[b],)
        both = add(low[0], over_chip(low[0]), after)
        gnt = [(both, over_core(both))]
        after = (down_part(1, 1, (both,)),)

        grad_middle, middle_low, grad_mixed, sums, head_sums, back_low = [], [], [], [], [], []
        for b in range(2):
            outs = call(
                functools.partial(backward_kernel, REACH[b]),
                (
                    whole_f,
                    whole_b,
                    shape((rows, 3 * width), bf16),
                    half_b,
                    half_f,
                    shape((4, features), f32),
                    shape((1, 3 * width), f32),
                ),
                (lengths[b],),
                (*gnt[b], middle[b], upstream[b], w_vecs, qk, wv, proj, qkv[b], lse[b]),
                after,
                24,
                [head_low] * 4 + [head_full] * 2,
            )
            grad_middle.append(outs[0])
            middle_low.append(outs[1])
            grad_mixed.append(outs[2])
            sums.append(outs[5])
            head_sums.append(outs[6])
            after = (outs[6],)
            if b == 0:
                both = add(low[1], over_chip(low[1]), after)
                gnt.append((both, over_core(both)))
                after = (both,)
            else:
                bulk = split(bulk[1], bulk_moved, r, 2, after)
                bulk_moved = swap(bulk[0], 2)
                chunk = parted((*normed, *grad_mixed, *middle_low, *att), n, (bulk[0],))
                chunks = [[*chunk, swap(chunk[0], 1)]]
                after = (chunk[0],)
            back_low.append(add(outs[4], over_core(outs[3]), after))
            after = (back_low[b],)

        def halved(chunk, bit, after):
            away, kept = split(chunk[1], chunk[2], r, bit, after)
            return [away, kept, swap(away, bit)]

        moved = down_part(0, 0, after)
        both = add(back_low[0], over_chip(back_low[0]), (moved,))
        piece = (both, over_core(both))
        part = [add(parts[0][1], over_core(parts[0][0]), (both,))]
        after = (part[0],)
        bulk = [*bulk, bulk_moved]
        bit = 4
        while bit < n:
            bulk = halved(bulk, bit, after)
            after = (bulk[0],)
            bit *= 2
        for i in range(len(chunks)):
            chunks[i] = halved(chunks[i], 2, after)
            after = (chunks[i][0],)
        input_grad, pair = input_grad_call(0, *piece, stream[0], grad_middle[0], w_vecs, (), after)
        norm_sums = [pair]
        after = (pair,)
        moved = down_part(1, 0, after)
        both = add(back_low[1], over_chip(back_low[1]), (moved,))
        piece = (both, over_core(both))
        part.append(add(parts[1][1], over_core(parts[1][0]), (both,)))
        input_grad, pair = input_grad_call(
            1, *piece, stream[1], grad_middle[1], w_vecs, (input_grad,), (part[1],)
        )
        norm_sums.append(pair)

        def hop(v, moved, after=(), more=()):
            return call(sum_kernel, shape(v.shape, f32), (), (v, moved, *more), after, 8)

        message = call(
            message_kernel, shape((16, features), f32), (), (*norm_sums, *sums, *offsets, *head_sums), (), 8
        )
        after = (message,)
        bit = 4
        while bit < n:
            for i in range(len(chunks)):
                chunks[i] = halved(chunks[i], bit, after)
                after = (chunks[i][0],)
            bit *= 2
        both = add(part[0], over_chip(part[0]), after)
        two = [(both, over_core(both))]
        message = hop(message, swap(message, 1), (both,))
        filled = output_call(0, lengths[0], *two[0], middle[0], w_vecs, branch_square[0], (), (message,))
        message = hop(message, swap(message, 2), (filled[1],))
        grads, squares = call(
            shards_kernel,
            (shape((r, 4 * width + 2 * hidden), f32), shape((8, 128), f32)),
            (),
            tuple(v for chunk in (*chunks, bulk) for v in chunk[1:]),
            (message,),
        )
        after = (squares,)
        bit = 4
        while bit < n:
            message = hop(message, swap(message, bit), after)
            after = ()
            bit *= 2
        partial = call(partial_kernel, shape((8, 128), f32), (), (message,), (), 8)
        both = add(part[1], over_chip(part[1]), (partial,))
        two.append((both, over_core(both)))
        squares = hop(squares, swap(squares, 1), (both,))
        block_out, out_sums = output_call(
            1, lengths[1], *two[1], middle[1], w_vecs, branch_square[1], tuple(filled), (squares,)
        )
        arrived = [swap(squares, mask) for mask in range(2, n, 2)]
        squares = call(
            tree_kernel, shape((8, 128), f32), (), (squares, *arrived, partial), (out_sums,), 8
        )
        out_sums = hop(out_sums, swap(out_sums, 1), (squares,))
        partial = hop(squares, over_core(squares), (out_sums,))
        out_sums = hop(out_sums, swap(out_sums, 2), (partial,))
        bit = 4
        last = out_sums
        state = (
            *(v.transpose(1, 0, 2) for v in (w_qkv, m_qkv, v_qkv)),
            *(w_proj, m_proj, v_proj),
            *(w_up, m_up, v_up),
            *(v.T for v in (w_down, m_down, v_down)),
            *(w_vecs, m_vecs, v_vecs),
            *(b_heads, m_heads, v_heads),
            *(b_hidden, m_hidden, v_hidden),
        )
        *updated, grad_norm = adamw_call(partial, over_chip(partial), message, grads, state, (last,))
        while 2 * bit < n:
            out_sums = hop(out_sums, swap(out_sums, bit), (grad_norm,))
            bit *= 2
        stream_rms = rms_call(out_sums, swap(out_sums, bit), features, grad_norm)
        return (
            block_out,
            input_grad,
            grad_norm,
            stream_rms,
            *(v.transpose(1, 0, 2) for v in updated[:3]),
            *updated[3:9],
            *(v.T for v in updated[9:12]),
            *updated[12:18],
            *updated[18:],
        )

    return local


def solution(mesh):
    rows = P(None, "dp", None)
    group = P("dp", None, None)
    qkv, proj, up = P("dp", None, "tensor"), P("tensor", "dp"), P("dp", "tensor")
    params = [qkv] * 3 + [proj] * 3 + [up] * 3 + [proj] * 3 + [P()] * 3
    params += [P(None, "tensor")] * 3 + [P("tensor")] * 3
    return jax.shard_map(
        build(mesh.shape["dp"]),
        mesh=mesh,
        in_specs=(rows, group, group, P("dp", None), P("dp", None), rows, *params),
        out_specs=(rows, rows, P(), P(), *params),
        check_vma=False,
    )
```
